32 devices in a mesh: dp: 8 (over z, y), mp: 4 (over x, core).
Axes of the slice: x: 2, y: 2, z: 4, core: 2. Of those that a mesh axis runs over, the one named last changes fastest.
Arguments:
- patches: bfloat16 [37632, 1536], P('dp', 'mp'), may hold values from -5 to 13, as said below
- vis_count: int32 [256], P('dp'), may hold values from 24 to 64, as said below
- vis_pos: int32 [256, 64], P('dp'), may hold values from 0 to 146, as said below
- tile_sample: int32 [256], P('dp'), may hold values from 0 to 63, as said below
- tile_quad: int32 [256], P('dp'), may hold values from 0 to 3, as said below
- w_embed: bfloat16 [1536, 768], P('mp'), may hold values from -1 to 1
- b_embed: bfloat16 [768], P('mp'), may hold values from -3 to 3
- norm1_gain: bfloat16 [768], replicated, may hold values from 0.25 to 1.75
- norm1_bias: bfloat16 [768], replicated, may hold values from -3 to 3
- w_query: bfloat16 [768, 768], P(None, 'mp'), may hold values from -0.3125 to 0.3125
- b_query: bfloat16 [768], P('mp'), may hold values from -3 to 3
- w_key: bfloat16 [768, 768], P(None, 'mp'), may hold values from -0.3125 to 0.3125
- w_value: bfloat16 [768, 768], P(None, 'mp'), may hold values from -0.21875 to 0.21875
- b_value: bfloat16 [768], P('mp'), may hold values from -3 to 3
- w_attn_out: bfloat16 [768, 768], P('mp'), may hold values from -0.875 to 0.875
- b_attn_out: bfloat16 [768], P('mp'), may hold values from -3 to 3
- norm2_gain: bfloat16 [768], replicated, may hold values from 0.25 to 1.75
- norm2_bias: bfloat16 [768], replicated, may hold values from -3 to 3
- w_hidden: bfloat16 [768, 3072], P(None, 'mp'), may hold values from -0.21875 to 0.21875
- b_hidden: bfloat16 [3072], P('mp'), may hold values from -3 to 3
- w_mlp_out: bfloat16 [3072, 768], P('mp'), may hold values from -0.21875 to 0.21875
- b_mlp_out: bfloat16 [768], P('mp'), may hold values from -3 to 3
- w_decoder: bfloat16 [768, 512], P(None, 'mp'), may hold values from -0.21875 to 0.21875
- b_decoder: bfloat16 [512], P('mp'), may hold values from -3 to 3
- mask_token: bfloat16 [512], P('mp'), may hold values from -4 to 4
- cotangent: bfloat16 [37632, 512], P('dp', 'mp'), may hold values from -13 to 13
Outputs:
- decoded: bfloat16 [37632, 512], P('dp', 'mp')
- patch_grad: float32 [37632, 1536], P('dp', 'mp')
- grad_w_embed: float32 [1536, 768], P('mp')
- grad_b_embed: float32 [768], P('mp')
- grad_norm1_gain: float32 [768], replicated
- grad_norm1_bias: float32 [768], replicated
- grad_w_query: float32 [768, 768], P(None, 'mp')
- grad_b_query: float32 [768], P('mp')
- grad_w_key: float32 [768, 768], P(None, 'mp')
- grad_w_value: float32 [768, 768], P(None, 'mp')
- grad_b_value: float32 [768], P('mp')
- grad_w_attn_out: float32 [768, 768], P('mp')
- grad_b_attn_out: float32 [768], P('mp')
- grad_norm2_gain: float32 [768], replicated
- grad_norm2_bias: float32 [768], replicated
- grad_w_hidden: float32 [768, 3072], P(None, 'mp')
- grad_b_hidden: float32 [3072], P('mp')
- grad_w_mlp_out: float32 [3072, 768], P('mp')
- grad_b_mlp_out: float32 [768], P('mp')
- grad_w_decoder: float32 [768, 512], P(None, 'mp')
- grad_b_decoder: float32 [512], P('mp')
- grad_mask_token: float32 [512], P('mp')
The draws below stay inside these ranges and needn't reach their ends.
Inputs may be any that keep to these rules, and one draw needn't show every extreme that they name: `tile_sample`: sample m has four tiles, one of each quadrant, and is processed by block owner m // 8 of dp; at most 4 tiles of one data device belong to the samples of one owner, and some device reaches 4. `tile_quad`: quadrant q covers patch rows from (q // 2) * 7 and patch columns from (q % 2) * 7 of its sample. `vis_count`: some sample has 64 visible tokens in each of its four tiles. `vis_pos`: the entries of a tile are distinct; its first vis_count entries are its visible tokens. `patches`: pixel column c holds band c % 6.
All inputs are finite; a program needn't handle non-finite values.
Results may differ from the reference program's by a relative error of at most 0.035.
Values may be sent and summed in bfloat16 or wider, within the bound.
No kernel may reach another device: no remote copies, remote signals or barrier semaphores. Data moves between devices by JAX's collectives and lax.ppermute only.
A program may use at most 192 MiB of HBM per device.

```python
import jax
import jax.numpy as jnp
from jax import lax

D = 768
HEADS = 12
HEAD_DIM = 64
FF = 3072
DEC = 512
BANDS = 6
PIX = 1536
SIDE = 7
TILE_TOK = 147
VIS_TILE = 64
VIS_MIN = 24
SAMP_OWN = 8
TILES_DEV = 32
SAMPLES = 64
TILES = 256
N_DP = 8


def layout(key):
    base_key = jax.random.fold_in(key, 11)
    key_offsets, key_codes, key_counts, key_full = jax.random.split(base_key, 4)
    pair_tiles = (TILES_DEV + N_DP - 1) // N_DP
    pool_size = pair_tiles * N_DP
    shuffled = jax.random.permutation(key_offsets, pool_size).astype(jnp.int32)
    residues = shuffled % N_DP
    needed = (residues == 1) | (residues == N_DP - 1) | (residues == N_DP // 2)
    ranking = jnp.where(needed, 0, pool_size) + jnp.arange(pool_size, dtype=jnp.int32)
    offsets = residues[jnp.argsort(ranking)][:TILES_DEV].astype(jnp.int32)
    sources = jnp.arange(N_DP, dtype=jnp.int32)[:, None]
    owners = (sources + offsets[None, :]) % N_DP

    def owner_codes(code_key):
        return jax.random.permutation(code_key, TILES_DEV).astype(jnp.int32)
    codes = jax.vmap(owner_codes)(jax.random.split(key_codes, N_DP))
    arrival = jnp.broadcast_to(jnp.arange(TILES_DEV, dtype=jnp.int32)[None, :], owners.shape)
    code_here = codes[owners, arrival]
    samples = owners * SAMP_OWN + code_here // 4
    quadrants = code_here % 4
    counts = jax.random.randint(key_counts, (N_DP, TILES_DEV), VIS_MIN, VIS_TILE + 1)
    chosen = jax.random.randint(key_full, (), 0, N_DP * SAMP_OWN)
    counts = jnp.where(samples == chosen, VIS_TILE, counts)
    return (samples.reshape(-1).astype(jnp.int32), quadrants.reshape(-1).astype(jnp.int32), counts.reshape(-1).astype(jnp.int32))


def draw_tile_sample(key, part):
    return layout(key)[0]


def draw_tile_quad(key, part):
    return layout(key)[1]


def draw_vis_count(key, part):
    return layout(key)[2]


def draw_vis_pos(key, part):
    tile_keys = jax.random.split(jax.random.fold_in(key, 5), TILES_DEV * N_DP)

    def one_tile(tile_key):
        return jax.random.permutation(tile_key, TILE_TOK)[:VIS_TILE]
    return jax.vmap(one_tile)(tile_keys).astype(jnp.int32)


def draw_patches(key, part):
    base_key = jax.random.fold_in(key, 3)
    key_center, key_spread, key_noise, key_tile = jax.random.split(base_key, 4)
    centers = jax.random.uniform(key_center, (BANDS,), jnp.float32, 0.5, 2.0)
    spreads = jax.random.uniform(key_spread, (BANDS,), jnp.float32, 0.5, 1.5)
    rows_all = TILES_DEV * N_DP * TILE_TOK
    device_pos = (jnp.arange(rows_all) // (TILES_DEV * TILE_TOK)).astype(jnp.float32)
    rising = 1.0 + 2.0 * device_pos / max(N_DP - 1, 1)
    tile_scale = jnp.repeat(jax.random.uniform(key_tile, (TILES_DEV * N_DP,), jnp.float32, 0.6, 1.4), TILE_TOK)
    noise = jax.random.truncated_normal(key_noise, -3.0, 3.0, (rows_all, PIX), jnp.float32)
    mean_cols = jnp.tile(centers, PIX // BANDS)
    spread_cols = jnp.tile(spreads, PIX // BANDS)
    values = mean_cols[None, :] * (rising * tile_scale)[:, None] + spread_cols[None, :] * noise
    return values.astype(jnp.bfloat16)


def draw_w_embed(key, part):
    base_key = jax.random.fold_in(key, 17)
    key_noise, key_dirs = jax.random.split(base_key, 2)
    noise = jax.random.truncated_normal(key_noise, -3.0, 3.0, (PIX, D), jnp.float32)
    share = 0.12
    band_dirs = jax.random.truncated_normal(key_dirs, -3.0, 3.0, (BANDS, D), jnp.float32)
    band_rows = jnp.tile(band_dirs, (PIX // BANDS, 1))
    values = (noise + share * band_rows) * float(PIX) ** (-0.5)
    return values.astype(jnp.bfloat16)


def draw_cotangent(key, part):
    base_key = jax.random.fold_in(key, 23)
    key_noise, key_shared = jax.random.split(base_key, 2)
    rows_all = TILES_DEV * N_DP * TILE_TOK
    device_pos = (jnp.arange(rows_all) // (TILES_DEV * TILE_TOK)).astype(jnp.float32)
    ramp = 0.5 + device_pos / max(N_DP - 1, 1)
    shared = jax.random.truncated_normal(key_shared, -3.0, 3.0, (DEC,), jnp.float32)
    noise = jax.random.truncated_normal(key_noise, -3.0, 3.0, (rows_all, DEC), jnp.float32)
    amount = 2.0
    values = noise + amount * ramp[:, None] * shared[None, :]
    return values.astype(jnp.bfloat16)


def block_levels(key, extent, pieces, least, largest):
    factor_of, own = 1.0, jax.random.fold_in(key, 6)
    for axis_at, blocks in pieces:
        draws = jnp.exp(jax.random.uniform(jax.random.fold_in(own, axis_at), (blocks,), jnp.float32, least / len(pieces), largest / len(pieces)))
        factor_of = factor_of * jnp.repeat(draws, extent[axis_at] // blocks).reshape([-1 if axis == axis_at else 1 for axis in range(len(extent))])
    return factor_of


def bell_draw(own_key, shape, width, most, shards=(), kind=jnp.bfloat16):
    drawn = jax.random.normal(own_key, shape, jnp.float32) * width
    if len(shards) > 0:
        drawn = block_levels(own_key, shape, shards, -0.22, 0.18) * drawn
    return jnp.clip(drawn, min=-most, max=most).astype(kind)


def setup_inputs(seed: int = 0) -> dict:
    keys = jax.random.split(jax.random.key(seed), 27)
    return {
        "patches": draw_patches(jax.random.fold_in(keys[26], 71), 0),
        "vis_count": draw_vis_count(jax.random.fold_in(keys[26], 71), 0),
        "vis_pos": draw_vis_pos(jax.random.fold_in(keys[26], 71), 0),
        "tile_sample": draw_tile_sample(jax.random.fold_in(keys[26], 71), 0),
        "tile_quad": draw_tile_quad(jax.random.fold_in(keys[26], 71), 0),
        "w_embed": draw_w_embed(jax.random.fold_in(keys[26], 71), 0),
        "b_embed": bell_draw(keys[6], (D,), 0.5, 3.0, ((0, 4),)),
        "norm1_gain": jnp.clip(1.0 + 0.15 * jax.random.normal(keys[7], (D,), jnp.float32), 0.25, 1.75).astype(jnp.bfloat16),
        "norm1_bias": bell_draw(keys[8], (D,), 0.3, 3.0),
        "w_query": bell_draw(keys[9], (D, D), (D // 2) ** -0.5, 0.3125, ((1, 4),)),
        "b_query": bell_draw(keys[10], (D,), 0.5, 3.0, ((0, 4),)),
        "w_key": bell_draw(keys[11], (D, D), (D // 2) ** -0.5, 0.3125, ((1, 4),)),
        "w_value": bell_draw(keys[12], (D, D), D ** -0.5, 0.21875, ((1, 4),)),
        "b_value": bell_draw(keys[13], (D,), 0.5, 3.0, ((0, 4),)),
        "w_attn_out": bell_draw(keys[14], (D, D), (D // 16) ** -0.5, 0.875, ((0, 4),)),
        "b_attn_out": bell_draw(keys[15], (D,), 0.3, 3.0, ((0, 4),)),
        "norm2_gain": jnp.clip(1.0 + 0.15 * jax.random.normal(keys[16], (D,), jnp.float32), 0.25, 1.75).astype(jnp.bfloat16),
        "norm2_bias": bell_draw(keys[17], (D,), 0.3, 3.0),
        "w_hidden": bell_draw(keys[18], (D, FF), D ** -0.5, 0.21875, ((1, 4),)),
        "b_hidden": bell_draw(keys[19], (FF,), 0.5, 3.0, ((0, 4),)),
        "w_mlp_out": bell_draw(keys[20], (FF, D), (FF // 4) ** -0.5, 0.21875, ((0, 4),)),
        "b_mlp_out": bell_draw(keys[21], (D,), 0.3, 3.0, ((0, 4),)),
        "w_decoder": bell_draw(keys[22], (D, DEC), D ** -0.5, 0.21875, ((1, 4),)),
        "b_decoder": bell_draw(keys[23], (DEC,), 0.5, 3.0, ((0, 4),)),
        "mask_token": bell_draw(keys[24], (DEC,), 1.0, 4.0, ((0, 4),)),
        "cotangent": draw_cotangent(jax.random.fold_in(keys[26], 71), 0),
    }


@jax.custom_vjp
def low(v):
    return lax.optimization_barrier(v.astype(jnp.bfloat16)).astype(jnp.float32)

@jax.custom_vjp
def low_back(v):
    return v

def low_keep(v):
    return (low(v), None)

def low_pass(kept, grad):
    return (grad,)

def back_keep(v):
    return (v, None)

def back_low(kept, grad):
    return (low(grad),)
low.defvjp(low_keep, low_pass)
low_back.defvjp(back_keep, back_low)
highest = lax.Precision.HIGHEST
norm_eps = 1e-06
band_eps = 1e-06
big_negative = -1000000000.0

def sincos(position, full_width):
    half_width = full_width // 2
    frequency = 1.0 / 10000.0 ** (jnp.arange(half_width, dtype=jnp.float32) / half_width)
    angles = position.astype(jnp.float32)[..., None] * frequency
    return jnp.concatenate([jnp.sin(angles), jnp.cos(angles)], axis=-1)

def position_rows(quadrant, token_index, full_width, side_len):
    tile_area = side_len * side_len
    frame_pos = token_index // tile_area
    inner_pos = token_index % tile_area
    row_pos = quadrant // 2 * side_len + inner_pos // side_len
    col_pos = quadrant % 2 * side_len + inner_pos % side_len
    part_width = full_width // 16 * 6
    return jnp.concatenate([sincos(col_pos, part_width), sincos(row_pos, part_width), sincos(frame_pos, full_width - 2 * part_width)], axis=-1)

def matmul(left, right):
    return jnp.dot(left, right, precision=highest)

def layer_norm(values, gain_vec, bias_vec):
    centred = values - lax.optimization_barrier(jnp.mean(values, axis=-1, keepdims=True))
    variance = lax.optimization_barrier(jnp.mean(centred * centred, axis=-1, keepdims=True))
    return centred * lax.rsqrt(variance + norm_eps) * gain_vec + bias_vec

def block(params, start_rows, usable):
    w_embed, b_embed, norm1_gain, norm1_bias, w_query, b_query, w_key, w_value, b_value, w_attn_out, b_attn_out, norm2_gain, norm2_bias, w_hidden, b_hidden, w_mlp_out, b_mlp_out, w_decoder, b_decoder, mask_token = params
    samples_here = start_rows.shape[0]
    length = start_rows.shape[1]
    flat_rows = start_rows.reshape(-1, D)
    normed_one = low(layer_norm(flat_rows, norm1_gain, norm1_bias))
    queries = low_back(low(matmul(normed_one, w_query) + b_query))
    key_rows = low_back(low(matmul(normed_one, w_key)))
    value_rows = low_back(low(matmul(normed_one, w_value) + b_value))
    head_shape = (samples_here, length, HEADS, HEAD_DIM)
    scores = jnp.einsum('sqhe,skhe->shqk', queries.reshape(head_shape), key_rows.reshape(head_shape), precision=highest)
    scores = low_back(scores * HEAD_DIM ** (-0.5))
    scores = jnp.where(usable[:, None, None, :], scores, big_negative)
    probs_low = low(jax.nn.softmax(scores, axis=-1))
    attended = jnp.einsum('shqk,skhe->sqhe', probs_low, value_rows.reshape(head_shape), precision=highest)
    attended = low_back(low(attended.reshape(-1, D)))
    middle = flat_rows + low_back(matmul(attended, w_attn_out) + b_attn_out)
    normed_two = low(layer_norm(low(middle), norm2_gain, norm2_bias))
    hidden_pre = low_back(matmul(normed_two, w_hidden) + b_hidden)
    hidden = low(jax.nn.gelu(hidden_pre, approximate=False))
    final_rows = middle + low_back(matmul(hidden, w_mlp_out) + b_mlp_out)
    decoded = low(matmul(low(final_rows), w_decoder) + b_decoder)
    return decoded.reshape(samples_here, length, DEC)

def forward(pixel_rows, params, vis_count, vis_pos, tile_sample, tile_quad):
    w_embed = params[0]
    b_embed = params[1]
    mask_token = params[19]
    grid_vals = pixel_rows.reshape(pixel_rows.shape[0], -1, BANDS)
    per_band = grid_vals.shape[0] * grid_vals.shape[1]
    band_mean = lax.optimization_barrier(jnp.sum(grid_vals, axis=(0, 1))) / per_band
    band_var = lax.optimization_barrier(jnp.sum(grid_vals * grid_vals, axis=(0, 1))) / per_band - band_mean * band_mean
    normed = ((grid_vals - band_mean) * lax.rsqrt(band_var + band_eps)).reshape(TILES, TILE_TOK, PIX)
    tile_ids = jnp.arange(TILES, dtype=jnp.int32)
    picked = low(normed[tile_ids[:, None], vis_pos])
    embedded = matmul(picked.reshape(-1, PIX), w_embed).reshape(TILES, VIS_TILE, D)
    quadrant = jnp.broadcast_to(tile_quad[:, None], vis_pos.shape)
    embedded = embedded + b_embed + position_rows(quadrant, vis_pos, D, SIDE)
    usable = jnp.arange(VIS_TILE, dtype=jnp.int32)[None, :] < vis_count[:, None]
    start = low_back(low(embedded)) * usable[:, :, None].astype(jnp.float32)
    tile_code = (tile_sample * 4 + tile_quad).astype(jnp.int32)
    order = jnp.zeros((SAMPLES * 4,), jnp.int32).at[tile_code].set(tile_ids)
    sample_rows = start[order].reshape(N_DP, SAMP_OWN, 4 * VIS_TILE, D)
    sample_usable = usable[order].reshape(N_DP, SAMP_OWN, 4 * VIS_TILE)

    def one_owner(rows_owner, mask_owner):
        return block(params, rows_owner, mask_owner)
    stepper = jax.checkpoint(one_owner)

    def scan_step(carry_val, item_pair):
        return (carry_val, stepper(item_pair[0], item_pair[1]))
    unused, decoded = lax.scan(scan_step, jnp.zeros((), jnp.float32), (sample_rows, sample_usable))
    decoded = decoded.reshape(SAMPLES * 4, VIS_TILE, DEC)[tile_code]
    places = jnp.where(usable, tile_ids[:, None] * TILE_TOK + vis_pos, TILES * TILE_TOK).reshape(-1)
    grid_out = jnp.broadcast_to(mask_token[None, :], (TILES * TILE_TOK, DEC))
    return grid_out.at[places].set(decoded.reshape(-1, DEC), mode='drop')

def reference(patches, vis_count, vis_pos, tile_sample, tile_quad, w_embed, b_embed, norm1_gain, norm1_bias, w_query, b_query, w_key, w_value, b_value, w_attn_out, b_attn_out, norm2_gain, norm2_bias, w_hidden, b_hidden, w_mlp_out, b_mlp_out, w_decoder, b_decoder, mask_token, cotangent):
    params = tuple((weight.astype(jnp.float32) for weight in (w_embed, b_embed, norm1_gain, norm1_bias, w_query, b_query, w_key, w_value, b_value, w_attn_out, b_attn_out, norm2_gain, norm2_bias, w_hidden, b_hidden, w_mlp_out, b_mlp_out, w_decoder, b_decoder, mask_token)))

    def whole(pixel_rows, *param_list):
        return forward(pixel_rows, param_list, vis_count, vis_pos, tile_sample, tile_quad)
    decoded, pullback = jax.vjp(whole, patches.astype(jnp.float32), *params)
    grads = pullback(cotangent.astype(jnp.float32))
    return (decoded.astype(jnp.bfloat16), grads[0], grads[1], grads[2], grads[3], grads[4], grads[5], grads[6], grads[7], grads[8], grads[9], grads[10], grads[11], grads[12], grads[13], grads[14], grads[15], grads[16], grads[17], grads[18], grads[19], grads[20])
```

```python
import functools

import jax
import jax.numpy as jnp
import numpy as np
from jax import lax
from jax.experimental import pallas as pl
from jax.experimental.pallas import tpu as pltpu
from jax.sharding import PartitionSpec as P

HEAD_DIM = 64
BANDS = 6
SIDE = 7
SAMP_OWN = 8
WINDOW = 176
VMEM_BYTES = 56 * 1024 * 1024

norm_eps = 1e-06
band_eps = 1e-06
big_negative = -1000000000.0
F32 = jnp.float32
BF16 = jnp.bfloat16


def params():
    return pltpu.CompilerParams(vmem_limit_bytes=VMEM_BYTES)


VM = pl.BlockSpec(memory_space=pltpu.VMEM)
SM = pl.BlockSpec(memory_space=pltpu.SMEM)


def swap(values, axis, bit):
    size = lax.axis_size(axis)
    return lax.ppermute(values, axis, [(i, i ^ bit) for i in range(size)])


def bits_of(axis):
    size = lax.axis_size(axis)
    return [1 << k for k in range(size.bit_length() - 1)]


def after(value, *before):
    return lax.optimization_barrier((value,) + before)[0]


def dot(left, right):
    return jnp.dot(left, right, preferred_element_type=F32)


def dot_t(left, right):
    return lax.dot_general(left, right, (((1,), (1,)), ((), ())), preferred_element_type=F32)


def dot_tl(left, right):
    return lax.dot_general(left, right, (((0,), (0,)), ((), ())), preferred_element_type=F32)


def window_of(tile, tile_tokens, total):
    base = tile * tile_tokens
    start = jnp.minimum((base // 16) * 16, total - WINDOW)
    return pl.multiple_of(start, 16), base - start


def hot_rows(pos_ref, count, tile, rem):
    lane = lax.broadcasted_iota(jnp.int32, (1, 128), 1)
    target = jnp.where(lane < count, pos_ref[pl.ds(tile, 1), :] + rem, -1)
    row = lax.broadcasted_iota(jnp.int32, (WINDOW, 128), 0)
    return row == target


def stats_kernel(patches, stats):
    def sum_step(i, carry):
        first, second = carry
        at = pl.multiple_of(i * 336, 16)
        x = patches[pl.ds(at, 336), :].astype(F32).reshape(42, 8, patches.shape[1])
        return first + jnp.sum(x, axis=0), second + jnp.sum(x * x, axis=0)

    blank = jnp.zeros((8, patches.shape[1]), F32)
    first, second = lax.fori_loop(0, patches.shape[0] // 336, sum_step, (blank, blank))
    stats[...] = band_sums(
        jnp.sum(first, axis=0, keepdims=True), jnp.sum(second, axis=0, keepdims=True)
    )


def pick_kernel(tile_tokens, order, count, pos, patches, cot, picked, cot_picked, mask_sum):
    total = patches.shape[0]
    slots = order.shape[0]
    visible = picked.shape[0] // slots
    mask_total = jnp.zeros((8, cot.shape[1]), F32)
    row = lax.broadcasted_iota(jnp.int32, (WINDOW, 128), 0)
    lane = lax.broadcasted_iota(jnp.int32, (WINDOW, 128), 1)
    for slot in range(slots):
        tile = order[slot]
        start, rem = window_of(tile, tile_tokens, total)
        hot = hot_rows(pos, count[tile], tile, rem).astype(F32)
        shown = jnp.sum(hot, axis=1, keepdims=True)
        inside = jnp.logical_and(row >= rem, row < rem + tile_tokens)
        hidden = jnp.where(inside, 1.0 - shown, 0.0)
        chooser = jnp.where(lane == visible, hidden, hot).astype(BF16)
        got = dot_tl(chooser, patches[pl.ds(start, WINDOW), :])
        got_cot = dot_tl(chooser, cot[pl.ds(start, WINDOW), :])
        here = slice(slot * visible, (slot + 1) * visible)
        picked[here, :] = got[:visible].astype(BF16)
        cot_picked[here, :] = got_cot[:visible].astype(BF16)
        mask_total = mask_total + got_cot[visible : visible + 8]
    mask_sum[...] = mask_total


def place_in(codes, tiles, visible, blocks):
    rows, cols = tiles.shape
    each = rows // blocks

    def kernel(code_ref, tile_ref, *refs):
        outs, held = refs[:-1], refs[-1]
        for k in range(rows // visible):
            at = pl.multiple_of(code_ref[k] * visible, 16)
            held[pl.ds(at, visible), :] = tile_ref[k * visible : (k + 1) * visible, :]
        at = 0
        for out in outs:
            out[...] = held[at : at + out.shape[0], :]
            at += out.shape[0]

    return call(
        kernel,
        [((each, cols), tiles.dtype)] * 2 + [((2 * each, cols), tiles.dtype)],
        [codes, tiles],
        "place_tiles",
        [pltpu.VMEM((rows, cols), tiles.dtype)],
        scalars=1,
    )


def place_out(codes, parts, visible):
    rows, cols = parts[0].shape
    total = 4 * rows

    def kernel(code_ref, own, near, far, out, held):
        for b, ref in enumerate(blocks_of((own, near, far))):
            held[b * rows : (b + 1) * rows, :] = ref[...]
        for k in range(total // visible):
            at = pl.multiple_of(code_ref[k] * visible, 16)
            out[k * visible : (k + 1) * visible, :] = held[pl.ds(at, visible), :]

    return call(
        kernel,
        [((total, cols), parts[0].dtype)],
        [codes] + parts,
        "return_tiles",
        [pltpu.VMEM((total, cols), parts[0].dtype)],
        scalars=1,
    )[0]


def blocks_of(crossed):
    own, near, far = crossed
    rows = own.shape[0]
    return [own, near.at[:rows], far.at[:rows], near.at[rows:]]


class Crossing:
    def __init__(self, own, near, far):
        self.own, self.near = own, near
        self.far = swap(far, "mp", 2)

    def relay(self, line):
        rows = self.own.shape[0]
        both = jnp.concatenate([self.near, line.wait(self.far)[rows:]], axis=0)
        line.mark(both)
        self.parts = [self.own, swap(both, "mp", 1), self.far]


def spread_kernel(tile_tokens, order, count, pos, mask_token, given, out):
    total = out.shape[0]
    slots = order.shape[0]
    visible = given.shape[0] // slots
    out[...] = jnp.broadcast_to(mask_token[...], out.shape)
    for slot in range(slots):
        tile = order[slot]
        start, rem = window_of(tile, tile_tokens, total)
        hot = hot_rows(pos, count[tile], tile, rem).astype(F32)
        shown = jnp.sum(hot, axis=1, keepdims=True) > 0.5
        rows = given[slot * visible : (slot + 1) * visible, :]
        new = dot(hot[:, :visible].astype(BF16), rows).astype(BF16)
        here = pl.ds(start, WINDOW)
        out[here, :] = jnp.where(shown, new, out[here, :])


def patch_kernel(tile_tokens, order, count, pos, cols, patches, given, out):
    total = out.shape[0]
    slots = order.shape[0]
    visible = given.shape[0] // slots

    def base_step(i, carry):
        at = pl.multiple_of(i * 336, 16)
        here = pl.ds(at, 336)
        out[here, :] = cols[0:1, :] + patches[here, :].astype(F32) * cols[1:2, :]
        return carry

    lax.fori_loop(0, total // 336, base_step, 0)
    for slot in range(slots):
        tile = order[slot]
        start, rem = window_of(tile, tile_tokens, total)
        hot = hot_rows(pos, count[tile], tile, rem).astype(F32)
        rows = given[slot * visible : (slot + 1) * visible, :]
        new = dot(hot[:, :visible].astype(BF16), rows)
        here = pl.ds(start, WINDOW)
        out[here, :] = out[here, :] + new * cols[2:3, :]


def sincos_table(limit, full_width):
    half_width = full_width // 2
    frequency = 1.0 / 10000.0 ** (np.arange(half_width, dtype=np.float32) / half_width)
    angles = np.arange(limit, dtype=np.float32)[:, None] * frequency.astype(np.float32)
    return np.concatenate([np.sin(angles), np.cos(angles)], axis=-1).astype(np.float32)


def place_table(full_width, frames):
    part = full_width // 16 * 6
    lines = 2 * SIDE
    table = np.zeros((2 * lines + frames, full_width), np.float32)
    table[:lines, :part] = sincos_table(lines, part)
    table[lines : 2 * lines, part : 2 * part] = sincos_table(lines, part)
    table[2 * lines :, 2 * part :] = sincos_table(frames, full_width - 2 * part)
    return table


def norm_forward(full_rows, gain_vec, bias_vec):
    values = full_rows.astype(F32)
    centred = values - jnp.mean(values, axis=-1, keepdims=True)
    inverse_std = lax.rsqrt(jnp.mean(centred * centred, axis=-1, keepdims=True) + norm_eps)
    unit_rows = centred * inverse_std
    normed_low = (unit_rows * gain_vec + bias_vec).astype(BF16)
    return (unit_rows, inverse_std, normed_low)


def row_sum(values):
    return jnp.sum(values.astype(F32), axis=0, keepdims=True)


def norm_backward(out_grad, unit_rows, inverse_std, gain_vec):
    scaled = out_grad * gain_vec
    first_mean = jnp.mean(scaled, axis=-1, keepdims=True)
    cross_mean = jnp.mean(scaled * unit_rows, axis=-1, keepdims=True)
    input_grad = inverse_std * (scaled - first_mean - unit_rows * cross_mean)
    return (input_grad, row_sum(out_grad * unit_rows), row_sum(out_grad))


def prep_kernel(odd, q, k, v, attn, hid, out, dec, embed, *refs):
    biases, (first, second, first_cut, second_cut) = refs[:-4], refs[-4:]
    e, w, h = embed.shape[0], q.shape[0], hid.shape[1]
    first[:e, :] = embed[...]
    for i, ref in enumerate((q, k, v)):
        first[e + i * w : e + (i + 1) * w, :] = ref[...]
    first[e + 3 * w : e + 4 * w, :] = attn[...]
    base = e + 4 * w
    first[base:, :] = jnp.zeros((first.shape[0] - base, first.shape[1]), BF16)
    for i, ref in enumerate(biases):
        first[base + i : base + i + 1, : ref.shape[1]] = ref[...]
    second[:h, :] = hid[...].T
    second[h : 2 * h, :] = out[...]
    second[2 * h :, :] = dec[...].T
    for whole, part in ((first, first_cut), (second, second_cut)):
        half = part.shape[0]
        part[...] = whole[pl.ds(pl.multiple_of(odd[0] * half, 16), half), :]


def copy_rows(target, refs, start, count):
    for e, ref in enumerate(refs):
        target[e * count : (e + 1) * count, :] = ref[start : start + count, :]


def normed_pixels(pix, cols):
    centred = pix[...].astype(F32) - cols[0:1, :]
    return centred, (centred * cols[1:2, :]).astype(BF16)


def embed_kernel(sizes, chosen, table, cols, vecs, mask, *refs):
    n, part, rows_s = sizes
    pix, weights = blocks_of(refs[:3]), split_blocks(refs[3], refs[4], n)
    start_ref, q_ref, k_ref, v_ref, probs, att_ref, middle, full = refs[5:]
    e_rows = pix[0].shape[1]
    rows, width = start_ref.shape
    total = dot(chosen[...], table[...]) + vecs[0:1, :]
    for e in range(n):
        total = total + dot(normed_pixels(pix[e], cols)[1], weights[e][:e_rows, :])
    live = chosen[:, 127:128].astype(F32) > 0.5
    start = jnp.where(live, total, 0.0).astype(BF16)
    start_ref[...] = start
    normed = norm_forward(start, vecs[1:2, :], vecs[2:3, :])[2]
    copy_rows(full, weights, e_rows, part)
    q_ref[...] = (dot_t(normed, full[...]) + vecs[3:4, :]).astype(BF16)
    copy_rows(full, weights, e_rows + part, part)
    k_ref[...] = dot_t(normed, full[...]).astype(BF16)
    copy_rows(full, weights, e_rows + 2 * part, part)
    v_ref[...] = (dot_t(normed, full[...]) + vecs[4:5, :]).astype(BF16)
    scale = HEAD_DIM ** (-0.5)
    low = lax.broadcasted_iota(jnp.int32, (rows_s, 128), 1) < HEAD_DIM
    zero = jnp.zeros((rows_s, 128), BF16)

    def pair_step(i, carry):
        s, p = i // (width // 128), i % (width // 128)
        here = pl.ds(pl.multiple_of(s * rows_s, 16), rows_s)
        lanes = pl.ds(pl.multiple_of(p * 128, 128), 128)
        q2, k2, v2 = q_ref[here, lanes], k_ref[here, lanes], v_ref[here, lanes]
        extra = mask[pl.ds(s, 1), :]
        got = jnp.zeros((rows_s, 128), F32)
        for h in range(2):
            keep = low if h == 0 else jnp.logical_not(low)
            scores = dot_t(q2, jnp.where(keep, k2, zero)) * scale
            scores = jnp.where(extra > 0.5, scores, big_negative)
            shifted = jnp.exp(scores - jnp.max(scores, axis=-1, keepdims=True))
            share = (shifted / jnp.sum(shifted, axis=-1, keepdims=True)).astype(BF16)
            probs[i * 2 + h] = share
            got = got + dot(share, jnp.where(keep, v2, zero))
        att_ref[here, lanes] = got.astype(BF16)
        return carry

    lax.fori_loop(0, (rows // rows_s) * (width // 128), pair_step, 0)
    copy_rows(full, weights, e_rows + 3 * part, part)
    middle[...] = start_ref[...].astype(F32) + dot(att_ref[...], full[...]) + vecs[5:6, :]


def gelu_pair(x):
    cdf = 0.5 * (1.0 + lax.erf(x * (2.0**-0.5)))
    pdf = jnp.exp(-0.5 * x * x) * float(1.0 / np.sqrt(2.0 * np.pi))
    return x * cdf, cdf + x * pdf


def split_blocks(kept, sent, n):
    count = 2 * kept.shape[0] // n
    return [
        (kept if e % 2 == 0 else sent).at[e // 2 * count : (e // 2 + 1) * count] for e in range(n)
    ]


def mlp_kernel(n, middle, vecs, bias_hid, bias_dec, *refs):
    cot, weights = blocks_of(refs[:3]), split_blocks(refs[3], refs[4], n)
    rows = middle.shape[0]
    decoded = [refs[5], refs[6], refs[7].at[:rows], refs[7].at[rows:]]
    pre_refs = refs[8 : 8 + n]
    kept, sent, final_grad, sums, hidden, slope = refs[8 + n :]
    grads = split_blocks(kept, sent, n)
    h = pre_refs[0].shape[1]
    dec = decoded[0].shape[1]
    normed = norm_forward(middle[...].astype(BF16), vecs[6:7, :], vecs[7:8, :])[2]
    total = middle[...] + vecs[8:9, :]
    for e in range(n):
        pre = dot_t(normed, weights[e][:h, :]) + bias_hid[e : e + 1, :]
        value, grad = gelu_pair(pre)
        value = value.astype(BF16)
        hidden[e] = value
        slope[e] = grad.astype(BF16)
        total = total + dot(value, weights[e][h : 2 * h, :])
    final = total.astype(BF16)
    back = jnp.zeros(total.shape, F32)
    sums[...] = jnp.zeros(sums.shape, F32)
    for e in range(n):
        w_dec = weights[e][2 * h :, :]
        decoded[e][...] = (dot_t(final, w_dec) + bias_dec[e : e + 1, :]).astype(BF16)
        back = back + dot(cot[e][...], w_dec)
        grads[e][h:, :] = dot_tl(cot[e][...], final).astype(BF16)
        sums[n + 1 + e : n + 2 + e, :dec] = row_sum(cot[e][...])
    final_grad[...] = back
    low = back.astype(BF16)
    sums[n : n + 1, :] = row_sum(low)
    for e in range(n):
        grads[e][:h, :] = dot_tl(hidden[e], low).astype(BF16)
        pre_grad = (dot_t(low, weights[e][h : 2 * h, :]) * slope[e].astype(F32)).astype(BF16)
        pre_refs[e][...] = pre_grad
        sums[e : e + 1, :] = row_sum(pre_grad)


def hidden_kernel(n, middle, vecs, final_grad, *refs):
    pre, weights = refs[:n], split_blocks(refs[n], refs[n + 1], n)
    kept, sent, middle_grad, sums = refs[n + 2 :]
    grads = split_blocks(kept, sent, n)
    h = pre[0].shape[1]
    unit, rstd, normed = norm_forward(middle[...].astype(BF16), vecs[6:7, :], vecs[7:8, :])
    total = jnp.zeros(unit.shape, F32)
    for e in range(n):
        total = total + dot(pre[e][...], weights[e][:h, :])
        grads[e][...] = dot_tl(pre[e][...], normed).astype(BF16)
    term, gain, bias = norm_backward(total, unit, rstd, vecs[6:7, :])
    middle_grad[...] = final_grad[...] + term
    sums[0:1, :] = gain
    sums[1:2, :] = bias
    sums[2:8, :] = jnp.zeros((6, sums.shape[1]), F32)


def attn_back_kernel(sizes, middle_grad, start, q, k, v, probs, chosen, vecs, *refs):
    n, part, rows_s, e_rows = sizes
    weights = split_blocks(refs[0], refs[1], n)
    start_grad, dq, dk, dv, sums, full, ag = refs[2:]
    rows, width = start.shape
    copy_rows(full, weights, e_rows + 3 * part, part)
    low_grad = middle_grad[...].astype(BF16)
    ag[...] = dot_t(low_grad, full[...]).astype(BF16)
    scale = HEAD_DIM ** (-0.5)
    low = lax.broadcasted_iota(jnp.int32, (rows_s, 128), 1) < HEAD_DIM
    zero = jnp.zeros((rows_s, 128), BF16)

    def pair_step(i, carry):
        s, p = i // (width // 128), i % (width // 128)
        here = pl.ds(pl.multiple_of(s * rows_s, 16), rows_s)
        lanes = pl.ds(pl.multiple_of(p * 128, 128), 128)
        q2, k2, v2, g2 = q[here, lanes], k[here, lanes], v[here, lanes], ag[here, lanes]
        tq = jnp.zeros((rows_s, 128), F32)
        tk = jnp.zeros((rows_s, 128), F32)
        tv = jnp.zeros((rows_s, 128), F32)
        for h in range(2):
            keep = low if h == 0 else jnp.logical_not(low)
            share = probs[i * 2 + h]
            wide = share.astype(F32)
            prob_grad = dot_t(g2, jnp.where(keep, v2, zero))
            delta = jnp.sum(wide * prob_grad, axis=-1, keepdims=True)
            score_grad = (wide * (prob_grad - delta)).astype(BF16)
            tv = tv + dot_tl(share, jnp.where(keep, g2, zero))
            tq = tq + dot(score_grad, jnp.where(keep, k2, zero))
            tk = tk + dot_tl(score_grad, jnp.where(keep, q2, zero))
        dq[here, lanes] = (tq * scale).astype(BF16)
        dk[here, lanes] = (tk * scale).astype(BF16)
        dv[here, lanes] = tv.astype(BF16)
        return carry

    lax.fori_loop(0, (rows // rows_s) * (width // 128), pair_step, 0)
    copy_rows(full, weights, e_rows, part)
    total = dot(dq[...], full[...])
    copy_rows(full, weights, e_rows + part, part)
    total = total + dot(dk[...], full[...])
    copy_rows(full, weights, e_rows + 2 * part, part)
    total = total + dot(dv[...], full[...])
    unit, rstd, _ = norm_forward(start[...], vecs[1:2, :], vecs[2:3, :])
    term, gain, bias = norm_backward(total, unit, rstd, vecs[1:2, :])
    live = chosen[:, 127:128].astype(F32) > 0.5
    grad = jnp.where(live, middle_grad[...] + term, 0.0).astype(BF16)
    start_grad[...] = grad
    sums[0:1, :] = gain
    sums[1:2, :] = bias
    sums[2:3, :] = row_sum(grad)
    sums[3:4, :] = row_sum(low_grad)
    sums[4:5, :] = row_sum(dq[...])
    sums[5:6, :] = row_sum(dv[...])
    sums[6:8, :] = jnp.zeros((2, width), F32)


def pixel_grad_kernel(n, start_grad, cols, *refs):
    pix, weights = blocks_of(refs[:3]), split_blocks(refs[3], refs[4], n)
    rows = start_grad.shape[0]
    grads, bands = [refs[5], refs[6], refs[7].at[:rows], refs[7].at[rows:]], refs[8]
    e_rows = pix[0].shape[1]
    first = jnp.zeros((1, e_rows), F32)
    second = jnp.zeros((1, e_rows), F32)
    for e in range(n):
        got = dot_t(start_grad[...], weights[e][:e_rows, :])
        grads[e][...] = got.astype(BF16)
        first = first + row_sum(got)
        second = second + row_sum(got * (pix[e][...].astype(F32) - cols[0:1, :]))
    bands[...] = band_sums(first, second)


def weight_grads(n, part, base, pairs, kept, sent):
    grads = split_blocks(kept, sent, n)
    for i, (left, right) in enumerate(pairs):
        whole = dot_tl(left[...], right).astype(BF16)
        for e in range(n):
            at = base + i * part
            grads[e][at : at + part, :] = whole[e * part : (e + 1) * part, :]


def weight_kernel(sizes, start_grad, middle_grad, start, att, dq, dk, dv, cols, vecs, *refs):
    n, part = sizes
    pix, (kept, sent) = blocks_of(refs[:3]), refs[3:]
    e_rows = pix[0].shape[1]
    normed = norm_forward(start[...], vecs[1:2, :], vecs[2:3, :])[2]
    low_grad = middle_grad[...].astype(BF16)
    pairs = ((dq, normed), (dk, normed), (dv, normed), (att, low_grad))
    weight_grads(n, part, e_rows, pairs, kept, sent)
    grads = split_blocks(kept, sent, n)
    for e in range(n):
        got = dot_tl(normed_pixels(pix[e], cols)[1], start_grad[...])
        grads[e][:e_rows, :] = got.astype(BF16)


def join_kernel(half, flag, own, direct, handed, out):
    rows = own.shape[0]
    out[:rows, :] = own[...]
    at = pl.multiple_of(rows + flag[0] * half, 16)
    out[pl.ds(at, half), :] = direct[...]
    at = pl.multiple_of(rows + (1 - flag[0]) * half, 16)
    out[pl.ds(at, half), :] = handed[...]


def pack_kernel(sizes, place, mlp_sums, hid_sums, attn_sums, bands, mask_rows, out):
    n, part = sizes
    me = place[0]
    dec, width = mask_rows.shape[1], out.shape[1]
    base = 5 * n
    row = lax.broadcasted_iota(jnp.int32, (base, width), 0)
    total = jnp.zeros((base, width), F32)

    def widened(values):
        return jnp.concatenate([values, jnp.zeros((1, width - values.shape[1]), F32)], axis=1)

    for e in range(n):
        at = e ^ me
        lanes = slice(e * part, (e + 1) * part)
        total = jnp.where(row == at, mlp_sums[e : e + 1, :], total)
        total = jnp.where(row == n + at, widened(attn_sums[4:5, lanes]), total)
        total = jnp.where(row == 2 * n + at, widened(attn_sums[5:6, lanes]), total)
        total = jnp.where(row == 3 * n + at, mlp_sums[n + 1 + e : n + 2 + e, :], total)
    total = jnp.where(row == 4 * n + me, widened(mask_rows[0:1, :]), total)
    out[:base, :] = total
    out[base : base + 4, :] = attn_sums[:4, :]
    out[base + 4 : base + 6, :] = hid_sums[:2, :]
    out[base + 6 : base + 7, :] = mlp_sums[n : n + 1, :]
    out[base + 7 :, :] = jnp.zeros((out.shape[0] - base - 7, width), F32)
    out[base + 7 : base + 9, :128] = bands[:2, :]


def write_out(plan, values, outs):
    at = 0
    for out, turned in zip(outs, plan):
        if turned:
            count = out.shape[1]
            out[...] = values[at : at + count, :].T.astype(F32)
        else:
            count = out.shape[0]
            out[...] = values[at : at + count, :].astype(F32)
        at += count


def finish_kernel(half, plan, flag, own, came, *refs):
    outs, held = refs[:-1], refs[-1]
    first = flag[0] == 0

    @pl.when(first)
    def _():
        held[:half, :] = own[...]
        held[half:, :] = came[...]

    @pl.when(jnp.logical_not(first))
    def _():
        held[:half, :] = came[...]
        held[half:, :] = own[...]

    write_out(plan, held, outs)


def band_sums(first, second):
    columns = first.shape[1]
    band = lax.broadcasted_iota(jnp.int32, (columns, 128), 0) % BANDS
    pick_band = (band == lax.broadcasted_iota(jnp.int32, band.shape, 1)).astype(F32)
    rows = jnp.concatenate([first, second, jnp.zeros((6, columns), F32)], axis=0)
    return jnp.dot(rows, pick_band, precision=lax.Precision.HIGHEST, preferred_element_type=F32)


def call(kernel, outs, args, name, scratch=(), us=2.0, scalars=0):
    run = pl.pallas_call(
        kernel,
        out_shape=[jax.ShapeDtypeStruct(shape, kind) for shape, kind in outs],
        in_specs=[SM] * scalars + [VM] * (len(args) - scalars),
        out_specs=[VM] * len(outs),
        scratch_shapes=list(scratch),
        compiler_params=params(),
        cost_estimate=pl.CostEstimate(
            flops=0, bytes_accessed=int(us * 3.3e6), transcendentals=0
        ),
        name=name,
    )
    return list(run(*args))


class Weights:
    def __init__(self, own, part, data_index):
        self.own, self.half = own, part.shape[0]
        self.flag = (data_index & 1).astype(jnp.int32)[None]
        self.direct = swap(part, "mp", 2)

    def hand_on(self):
        self.handed = swap(self.direct, "dp", 1)

    def join(self, line):
        rows, width = self.own.shape
        [both] = call(
            functools.partial(join_kernel, self.half),
            [((2 * rows, width), BF16)],
            [self.flag, self.own, self.direct, line.wait(self.handed)],
            "join_weights",
            us=3.0,
            scalars=1,
        )
        line.mark(both)
        self.pair = [both, swap(both, "mp", 1)]


def to_absolute(blocks, model_index):
    size = blocks.shape[0]
    for bit in bits_of("mp"):
        turned = jnp.stack([blocks[i ^ bit] for i in range(size)])
        blocks = jnp.where((model_index & bit) != 0, turned, blocks)
    return blocks


class Line:
    def __init__(self):
        self.last = None

    def wait(self, value):
        return value if self.last is None else after(value, self.last)

    def mark(self, value):
        self.last = value


class Reduction:
    def __init__(self, kept, sent, order, data_index, line, plan, shapes, name):
        self.kept, self.came = kept, swap(sent, "mp", 1)
        self.quarters, self.line, self.name = 2, line, name
        self.plan, self.shapes = plan, shapes
        self.flags = [((data_index >> k) & 1).astype(jnp.int32)[None] for k in range(len(bits_of("dp")))]
        self.order = list(order) + [k for k in range(len(self.flags)) if k not in order]
        self.done, self.own = [], None

    def step(self):
        if self.order or self.own is None:
            self.scatter()
        elif len(self.done) > 1:
            self.gather()
        else:
            self.finish()

    def scatter(self):
        came = self.line.wait(self.came)
        axis = self.order.pop(0) if self.order else None
        rows = self.kept.shape[0] // self.quarters
        if axis is None:
            [self.own] = self.stage(came, None, 0)
            self.line.mark(self.own)
            self.came = swap(self.own, "dp", 1 << self.done[-1])
        elif axis == "x":
            self.kept, sent = self.stage(came, None, rows)
            self.line.mark(self.kept)
            self.quarters = 1
            self.came = swap(sent, "mp", 2)
        else:
            self.kept, sent = self.stage(came, self.flags[axis], rows // 2)
            self.line.mark(self.kept)
            self.done.append(axis)
            self.came = swap(sent, "dp", 1 << axis)

    def stage(self, came, flag, half):
        total, width = self.kept.shape
        quarters, rows = self.quarters, total // self.quarters
        if flag is not None and half % 16:
            summed = (self.kept.astype(F32) + came.astype(F32)).astype(BF16)
            summed = summed.reshape(quarters, rows, width)
            own = lax.dynamic_slice_in_dim(summed, flag[0] * half, half, 1)
            other = lax.dynamic_slice_in_dim(summed, (1 - flag[0]) * half, half, 1)
            return own.reshape(-1, width), other.reshape(-1, width)

        def total_of(a, b, at, count):
            here = pl.ds(at, count)
            return (a[here, :].astype(F32) + b[here, :].astype(F32)).astype(BF16)

        if flag is None:

            def kernel(a, b, *outs):
                for k, out in enumerate(outs):
                    out[...] = total_of(a, b, k * out.shape[0], out.shape[0])

            count = 1 if half == 0 else 2
            return call(
                kernel, [((total // count, width), BF16)] * count, [self.kept, came], "reduce_" + self.name
            )

        def kernel(mine, a, b, own, other):
            for q in range(quarters):
                here = slice(q * half, (q + 1) * half)
                at = pl.multiple_of(q * rows + mine[0] * half, 16)
                own[here, :] = total_of(a, b, at, half)
                at = pl.multiple_of(q * rows + (1 - mine[0]) * half, 16)
                other[here, :] = total_of(a, b, at, half)

        return call(
            kernel,
            [((total // 2, width), BF16)] * 2,
            [flag, self.kept, came],
            "reduce_" + self.name,
            scalars=1,
        )

    def gather(self):
        axis = self.done.pop()
        came = self.line.wait(self.came)
        self.own = jnp.where(
            self.flags[axis][0] == 0,
            jnp.concatenate([self.own, came], axis=0),
            jnp.concatenate([came, self.own], axis=0),
        )
        self.line.mark(self.own)
        self.came = swap(self.own, "dp", 1 << self.done[-1])

    def finish(self):
        half, width = self.own.shape
        self.result = call(
            functools.partial(finish_kernel, half, self.plan),
            [(shape, F32) for shape in self.shapes],
            [self.flags[self.done[0]], self.own, self.line.wait(self.came)],
            "finish_" + self.name,
            [pltpu.VMEM((2 * half, width), BF16)],
            us=3.0,
            scalars=1,
        )
        self.line.mark(self.result[0])


class Sums:
    def __init__(self, values, line):
        self.values, self.line = values, line
        self.left = [(axis, bit) for axis in ("mp", "dp") for bit in bits_of(axis)]
        self.came = swap(values, *self.left[0])

    def step(self):
        self.values = self.values + self.line.wait(self.came)
        self.line.mark(self.values)
        self.left.pop(0)
        if self.left:
            self.came = swap(self.values, *self.left[0])


def exchange(tiles):
    size = lax.axis_size("dp")
    blocks = tiles.reshape(size, tiles.shape[0] // size, tiles.shape[1])
    return lax.all_to_all(blocks, "dp", split_axis=0, concat_axis=0, tiled=True).reshape(tiles.shape)


def shards(
    patches,
    vis_count,
    vis_pos,
    tile_sample,
    tile_quad,
    w_embed,
    b_embed,
    norm1_gain,
    norm1_bias,
    w_query,
    b_query,
    w_key,
    w_value,
    b_value,
    w_attn_out,
    b_attn_out,
    norm2_gain,
    norm2_bias,
    w_hidden,
    b_hidden,
    w_mlp_out,
    b_mlp_out,
    w_decoder,
    b_decoder,
    mask_token,
    cotangent,
):
    data_size = lax.axis_size("dp")
    model_size = lax.axis_size("mp")
    data_index = lax.axis_index("dp")
    model_index = lax.axis_index("mp")
    tile_count = vis_count.shape[0]
    visible = vis_pos.shape[1]
    grid_count, pixel_cols = patches.shape
    tile_tokens = grid_count // tile_count
    full_width = w_embed.shape[1]
    part_width = b_embed.shape[0]
    dec_part = b_decoder.shape[0]
    hid_part = b_hidden.shape[0]
    pair_tiles = tile_count // data_size
    own_samples = SAMP_OWN // model_size
    sample_rows = 4 * visible
    rows = own_samples * sample_rows
    my_tiles = own_samples * 4
    score_scale = HEAD_DIM ** (-0.5)

    tile_ids = jnp.arange(tile_count, dtype=jnp.int32)
    owners = tile_sample // SAMP_OWN
    earlier = (owners[:, None] == owners[None, :]) & (tile_ids[None, :] < tile_ids[:, None])
    tile_ranks = jnp.sum(earlier.astype(jnp.int32), axis=1)
    slot_of = owners * pair_tiles + tile_ranks
    at_slot = slot_of[None, :] == tile_ids[:, None]
    order = jnp.sum(jnp.where(at_slot, tile_ids[None, :], 0), axis=1)
    tile_code = (tile_sample % SAMP_OWN) * 4 + tile_quad
    pos_wide = jnp.pad(vis_pos, ((0, 0), (0, 128 - visible)), constant_values=-1000)

    line = Line()
    [stats] = call(stats_kernel, [((8, 128), F32)], [patches], "band_sums", us=4.0)
    stats = stats + swap(stats, "mp", 1)
    stats = stats + swap(stats, "mp", 2)

    small = [b_embed, b_query, b_value, b_attn_out, b_mlp_out, b_decoder, b_hidden]
    base = pixel_cols + 4 * part_width
    own_first, own_second, cut_first, cut_second = call(
        prep_kernel,
        [((base + 32, full_width), BF16), ((2 * hid_part + dec_part, full_width), BF16)]
        + [(((base + 32) // 2, full_width), BF16), (((2 * hid_part + dec_part) // 2, full_width), BF16)],
        [(data_index & 1).astype(jnp.int32)[None]]
        + [w_query.T, w_key.T, w_value.T, w_attn_out, w_hidden, w_mlp_out, w_decoder]
        + [after(w_embed, stats)]
        + [v[None, :] for v in small],
        "prep_weights",
        us=5.0,
        scalars=1,
    )
    line.mark(own_first)
    first_w = Weights(own_first, cut_first, data_index)
    by_slot = jnp.where(at_slot, 1.0, 0.0)
    codes_slot = jnp.sum(by_slot * tile_code.astype(F32)[None, :], axis=1)
    counts_slot = jnp.sum(by_slot * vis_count.astype(F32)[None, :], axis=1)
    pos_slot = jnp.sum(by_slot[:, :, None] * vis_pos.astype(F32)[None, :, :], axis=1)
    info = jnp.concatenate([codes_slot[None], counts_slot[None]], axis=0)
    info = jnp.pad(info, ((0, 6), (0, 128 - tile_count)))
    packet = jnp.concatenate([stats, info, pos_slot.reshape(-1, 128)], axis=0)[None]
    for k, bit in enumerate(bits_of("dp")):
        came = swap(packet, "dp", bit)
        if k == 0:
            picked, cot_picked, mask_rows = call(
                functools.partial(pick_kernel, tile_tokens),
                [
                    ((tile_count * visible, pixel_cols), BF16),
                    ((tile_count * visible, dec_part), BF16),
                    ((8, dec_part), F32),
                ],
                [line.wait(order), vis_count, pos_wide, patches, cotangent],
                "pick_rows",
                us=7.5,
                scalars=2,
            )
            came = after(came, picked)
        packet = jnp.where(
            (data_index >> k) & 1 == 0,
            jnp.concatenate([packet, came], axis=0),
            jnp.concatenate([came, packet], axis=0),
        )

    arrived = exchange(after(picked, packet))

    second_w = Weights(own_second, after(cut_second, first_w.direct), data_index)
    first_w.hand_on()
    second_w.hand_on()

    own_info = lax.dynamic_slice_in_dim(packet[:, 8:10], data_index * pair_tiles, pair_tiles, 2)
    own_info = own_info.transpose(1, 0, 2).reshape(2, tile_count).astype(jnp.int32)
    my_tiles_bit = model_index * my_tiles
    codes = own_info[0] ^ my_tiles_bit
    line = Line()
    line.mark(second_w.direct)
    first_w.join(line)
    own, near, far = place_in(codes, line.wait(arrived), visible, model_size)
    line.mark(far)
    pix = Crossing(own, near, far)
    arrived_cot = exchange(after(cot_picked, far))
    pix.relay(line)
    own, near, far = place_in(codes, line.wait(arrived_cot), visible, model_size)
    line.mark(far)
    cot = Crossing(own, near, far)
    second_w.join(line)

    bias_rel = [first_w.pair[e % 2][e // 2 * own_first.shape[0] + base :][:16] for e in range(4)]
    bias_rel = jnp.stack(bias_rel).astype(F32)
    bias_abs = to_absolute(bias_rel, model_index)

    def rel_vec(k):
        return bias_rel[:, k, : small[k].shape[0]].reshape(1, -1)

    def abs_vec(k):
        return bias_abs[:, k, : small[k].shape[0]].reshape(1, -1)

    gains = [norm1_gain, norm1_bias, norm2_gain, norm2_bias]
    gains = [v[None].astype(F32) for v in gains]
    vecs = jnp.concatenate(
        [abs_vec(0), gains[0], gains[1], rel_vec(1), rel_vec(2), abs_vec(3)]
        + [gains[2], gains[3], abs_vec(4), jnp.zeros((7, full_width), F32)]
    )
    bias_hid, bias_dec = bias_rel[:, 6, :hid_part], bias_rel[:, 5, :dec_part]

    total = jnp.sum(packet[:, :2, :BANDS], axis=0)
    per_band = float(grid_count * data_size * (pixel_cols // BANDS) * model_size)
    band_mean = total[0] / per_band
    band_var = total[1] / per_band - band_mean * band_mean
    band_rstd = lax.rsqrt(band_var + band_eps)
    mean_cols = jnp.tile(band_mean, pixel_cols // BANDS)
    rstd_cols = jnp.tile(band_rstd, pixel_cols // BANDS)

    own_pos = packet[:, 16:].reshape(data_size, tile_count, visible)
    own_pos = lax.dynamic_slice_in_dim(own_pos, data_index * pair_tiles, pair_tiles, 1)
    own_pos = own_pos.reshape(tile_count, visible)
    mine = (codes[None, :] == jnp.arange(my_tiles)[:, None]).astype(F32)
    my_counts = jnp.sum(mine * own_info[1].astype(F32)[None, :], axis=1)
    my_pos = jnp.sum(mine[:, :, None] * own_pos[None], axis=1)
    my_pos = my_pos.astype(jnp.int32)
    live = jnp.arange(visible)[None, :] < my_counts.astype(jnp.int32)[:, None]
    live_col = live.reshape(rows, 1)
    usable = live.reshape(own_samples, sample_rows)
    quadrant = (jnp.arange(my_tiles) % 4)[:, None]
    inner = my_pos % (SIDE * SIDE)
    frames = tile_tokens // (SIDE * SIDE)
    col_at = quadrant % 2 * SIDE + inner % SIDE
    row_at = quadrant // 2 * SIDE + inner // SIDE + 2 * SIDE
    frame_at = my_pos // (SIDE * SIDE) + 4 * SIDE
    table = place_table(full_width, frames)
    high = table.astype(jnp.bfloat16)
    low = (table - high.astype(np.float32)).astype(jnp.bfloat16)
    wide = np.zeros((128, full_width), jnp.bfloat16)
    wide[: table.shape[0]], wide[64 : 64 + table.shape[0]] = high, low
    lane = jnp.arange(128)[None, :]
    spots = jnp.where(lane < 127, lane % 64, -1)
    chosen = (
        (col_at.reshape(rows, 1) == spots)
        | (row_at.reshape(rows, 1) == spots)
        | (frame_at.reshape(rows, 1) == spots)
        | ((lane == 127) & live_col)
    ).astype(BF16)
    key_mask = jnp.pad(usable.astype(F32), ((0, 8 - own_samples), (0, 0)))
    cols = jnp.pad(jnp.stack([mean_cols, rstd_cols]), ((0, 6), (0, 0)))

    square = ((rows, full_width), BF16)
    wide_rows = ((rows, full_width), F32)
    heads = own_samples * full_width // HEAD_DIM
    weight_scratch = pltpu.VMEM((full_width, full_width), BF16)
    start, queries, key_rows, value_rows, probs, attended, middle = call(
        functools.partial(embed_kernel, (model_size, part_width, sample_rows)),
        [square] * 4 + [((heads, sample_rows, sample_rows), BF16), square, wide_rows],
        [chosen, jnp.asarray(wide), cols, vecs, line.wait(key_mask)] + pix.parts + first_w.pair,
        "embed_attend",
        [weight_scratch],
        us=19.0,
    )
    line.mark(middle)
    cot.relay(line)
    decoded_shape = ((rows, dec_part), BF16)
    hidden_shape = ((rows, hid_part), BF16)
    out = call(
        functools.partial(mlp_kernel, model_size),
        [decoded_shape] * 2
        + [((2 * rows, dec_part), BF16)]
        + [hidden_shape] * model_size
        + [((2 * (hid_part + dec_part), full_width), BF16)] * 2
        + [wide_rows, ((16, full_width), F32)],
        [middle, vecs, bias_hid, bias_dec] + cot.parts + second_w.pair,
        "mlp_decode",
        [pltpu.VMEM((model_size, rows, hid_part), BF16)] * 2,
        us=20.0,
    )
    decoded_rows, pre_grads = out[:3], out[3 : 3 + model_size]
    out_kept, out_sent, final_grad, mlp_sums = out[3 + model_size :]
    red_a = Reduction(
        out_kept,
        out_sent,
        ["x", 0, 1, 2],
        data_index,
        line,
        (False, True),
        [w_mlp_out.shape, w_decoder.shape],
        "out",
    )
    out = call(
        functools.partial(hidden_kernel, model_size),
        [((2 * hid_part, full_width), BF16)] * 2 + [wide_rows, ((8, full_width), F32)],
        [middle, vecs, final_grad] + pre_grads + second_w.pair,
        "hidden_back",
        us=13.0,
    )
    hid_kept, hid_sent, middle_grad, hid_sums = out
    line.mark(middle_grad)
    red_b = Reduction(
        hid_kept, hid_sent, ["x", 0, 1, 2], data_index, line, (True,), [w_hidden.shape], "hidden"
    )
    red_a.step()
    start_grad, dq, dk, dv, attn_sums = call(
        functools.partial(attn_back_kernel, (model_size, part_width, sample_rows, pixel_cols)),
        [square] * 4 + [((8, full_width), F32)],
        [line.wait(middle_grad), start, queries, key_rows, value_rows]
        + [probs, chosen, vecs]
        + first_w.pair,
        "attend_back",
        [weight_scratch, pltpu.VMEM((rows, full_width), BF16)],
        us=18.0,
    )
    line.mark(start_grad)
    out = call(
        functools.partial(pixel_grad_kernel, model_size),
        [((rows, pixel_cols), BF16)] * 2 + [((2 * rows, pixel_cols), BF16), ((8, 128), F32)],
        [line.wait(start_grad), cols] + pix.parts + first_w.pair,
        "pixel_grad",
        us=6.7,
    )
    normed_grad, bands = out[:3], out[3]
    line.mark(bands)
    grad_mp = Crossing(*normed_grad)
    red_a.step()
    first_kept, first_sent = call(
        functools.partial(weight_kernel, (model_size, part_width)),
        [((2 * base, full_width), BF16)] * 2,
        [line.wait(start_grad), middle_grad, start, attended, dq, dk, dv, cols, vecs] + pix.parts,
        "weight_grad",
        us=10.0,
    )
    line.mark(first_kept)
    grad_mp.relay(line)
    [sums] = call(
        functools.partial(pack_kernel, (model_size, part_width)),
        [((32, full_width), F32)],
        [model_index.astype(jnp.int32)[None], mlp_sums, hid_sums, attn_sums, line.wait(bands)]
        + [mask_rows],
        "pack_sums",
        us=1.5,
        scalars=1,
    )
    line.mark(sums)
    sums = Sums(sums, line)
    red_c = Reduction(
        first_kept,
        first_sent,
        ["x", 0, 1, 2],
        data_index,
        line,
        (False,) * 5,
        [w_embed.shape] + [w_attn_out.shape] * 4,
        "first",
    )

    def go_home(crossing):
        parts = crossing.parts
        tiles = place_out(codes, [parts[0], line.wait(parts[1]), parts[2]], visible)
        line.mark(tiles)
        return exchange(tiles)

    def patch_step():
        bands_all = sums.values[5 * model_size + 7 : 5 * model_size + 9, :BANDS]
        grad_all, cross_all = bands_all[0], bands_all[1]
        grad_var = -0.5 * cross_all * band_rstd * band_rstd * band_rstd
        grad_mean = -band_rstd * grad_all - 2.0 * band_mean * grad_var
        terms = jnp.stack([grad_mean / per_band, 2.0 * grad_var / per_band, band_rstd])
        terms = jnp.pad(jnp.tile(terms, (1, pixel_cols // BANDS)), ((0, 5), (0, 0)))
        out = call(
            functools.partial(patch_kernel, tile_tokens),
            [((grid_count, pixel_cols), F32)],
            [order, vis_count, pos_wide, terms, patches, line.wait(grad_dp)],
            "spread_patch_grad",
            us=8.0,
            scalars=2,
        )
        line.mark(out[0])
        return out

    def decoded_step():
        out = call(
            functools.partial(spread_kernel, tile_tokens),
            [((grid_count, dec_part), BF16)],
            [order, vis_count, pos_wide, mask_token[None, :], line.wait(decoded_dp)],
            "spread_decoded",
            us=3.5,
            scalars=2,
        )
        line.mark(out[0])
        return out

    def steps(*chains):
        for chain in chains:
            chain.step()

    steps(sums)
    grad_dp = go_home(grad_mp)
    steps(sums, red_c, red_a, red_b, sums, red_a, sums, red_a)
    while sums.left:
        sums.step()
    steps(red_c, red_a, red_a, red_c, red_b)
    [patch_grad] = patch_step()
    steps(red_c, red_b, red_a, red_c, red_b, red_c)
    decoded_mp = Crossing(decoded_rows[0], decoded_rows[1], line.wait(decoded_rows[2]))
    steps(red_b, red_c)
    decoded_mp.relay(line)
    steps(red_b)
    decoded_dp = go_home(decoded_mp)
    steps(red_b)
    while not all(hasattr(chain, "result") for chain in (red_a, red_b, red_c)):
        for chain in (red_a, red_c, red_b):
            if not hasattr(chain, "result"):
                chain.step()
    [decoded] = decoded_step()

    n = model_size
    sums = sums.values
    own_rows = [
        lax.dynamic_slice_in_dim(sums, model_index + k * n, 1, 0)[0] for k in range(5)
    ]
    sum_hidden = own_rows[0]
    sum_query, sum_value = own_rows[1][:part_width], own_rows[2][:part_width]
    sum_dec, grad_mask_token = own_rows[3][:dec_part], own_rows[4][:dec_part]
    gain_one, bias_one, embed_sum, attn_out_sum, gain_two, bias_two, mlp_out_sum = (
        sums[5 * n + k] for k in range(7)
    )

    def mine_of(vector):
        part = vector.shape[0] // model_size
        return lax.dynamic_slice_in_dim(vector, model_index * part, part, 0)

    (g_out, g_dec), [g_hid] = red_a.result, red_b.result
    g_embed, g_query, g_key, g_value, g_attn = red_c.result

    return (
        decoded,
        patch_grad,
        g_embed,
        mine_of(embed_sum),
        gain_one,
        bias_one,
        g_query.T,
        sum_query,
        g_key.T,
        g_value.T,
        sum_value,
        g_attn,
        mine_of(attn_out_sum),
        gain_two,
        bias_two,
        g_hid,
        sum_hidden,
        g_out,
        mine_of(mlp_out_sum),
        g_dec,
        sum_dec,
        grad_mask_token,
    )


def solution(mesh):
    in_specs = (
        P("dp", "mp"),
        P("dp"),
        P("dp", None),
        P("dp"),
        P("dp"),
        P("mp", None),
        P("mp"),
        P(),
        P(),
        P(None, "mp"),
        P("mp"),
        P(None, "mp"),
        P(None, "mp"),
        P("mp"),
        P("mp", None),
        P("mp"),
        P(),
        P(),
        P(None, "mp"),
        P("mp"),
        P("mp", None),
        P("mp"),
        P(None, "mp"),
        P("mp"),
        P("mp"),
        P("dp", "mp"),
    )
    out_specs = (
        P("dp", "mp"),
        P("dp", "mp"),
        P("mp", None),
        P("mp"),
        P(),
        P(),
        P(None, "mp"),
        P("mp"),
        P(None, "mp"),
        P(None, "mp"),
        P("mp"),
        P("mp", None),
        P("mp"),
        P(),
        P(),
        P(None, "mp"),
        P("mp"),
        P("mp", None),
        P("mp"),
        P(None, "mp"),
        P("mp"),
        P("mp"),
    )
    return jax.shard_map(shards, mesh=mesh, in_specs=in_specs, out_specs=out_specs, check_vma=False)
```

```python
import functools

import jax
import jax.numpy as jnp
import numpy as np
from jax import lax
from jax.experimental import pallas as pl
from jax.experimental.pallas import tpu as pltpu
from jax.sharding import PartitionSpec as P

HEAD_DIM = 64
BANDS = 6
SIDE = 7
SAMP_OWN = 8
WINDOW = 176
VMEM_BYTES = 56 * 1024 * 1024

norm_eps = 1e-06
band_eps = 1e-06
big_negative = -1000000000.0
F32 = jnp.float32
BF16 = jnp.bfloat16


def params():
    return pltpu.CompilerParams(vmem_limit_bytes=VMEM_BYTES)


VM = pl.BlockSpec(memory_space=pltpu.VMEM)
SM = pl.BlockSpec(memory_space=pltpu.SMEM)


def swap(values, axis, bit):
    size = lax.axis_size(axis)
    return lax.ppermute(values, axis, [(i, i ^ bit) for i in range(size)])


def bits_of(axis):
    size = lax.axis_size(axis)
    return [1 << k for k in range(size.bit_length() - 1)]


def after(value, *before):
    return lax.optimization_barrier((value,) + before)[0]


def dot(left, right):
    return jnp.dot(left, right, preferred_element_type=F32)


def dot_t(left, right):
    return lax.dot_general(left, right, (((1,), (1,)), ((), ())), preferred_element_type=F32)


def dot_tl(left, right):
    return lax.dot_general(left, right, (((0,), (0,)), ((), ())), preferred_element_type=F32)


def window_of(tile, tile_tokens, total):
    base = tile * tile_tokens
    start = jnp.minimum((base // 16) * 16, total - WINDOW)
    return pl.multiple_of(start, 16), base - start


def hot_rows(pos_ref, count, tile, rem):
    lane = lax.broadcasted_iota(jnp.int32, (1, 128), 1)
    target = jnp.where(lane < count, pos_ref[pl.ds(tile, 1), :] + rem, -1)
    row = lax.broadcasted_iota(jnp.int32, (WINDOW, 128), 0)
    return row == target


def stats_kernel(patches, stats):
    def sum_step(i, carry):
        first, second = carry
        at = pl.multiple_of(i * 336, 16)
        x = patches[pl.ds(at, 336), :].astype(F32).reshape(42, 8, patches.shape[1])
        return first + jnp.sum(x, axis=0), second + jnp.sum(x * x, axis=0)

    blank = jnp.zeros((8, patches.shape[1]), F32)
    first, second = lax.fori_loop(0, patches.shape[0] // 336, sum_step, (blank, blank))
    stats[...] = band_sums(
        jnp.sum(first, axis=0, keepdims=True), jnp.sum(second, axis=0, keepdims=True)
    )


def pick_kernel(tile_tokens, order, count, pos, patches, cot, picked, cot_picked, mask_sum):
    total = patches.shape[0]
    slots = order.shape[0]
    visible = picked.shape[0] // slots
    mask_total = jnp.zeros((8, cot.shape[1]), F32)
    row = lax.broadcasted_iota(jnp.int32, (WINDOW, 128), 0)
    lane = lax.broadcasted_iota(jnp.int32, (WINDOW, 128), 1)
    for slot in range(slots):
        tile = order[slot]
        start, rem = window_of(tile, tile_tokens, total)
        hot = hot_rows(pos, count[tile], tile, rem).astype(F32)
        shown = jnp.sum(hot, axis=1, keepdims=True)
        inside = jnp.logical_and(row >= rem, row < rem + tile_tokens)
        hidden = jnp.where(inside, 1.0 - shown, 0.0)
        chooser = jnp.where(lane == visible, hidden, hot).astype(BF16)
        got = dot_tl(chooser, patches[pl.ds(start, WINDOW), :])
        got_cot = dot_tl(chooser, cot[pl.ds(start, WINDOW), :])
        here = slice(slot * visible, (slot + 1) * visible)
        picked[here, :] = got[:visible].astype(BF16)
        cot_picked[here, :] = got_cot[:visible].astype(BF16)
        mask_total = mask_total + got_cot[visible : visible + 8]
    mask_sum[...] = mask_total


def place_in(codes, tiles, visible, blocks):
    rows, cols = tiles.shape
    each = rows // blocks

    def kernel(code_ref, tile_ref, *refs):
        outs, held = refs[:-1], refs[-1]
        for k in range(rows // visible):
            at = pl.multiple_of(code_ref[k] * visible, 16)
            held[pl.ds(at, visible), :] = tile_ref[k * visible : (k + 1) * visible, :]
        at = 0
        for out in outs:
            out[...] = held[at : at + out.shape[0], :]
            at += out.shape[0]

    return call(
        kernel,
        [((each, cols), tiles.dtype)] * 2 + [((2 * each, cols), tiles.dtype)],
        [codes, tiles],
        "place_tiles",
        [pltpu.VMEM((rows, cols), tiles.dtype)],
        scalars=1,
    )


def place_out(codes, parts, visible):
    rows, cols = parts[0].shape
    total = 4 * rows

    def kernel(code_ref, own, near, far, out, held):
        for b, ref in enumerate(blocks_of((own, near, far))):
            held[b * rows : (b + 1) * rows, :] = ref[...]
        for k in range(total // visible):
            at = pl.multiple_of(code_ref[k] * visible, 16)
            out[k * visible : (k + 1) * visible, :] = held[pl.ds(at, visible), :]

    return call(
        kernel,
        [((total, cols), parts[0].dtype)],
        [codes] + parts,
        "return_tiles",
        [pltpu.VMEM((total, cols), parts[0].dtype)],
        scalars=1,
    )[0]


def blocks_of(crossed):
    own, near, far = crossed
    rows = own.shape[0]
    return [own, near.at[:rows], far.at[:rows], near.at[rows:]]


class Crossing:
    def __init__(self, own, near, far):
        self.own, self.near = own, near
        self.far = swap(far, "mp", 2)

    def relay(self, line):
        rows = self.own.shape[0]
        both = jnp.concatenate([self.near, line.wait(self.far)[rows:]], axis=0)
        line.mark(both)
        self.parts = [self.own, swap(both, "mp", 1), self.far]


def spread_kernel(tile_tokens, order, count, pos, mask_token, given, out):
    total = out.shape[0]
    slots = order.shape[0]
    visible = given.shape[0] // slots
    out[...] = jnp.broadcast_to(mask_token[...], out.shape)
    for slot in range(slots):
        tile = order[slot]
        start, rem = window_of(tile, tile_tokens, total)
        hot = hot_rows(pos, count[tile], tile, rem).astype(F32)
        shown = jnp.sum(hot, axis=1, keepdims=True) > 0.5
        rows = given[slot * visible : (slot + 1) * visible, :]
        new = dot(hot[:, :visible].astype(BF16), rows).astype(BF16)
        here = pl.ds(start, WINDOW)
        out[here, :] = jnp.where(shown, new, out[here, :])


def patch_kernel(tile_tokens, order, count, pos, cols, patches, given, out):
    total = out.shape[0]
    slots = order.shape[0]
    visible = given.shape[0] // slots

    def base_step(i, carry):
        at = pl.multiple_of(i * 336, 16)
        here = pl.ds(at, 336)
        out[here, :] = cols[0:1, :] + patches[here, :].astype(F32) * cols[1:2, :]
        return carry

    lax.fori_loop(0, total // 336, base_step, 0)
    for slot in range(slots):
        tile = order[slot]
        start, rem = window_of(tile, tile_tokens, total)
        hot = hot_rows(pos, count[tile], tile, rem).astype(F32)
        rows = given[slot * visible : (slot + 1) * visible, :]
        new = dot(hot[:, :visible].astype(BF16), rows)
        here = pl.ds(start, WINDOW)
        out[here, :] = out[here, :] + new * cols[2:3, :]


def sincos_table(limit, full_width):
    half_width = full_width // 2
    frequency = 1.0 / 10000.0 ** (np.arange(half_width, dtype=np.float32) / half_width)
    angles = np.arange(limit, dtype=np.float32)[:, None] * frequency.astype(np.float32)
    return np.concatenate([np.sin(angles), np.cos(angles)], axis=-1).astype(np.float32)


def place_table(full_width, frames):
    part = full_width // 16 * 6
    lines = 2 * SIDE
    table = np.zeros((2 * lines + frames, full_width), np.float32)
    table[:lines, :part] = sincos_table(lines, part)
    table[lines : 2 * lines, part : 2 * part] = sincos_table(lines, part)
    table[2 * lines :, 2 * part :] = sincos_table(frames, full_width - 2 * part)
    return table


def norm_forward(full_rows, gain_vec, bias_vec):
    values = full_rows.astype(F32)
    centred = values - jnp.mean(values, axis=-1, keepdims=True)
    inverse_std = lax.rsqrt(jnp.mean(centred * centred, axis=-1, keepdims=True) + norm_eps)
    unit_rows = centred * inverse_std
    normed_low = (unit_rows * gain_vec + bias_vec).astype(BF16)
    return (unit_rows, inverse_std, normed_low)


def row_sum(values):
    return jnp.sum(values.astype(F32), axis=0, keepdims=True)


def norm_backward(out_grad, unit_rows, inverse_std, gain_vec):
    scaled = out_grad * gain_vec
    first_mean = jnp.mean(scaled, axis=-1, keepdims=True)
    cross_mean = jnp.mean(scaled * unit_rows, axis=-1, keepdims=True)
    input_grad = inverse_std * (scaled - first_mean - unit_rows * cross_mean)
    return (input_grad, row_sum(out_grad * unit_rows), row_sum(out_grad))


def prep_kernel(odd, q, k, v, attn, hid, out, dec, embed, *refs):
    biases, (first, second, first_cut, second_cut) = refs[:-4], refs[-4:]
    e, w, h = embed.shape[0], q.shape[0], hid.shape[1]
    first[:e, :] = embed[...]
    for i, ref in enumerate((q, k, v)):
        first[e + i * w : e + (i + 1) * w, :] = ref[...]
    first[e + 3 * w : e + 4 * w, :] = attn[...]
    base = e + 4 * w
    first[base:, :] = jnp.zeros((first.shape[0] - base, first.shape[1]), BF16)
    for i, ref in enumerate(biases):
        first[base + i : base + i + 1, : ref.shape[1]] = ref[...]
    second[:h, :] = hid[...].T
    second[h : 2 * h, :] = out[...]
    second[2 * h :, :] = dec[...].T
    for whole, part in ((first, first_cut), (second, second_cut)):
        half = part.shape[0]
        part[...] = whole[pl.ds(pl.multiple_of(odd[0] * half, 16), half), :]


def copy_rows(target, refs, start, count):
    for e, ref in enumerate(refs):
        target[e * count : (e + 1) * count, :] = ref[start : start + count, :]


def normed_pixels(pix, cols):
    centred = pix[...].astype(F32) - cols[0:1, :]
    return centred, (centred * cols[1:2, :]).astype(BF16)


def embed_kernel(sizes, chosen, table, cols, vecs, mask, *refs):
    n, part, rows_s = sizes
    pix, weights = blocks_of(refs[:3]), refs[3 : 3 + n]
    start_ref, q_ref, k_ref, v_ref, probs, att_ref, middle, full = refs[3 + n :]
    e_rows = pix[0].shape[1]
    rows, width = start_ref.shape
    total = dot(chosen[...], table[...]) + vecs[0:1, :]
    for e in range(n):
        total = total + dot(normed_pixels(pix[e], cols)[1], weights[e][:e_rows, :])
    live = chosen[:, 127:128].astype(F32) > 0.5
    start = jnp.where(live, total, 0.0).astype(BF16)
    start_ref[...] = start
    normed = norm_forward(start, vecs[1:2, :], vecs[2:3, :])[2]
    copy_rows(full, weights, e_rows, part)
    q_ref[...] = (dot_t(normed, full[...]) + vecs[3:4, :]).astype(BF16)
    copy_rows(full, weights, e_rows + part, part)
    k_ref[...] = dot_t(normed, full[...]).astype(BF16)
    copy_rows(full, weights, e_rows + 2 * part, part)
    v_ref[...] = (dot_t(normed, full[...]) + vecs[4:5, :]).astype(BF16)
    scale = HEAD_DIM ** (-0.5)
    low = lax.broadcasted_iota(jnp.int32, (rows_s, 128), 1) < HEAD_DIM
    zero = jnp.zeros((rows_s, 128), BF16)

    def pair_step(i, carry):
        s, p = i // (width // 128), i % (width // 128)
        here = pl.ds(pl.multiple_of(s * rows_s, 16), rows_s)
        lanes = pl.ds(pl.multiple_of(p * 128, 128), 128)
        q2, k2, v2 = q_ref[here, lanes], k_ref[here, lanes], v_ref[here, lanes]
        extra = mask[pl.ds(s, 1), :]
        got = jnp.zeros((rows_s, 128), F32)
        for h in range(2):
            keep = low if h == 0 else jnp.logical_not(low)
            scores = dot_t(q2, jnp.where(keep, k2, zero)) * scale
            scores = jnp.where(extra > 0.5, scores, big_negative)
            shifted = jnp.exp(scores - jnp.max(scores, axis=-1, keepdims=True))
            share = (shifted / jnp.sum(shifted, axis=-1, keepdims=True)).astype(BF16)
            probs[i * 2 + h] = share
            got = got + dot(share, jnp.where(keep, v2, zero))
        att_ref[here, lanes] = got.astype(BF16)
        return carry

    lax.fori_loop(0, (rows // rows_s) * (width // 128), pair_step, 0)
    copy_rows(full, weights, e_rows + 3 * part, part)
    middle[...] = start_ref[...].astype(F32) + dot(att_ref[...], full[...]) + vecs[5:6, :]


def gelu_pair(x):
    cdf = 0.5 * (1.0 + lax.erf(x * (2.0**-0.5)))
    pdf = jnp.exp(-0.5 * x * x) * float(1.0 / np.sqrt(2.0 * np.pi))
    return x * cdf, cdf + x * pdf


def split_blocks(kept, sent, n):
    count = 2 * kept.shape[0] // n
    return [
        (kept if e % 2 == 0 else sent).at[e // 2 * count : (e // 2 + 1) * count] for e in range(n)
    ]


def mlp_kernel(n, middle, vecs, bias_hid, bias_dec, *refs):
    cot, weights, refs = blocks_of(refs[:3]), refs[3 : 3 + n], refs[3 + n :]
    rows = middle.shape[0]
    decoded = [refs[0], refs[1], refs[2].at[:rows], refs[2].at[rows:]]
    pre_refs = refs[3 : 3 + n]
    kept, sent, final_grad, sums, hidden, slope = refs[3 + n :]
    grads = split_blocks(kept, sent, n)
    h = pre_refs[0].shape[1]
    dec = decoded[0].shape[1]
    normed = norm_forward(middle[...].astype(BF16), vecs[6:7, :], vecs[7:8, :])[2]
    total = middle[...] + vecs[8:9, :]
    for e in range(n):
        pre = dot_t(normed, weights[e][:h, :]) + bias_hid[e : e + 1, :]
        value, grad = gelu_pair(pre)
        value = value.astype(BF16)
        hidden[e] = value
        slope[e] = grad.astype(BF16)
        total = total + dot(value, weights[e][h : 2 * h, :])
    final = total.astype(BF16)
    back = jnp.zeros(total.shape, F32)
    sums[...] = jnp.zeros(sums.shape, F32)
    for e in range(n):
        w_dec = weights[e][2 * h :, :]
        decoded[e][...] = (dot_t(final, w_dec) + bias_dec[e : e + 1, :]).astype(BF16)
        back = back + dot(cot[e][...], w_dec)
        grads[e][h:, :] = dot_tl(cot[e][...], final).astype(BF16)
        sums[n + 1 + e : n + 2 + e, :dec] = row_sum(cot[e][...])
    final_grad[...] = back
    low = back.astype(BF16)
    sums[n : n + 1, :] = row_sum(low)
    for e in range(n):
        grads[e][:h, :] = dot_tl(hidden[e], low).astype(BF16)
        pre_grad = (dot_t(low, weights[e][h : 2 * h, :]) * slope[e].astype(F32)).astype(BF16)
        pre_refs[e][...] = pre_grad
        sums[e : e + 1, :] = row_sum(pre_grad)


def hidden_kernel(n, middle, vecs, final_grad, att, *refs):
    pre, weights = refs[:n], refs[n : 2 * n]
    kept, sent, middle_grad, sums = refs[2 * n :]
    grads = split_blocks(kept, sent, n)
    h = pre[0].shape[1]
    unit, rstd, normed = norm_forward(middle[...].astype(BF16), vecs[6:7, :], vecs[7:8, :])
    total = jnp.zeros(unit.shape, F32)
    for e in range(n):
        total = total + dot(pre[e][...], weights[e][:h, :])
        grads[e][:h, :] = dot_tl(pre[e][...], normed).astype(BF16)
    term, gain, bias = norm_backward(total, unit, rstd, vecs[6:7, :])
    middle_grad[...] = final_grad[...] + term
    part = kept.shape[0] // 2 - h
    low_grad = middle_grad[...].astype(BF16)
    weight_grads(n, part, h, ((att, low_grad),), kept, sent)
    sums[0:1, :] = gain
    sums[1:2, :] = bias
    sums[2:8, :] = jnp.zeros((6, sums.shape[1]), F32)


def attn_back_kernel(sizes, middle_grad, start, q, k, v, probs, chosen, vecs, *refs):
    n, part, rows_s, e_rows = sizes
    weights = refs[:n]
    start_grad, dq, dk, dv, sums, full, ag = refs[n:]
    rows, width = start.shape
    copy_rows(full, weights, e_rows + 3 * part, part)
    low_grad = middle_grad[...].astype(BF16)
    ag[...] = dot_t(low_grad, full[...]).astype(BF16)
    scale = HEAD_DIM ** (-0.5)
    low = lax.broadcasted_iota(jnp.int32, (rows_s, 128), 1) < HEAD_DIM
    zero = jnp.zeros((rows_s, 128), BF16)

    def pair_step(i, carry):
        s, p = i // (width // 128), i % (width // 128)
        here = pl.ds(pl.multiple_of(s * rows_s, 16), rows_s)
        lanes = pl.ds(pl.multiple_of(p * 128, 128), 128)
        q2, k2, v2, g2 = q[here, lanes], k[here, lanes], v[here, lanes], ag[here, lanes]
        tq = jnp.zeros((rows_s, 128), F32)
        tk = jnp.zeros((rows_s, 128), F32)
        tv = jnp.zeros((rows_s, 128), F32)
        for h in range(2):
            keep = low if h == 0 else jnp.logical_not(low)
            share = probs[i * 2 + h]
            wide = share.astype(F32)
            prob_grad = dot_t(g2, jnp.where(keep, v2, zero))
            delta = jnp.sum(wide * prob_grad, axis=-1, keepdims=True)
            score_grad = (wide * (prob_grad - delta)).astype(BF16)
            tv = tv + dot_tl(share, jnp.where(keep, g2, zero))
            tq = tq + dot(score_grad, jnp.where(keep, k2, zero))
            tk = tk + dot_tl(score_grad, jnp.where(keep, q2, zero))
        dq[here, lanes] = (tq * scale).astype(BF16)
        dk[here, lanes] = (tk * scale).astype(BF16)
        dv[here, lanes] = tv.astype(BF16)
        return carry

    lax.fori_loop(0, (rows // rows_s) * (width // 128), pair_step, 0)
    copy_rows(full, weights, e_rows, part)
    total = dot(dq[...], full[...])
    copy_rows(full, weights, e_rows + part, part)
    total = total + dot(dk[...], full[...])
    copy_rows(full, weights, e_rows + 2 * part, part)
    total = total + dot(dv[...], full[...])
    unit, rstd, _ = norm_forward(start[...], vecs[1:2, :], vecs[2:3, :])
    term, gain, bias = norm_backward(total, unit, rstd, vecs[1:2, :])
    live = chosen[:, 127:128].astype(F32) > 0.5
    grad = jnp.where(live, middle_grad[...] + term, 0.0).astype(BF16)
    start_grad[...] = grad
    sums[0:1, :] = gain
    sums[1:2, :] = bias
    sums[2:3, :] = row_sum(grad)
    sums[3:4, :] = row_sum(low_grad)
    sums[4:5, :] = row_sum(dq[...])
    sums[5:6, :] = row_sum(dv[...])
    sums[6:8, :] = jnp.zeros((2, width), F32)


def pixel_grad_kernel(n, start_grad, cols, *refs):
    pix, weights, refs = blocks_of(refs[:3]), refs[3 : 3 + n], refs[3 + n :]
    rows = start_grad.shape[0]
    grads, bands = [refs[0], refs[1], refs[2].at[:rows], refs[2].at[rows:]], refs[3]
    e_rows = pix[0].shape[1]
    first = jnp.zeros((1, e_rows), F32)
    second = jnp.zeros((1, e_rows), F32)
    for e in range(n):
        got = dot_t(start_grad[...], weights[e][:e_rows, :])
        grads[e][...] = got.astype(BF16)
        first = first + row_sum(got)
        second = second + row_sum(got * (pix[e][...].astype(F32) - cols[0:1, :]))
    bands[...] = band_sums(first, second)


def weight_grads(n, part, base, pairs, kept, sent):
    grads = split_blocks(kept, sent, n)
    for i, (left, right) in enumerate(pairs):
        whole = dot_tl(left[...], right).astype(BF16)
        for e in range(n):
            at = base + i * part
            grads[e][at : at + part, :] = whole[e * part : (e + 1) * part, :]


def weight_kernel(sizes, start_grad, start, dq, dk, dv, cols, vecs, *refs):
    n, part = sizes
    pix, (kept, sent) = blocks_of(refs[:3]), refs[3:]
    e_rows = pix[0].shape[1]
    normed = norm_forward(start[...], vecs[1:2, :], vecs[2:3, :])[2]
    pairs = ((dq, normed), (dk, normed), (dv, normed))
    weight_grads(n, part, e_rows, pairs, kept, sent)
    grads = split_blocks(kept, sent, n)
    for e in range(n):
        got = dot_tl(normed_pixels(pix[e], cols)[1], start_grad[...])
        grads[e][:e_rows, :] = got.astype(BF16)


def join_kernel(half, flag, direct, handed, out):
    at = pl.multiple_of(flag[0] * half, 16)
    out[pl.ds(at, half), :] = direct[...]
    at = pl.multiple_of((1 - flag[0]) * half, 16)
    out[pl.ds(at, half), :] = handed[...]


def pack_kernel(sizes, place, mlp_sums, hid_sums, attn_sums, bands, mask_rows, out):
    n, part = sizes
    me = place[0]
    dec, width = mask_rows.shape[1], out.shape[1]
    base = 5 * n
    row = lax.broadcasted_iota(jnp.int32, (base, width), 0)
    total = jnp.zeros((base, width), F32)

    def widened(values):
        return jnp.concatenate([values, jnp.zeros((1, width - values.shape[1]), F32)], axis=1)

    for e in range(n):
        at = e ^ me
        lanes = slice(e * part, (e + 1) * part)
        total = jnp.where(row == at, mlp_sums[e : e + 1, :], total)
        total = jnp.where(row == n + at, widened(attn_sums[4:5, lanes]), total)
        total = jnp.where(row == 2 * n + at, widened(attn_sums[5:6, lanes]), total)
        total = jnp.where(row == 3 * n + at, mlp_sums[n + 1 + e : n + 2 + e, :], total)
    total = jnp.where(row == 4 * n + me, widened(mask_rows[0:1, :]), total)
    out[:base, :] = total
    out[base : base + 4, :] = attn_sums[:4, :]
    out[base + 4 : base + 6, :] = hid_sums[:2, :]
    out[base + 6 : base + 7, :] = mlp_sums[n : n + 1, :]
    out[base + 7 :, :] = jnp.zeros((out.shape[0] - base - 7, width), F32)
    out[base + 7 : base + 9, :128] = bands[:2, :]


def write_out(plan, values, outs):
    at = 0
    for out, turned in zip(outs, plan):
        if turned:
            count = out.shape[1]
            out[...] = values[at : at + count, :].T.astype(F32)
        else:
            count = out.shape[0]
            out[...] = values[at : at + count, :].astype(F32)
        at += count


def finish_kernel(half, plan, flag, own, came, *refs):
    outs, held = refs[:-1], refs[-1]
    first = flag[0] == 0

    @pl.when(first)
    def _():
        held[:half, :] = own[...]
        held[half:, :] = came[...]

    @pl.when(jnp.logical_not(first))
    def _():
        held[:half, :] = came[...]
        held[half:, :] = own[...]

    write_out(plan, held, outs)


def band_sums(first, second):
    columns = first.shape[1]
    band = lax.broadcasted_iota(jnp.int32, (columns, 128), 0) % BANDS
    pick_band = (band == lax.broadcasted_iota(jnp.int32, band.shape, 1)).astype(F32)
    rows = jnp.concatenate([first, second, jnp.zeros((6, columns), F32)], axis=0)
    return jnp.dot(rows, pick_band, precision=lax.Precision.HIGHEST, preferred_element_type=F32)


def call(kernel, outs, args, name, scratch=(), us=2.0, scalars=0):
    run = pl.pallas_call(
        kernel,
        out_shape=[jax.ShapeDtypeStruct(shape, kind) for shape, kind in outs],
        in_specs=[SM] * scalars + [VM] * (len(args) - scalars),
        out_specs=[VM] * len(outs),
        scratch_shapes=list(scratch),
        compiler_params=params(),
        cost_estimate=pl.CostEstimate(
            flops=0, bytes_accessed=int(us * 3.3e6), transcendentals=0
        ),
        name=name,
    )
    return list(run(*args))


class Weights:
    def __init__(self, own, part, data_index):
        self.own, self.half = own, part.shape[0]
        self.flag = (data_index & 1).astype(jnp.int32)[None]
        self.direct = swap(part, "mp", 2)
        self.near = swap(own, "mp", 1)

    def hand_on(self):
        self.handed = swap(self.direct, "dp", 1)

    def join(self, line):
        rows, width = self.own.shape
        [far] = call(
            functools.partial(join_kernel, self.half),
            [((rows, width), BF16)],
            [self.flag, self.direct, line.wait(self.handed)],
            "join_weights",
            us=2.0,
            scalars=1,
        )
        line.mark(far)
        self.blocks = [self.own, self.near, far, swap(far, "mp", 1)]


def to_absolute(blocks, model_index):
    size = blocks.shape[0]
    for bit in bits_of("mp"):
        turned = jnp.stack([blocks[i ^ bit] for i in range(size)])
        blocks = jnp.where((model_index & bit) != 0, turned, blocks)
    return blocks


class Line:
    def __init__(self):
        self.last = None

    def wait(self, value):
        return value if self.last is None else after(value, self.last)

    def mark(self, value):
        self.last = value


class Reduction:
    def __init__(self, kept, sent, order, data_index, line, plan, shapes, name):
        self.kept, self.came = kept, swap(sent, "mp", 1)
        self.quarters, self.line, self.name = 2, line, name
        self.plan, self.shapes = plan, shapes
        self.flags = [((data_index >> k) & 1).astype(jnp.int32)[None] for k in range(len(bits_of("dp")))]
        self.order = list(order) + [k for k in range(len(self.flags)) if k not in order]
        self.done, self.own, self.hold = [], None, False

    def step(self):
        if self.order or self.own is None:
            self.scatter()
        elif len(self.done) > 1:
            self.gather()
        else:
            self.finish()

    def scatter(self):
        came = self.line.wait(self.came)
        axis = self.order.pop(0) if self.order else None
        rows = self.kept.shape[0] // self.quarters
        if axis is None:
            [self.own] = self.stage(came, None, 0)
            self.line.mark(self.own)
            self.came = swap(self.own, "dp", 1 << self.done[-1][0])
        elif axis == "x":
            self.kept, sent = self.stage(came, None, rows)
            self.line.mark(self.kept)
            self.quarters = 1
            self.sent = sent
            if not self.hold:
                self.launch()
        else:
            self.kept, sent = self.stage(came, self.flags[axis], rows // 2)
            self.line.mark(self.kept)
            self.done.append((axis, int(self.kept.shape[1] < came.shape[1])))
            self.came = swap(sent, "dp", 1 << axis)

    def launch(self, *before):
        self.came = swap(after(self.sent, *before) if before else self.sent, "mp", 2)

    def stage(self, came, flag, half):
        total, width = self.kept.shape
        quarters, rows = self.quarters, total // self.quarters
        if flag is not None and half % 16 and width % 256 == 0:
            part = width // 2

            def kernel(mine, a, b, own, other):
                for out, which in ((own, mine[0]), (other, 1 - mine[0])):
                    here = pl.ds(pl.multiple_of(which * part, 128), part)
                    out[...] = (a[:, here].astype(F32) + b[:, here].astype(F32)).astype(BF16)

            return call(
                kernel,
                [((total, part), BF16)] * 2,
                [flag, self.kept, came],
                "reduce_" + self.name,
                scalars=1,
            )
        if flag is not None and half % 16:
            summed = (self.kept.astype(F32) + came.astype(F32)).astype(BF16)
            summed = summed.reshape(quarters, rows, width)
            own = lax.dynamic_slice_in_dim(summed, flag[0] * half, half, 1)
            other = lax.dynamic_slice_in_dim(summed, (1 - flag[0]) * half, half, 1)
            return own.reshape(-1, width), other.reshape(-1, width)

        def total_of(a, b, at, count):
            here = pl.ds(at, count)
            return (a[here, :].astype(F32) + b[here, :].astype(F32)).astype(BF16)

        if flag is None:

            def kernel(a, b, *outs):
                for k, out in enumerate(outs):
                    out[...] = total_of(a, b, k * out.shape[0], out.shape[0])

            count = 1 if half == 0 else 2
            return call(
                kernel, [((total // count, width), BF16)] * count, [self.kept, came], "reduce_" + self.name
            )

        def kernel(mine, a, b, own, other):
            for q in range(quarters):
                here = slice(q * half, (q + 1) * half)
                at = pl.multiple_of(q * rows + mine[0] * half, 16)
                own[here, :] = total_of(a, b, at, half)
                at = pl.multiple_of(q * rows + (1 - mine[0]) * half, 16)
                other[here, :] = total_of(a, b, at, half)

        return call(
            kernel,
            [((total // 2, width), BF16)] * 2,
            [flag, self.kept, came],
            "reduce_" + self.name,
            scalars=1,
        )

    def gather(self):
        axis, dim = self.done.pop()
        came = self.line.wait(self.came)
        self.own = jnp.where(
            self.flags[axis][0] == 0,
            jnp.concatenate([self.own, came], axis=dim),
            jnp.concatenate([came, self.own], axis=dim),
        )
        self.line.mark(self.own)
        self.came = swap(self.own, "dp", 1 << self.done[-1][0])

    def finish(self):
        half, width = self.own.shape
        self.result = call(
            functools.partial(finish_kernel, half, self.plan),
            [(shape, F32) for shape in self.shapes],
            [self.flags[self.done[0][0]], self.own, self.line.wait(self.came)],
            "finish_" + self.name,
            [pltpu.VMEM((2 * half, width), BF16)],
            us=3.0,
            scalars=1,
        )
        self.line.mark(self.result[0])


class Sums:
    def __init__(self, values, line):
        self.values, self.line = values, line
        self.left = [(axis, bit) for axis in ("mp", "dp") for bit in bits_of(axis)]
        self.came = swap(values, *self.left[0])

    def step(self):
        self.values = self.values + self.line.wait(self.came)
        self.line.mark(self.values)
        self.left.pop(0)
        if self.left:
            self.came = swap(self.values, *self.left[0])


def exchange(tiles):
    size = lax.axis_size("dp")
    blocks = tiles.reshape(size, tiles.shape[0] // size, tiles.shape[1])
    return lax.all_to_all(blocks, "dp", split_axis=0, concat_axis=0, tiled=True).reshape(tiles.shape)


def shards(
    patches,
    vis_count,
    vis_pos,
    tile_sample,
    tile_quad,
    w_embed,
    b_embed,
    norm1_gain,
    norm1_bias,
    w_query,
    b_query,
    w_key,
    w_value,
    b_value,
    w_attn_out,
    b_attn_out,
    norm2_gain,
    norm2_bias,
    w_hidden,
    b_hidden,
    w_mlp_out,
    b_mlp_out,
    w_decoder,
    b_decoder,
    mask_token,
    cotangent,
):
    data_size = lax.axis_size("dp")
    model_size = lax.axis_size("mp")
    data_index = lax.axis_index("dp")
    model_index = lax.axis_index("mp")
    tile_count = vis_count.shape[0]
    visible = vis_pos.shape[1]
    grid_count, pixel_cols = patches.shape
    tile_tokens = grid_count // tile_count
    full_width = w_embed.shape[1]
    part_width = b_embed.shape[0]
    dec_part = b_decoder.shape[0]
    hid_part = b_hidden.shape[0]
    pair_tiles = tile_count // data_size
    own_samples = SAMP_OWN // model_size
    sample_rows = 4 * visible
    rows = own_samples * sample_rows
    my_tiles = own_samples * 4
    score_scale = HEAD_DIM ** (-0.5)

    tile_ids = jnp.arange(tile_count, dtype=jnp.int32)
    owners = tile_sample // SAMP_OWN
    earlier = (owners[:, None] == owners[None, :]) & (tile_ids[None, :] < tile_ids[:, None])
    tile_ranks = jnp.sum(earlier.astype(jnp.int32), axis=1)
    slot_of = owners * pair_tiles + tile_ranks
    at_slot = slot_of[None, :] == tile_ids[:, None]
    order = jnp.sum(jnp.where(at_slot, tile_ids[None, :], 0), axis=1)
    tile_code = (tile_sample % SAMP_OWN) * 4 + tile_quad
    pos_wide = jnp.pad(vis_pos, ((0, 0), (0, 128 - visible)), constant_values=-1000)

    line = Line()
    [stats] = call(stats_kernel, [((8, 128), F32)], [patches], "band_sums", us=4.0)
    stats = stats + swap(stats, "mp", 1)
    stats = stats + swap(stats, "mp", 2)

    small = [b_embed, b_query, b_value, b_attn_out, b_mlp_out, b_decoder, b_hidden]
    base = pixel_cols + 4 * part_width
    own_first, own_second, cut_first, cut_second = call(
        prep_kernel,
        [((base + 32, full_width), BF16), ((2 * hid_part + dec_part, full_width), BF16)]
        + [(((base + 32) // 2, full_width), BF16), (((2 * hid_part + dec_part) // 2, full_width), BF16)],
        [(data_index & 1).astype(jnp.int32)[None]]
        + [w_query.T, w_key.T, w_value.T, w_attn_out, w_hidden, w_mlp_out, w_decoder]
        + [after(w_embed, stats)]
        + [v[None, :] for v in small],
        "prep_weights",
        us=5.0,
        scalars=1,
    )
    line.mark(own_first)
    first_w = Weights(own_first, cut_first, data_index)
    by_slot = jnp.where(at_slot, 1.0, 0.0)
    codes_slot = jnp.sum(by_slot * tile_code.astype(F32)[None, :], axis=1)
    counts_slot = jnp.sum(by_slot * vis_count.astype(F32)[None, :], axis=1)
    pos_slot = jnp.sum(by_slot[:, :, None] * vis_pos.astype(F32)[None, :, :], axis=1)
    info = jnp.concatenate([codes_slot[None], counts_slot[None]], axis=0)
    info = jnp.pad(info, ((0, 6), (0, 128 - tile_count)))
    packet = jnp.concatenate([stats, info, pos_slot.reshape(-1, 128)], axis=0)[None]
    for k, bit in enumerate(bits_of("dp")):
        came = swap(packet, "dp", bit)
        if k == 0:
            picked, cot_picked, mask_rows = call(
                functools.partial(pick_kernel, tile_tokens),
                [
                    ((tile_count * visible, pixel_cols), BF16),
                    ((tile_count * visible, dec_part), BF16),
                    ((8, dec_part), F32),
                ],
                [line.wait(order), vis_count, pos_wide, patches, cotangent],
                "pick_rows",
                us=7.5,
                scalars=2,
            )
            came = after(came, picked)
        packet = jnp.where(
            (data_index >> k) & 1 == 0,
            jnp.concatenate([packet, came], axis=0),
            jnp.concatenate([came, packet], axis=0),
        )

    arrived = exchange(after(picked, packet, first_w.direct))

    second_w = Weights(own_second, after(cut_second, first_w.direct), data_index)
    first_w.hand_on()
    second_w.hand_on()

    own_info = lax.dynamic_slice_in_dim(packet[:, 8:10], data_index * pair_tiles, pair_tiles, 2)
    own_info = own_info.transpose(1, 0, 2).reshape(2, tile_count).astype(jnp.int32)
    my_tiles_bit = model_index * my_tiles
    codes = own_info[0] ^ my_tiles_bit
    total = jnp.sum(packet[:, :2, :BANDS], axis=0)
    per_band = float(grid_count * data_size * (pixel_cols // BANDS) * model_size)
    band_mean = total[0] / per_band
    band_var = total[1] / per_band - band_mean * band_mean
    band_rstd = lax.rsqrt(band_var + band_eps)
    mean_cols = jnp.tile(band_mean, pixel_cols // BANDS)
    rstd_cols = jnp.tile(band_rstd, pixel_cols // BANDS)

    own_pos = packet[:, 16:].reshape(data_size, tile_count, visible)
    own_pos = lax.dynamic_slice_in_dim(own_pos, data_index * pair_tiles, pair_tiles, 1)
    own_pos = own_pos.reshape(tile_count, visible)
    mine = (codes[None, :] == jnp.arange(my_tiles)[:, None]).astype(F32)
    my_counts = jnp.sum(mine * own_info[1].astype(F32)[None, :], axis=1)
    my_pos = jnp.sum(mine[:, :, None] * own_pos[None], axis=1)
    my_pos = my_pos.astype(jnp.int32)
    live = jnp.arange(visible)[None, :] < my_counts.astype(jnp.int32)[:, None]
    live_col = live.reshape(rows, 1)
    usable = live.reshape(own_samples, sample_rows)
    quadrant = (jnp.arange(my_tiles) % 4)[:, None]
    inner = my_pos % (SIDE * SIDE)
    frames = tile_tokens // (SIDE * SIDE)
    col_at = quadrant % 2 * SIDE + inner % SIDE
    row_at = quadrant // 2 * SIDE + inner // SIDE + 2 * SIDE
    frame_at = my_pos // (SIDE * SIDE) + 4 * SIDE
    table = place_table(full_width, frames)
    high = table.astype(jnp.bfloat16)
    low = (table - high.astype(np.float32)).astype(jnp.bfloat16)
    wide = np.zeros((128, full_width), jnp.bfloat16)
    wide[: table.shape[0]], wide[64 : 64 + table.shape[0]] = high, low
    lane = jnp.arange(128)[None, :]
    spots = jnp.where(lane < 127, lane % 64, -1)
    chosen = (
        (col_at.reshape(rows, 1) == spots)
        | (row_at.reshape(rows, 1) == spots)
        | (frame_at.reshape(rows, 1) == spots)
        | ((lane == 127) & live_col)
    ).astype(BF16)
    key_mask = jnp.pad(usable.astype(F32), ((0, 8 - own_samples), (0, 0)))
    cols = jnp.pad(jnp.stack([mean_cols, rstd_cols]), ((0, 6), (0, 0)))

    line = Line()
    held = after(arrived, second_w.direct, chosen, key_mask, cols)
    own, near, far = place_in(codes, held, visible, model_size)
    line.mark(far)
    pix = Crossing(own, near, far)
    arrived_cot = exchange(after(cot_picked, far))
    first_w.join(line)
    pix.relay(line)
    line.mark(pix.parts[1])
    bias_rel = [first_w.blocks[e][base : base + 16] for e in range(4)]
    bias_rel = jnp.stack(bias_rel).astype(F32)
    bias_abs = to_absolute(bias_rel, model_index)

    def rel_vec(k):
        return bias_rel[:, k, : small[k].shape[0]].reshape(1, -1)

    def abs_vec(k):
        return bias_abs[:, k, : small[k].shape[0]].reshape(1, -1)

    gains = [norm1_gain, norm1_bias, norm2_gain, norm2_bias]
    gains = [v[None].astype(F32) for v in gains]
    vecs = jnp.concatenate(
        [abs_vec(0), gains[0], gains[1], rel_vec(1), rel_vec(2), abs_vec(3)]
        + [gains[2], gains[3], abs_vec(4), jnp.zeros((7, full_width), F32)]
    )
    bias_hid, bias_dec = bias_rel[:, 6, :hid_part], bias_rel[:, 5, :dec_part]

    square = ((rows, full_width), BF16)
    wide_rows = ((rows, full_width), F32)
    heads = own_samples * full_width // HEAD_DIM
    weight_scratch = pltpu.VMEM((full_width, full_width), BF16)
    start, queries, key_rows, value_rows, probs, attended, middle = call(
        functools.partial(embed_kernel, (model_size, part_width, sample_rows)),
        [square] * 4 + [((heads, sample_rows, sample_rows), BF16), square, wide_rows],
        [chosen, jnp.asarray(wide), cols, vecs, line.wait(key_mask)] + pix.parts + first_w.blocks,
        "embed_attend",
        [weight_scratch],
        us=19.0,
    )
    line.mark(middle)
    own, near, far = place_in(codes, line.wait(arrived_cot), visible, model_size)
    line.mark(far)
    cot = Crossing(own, near, far)
    second_w.join(line)
    cot.relay(line)
    decoded_shape = ((rows, dec_part), BF16)
    hidden_shape = ((rows, hid_part), BF16)
    out = call(
        functools.partial(mlp_kernel, model_size),
        [decoded_shape] * 2
        + [((2 * rows, dec_part), BF16)]
        + [hidden_shape] * model_size
        + [((2 * (hid_part + dec_part), full_width), BF16)] * 2
        + [wide_rows, ((16, full_width), F32)],
        [middle, vecs, bias_hid, bias_dec] + cot.parts + second_w.blocks,
        "mlp_decode",
        [pltpu.VMEM((model_size, rows, hid_part), BF16)] * 2,
        us=20.0,
    )
    decoded_rows, pre_grads = out[:3], out[3 : 3 + model_size]
    out_kept, out_sent, final_grad, mlp_sums = out[3 + model_size :]
    decoded_mp = Crossing(*decoded_rows)
    red_a = Reduction(
        out_kept,
        out_sent,
        ["x", 0, 1, 2],
        data_index,
        line,
        (False, True),
        [w_mlp_out.shape, w_decoder.shape],
        "out",
    )
    def decoded_step(decoded_dp):
        out = call(
            functools.partial(spread_kernel, tile_tokens),
            [((grid_count, dec_part), BF16)],
            [order, vis_count, pos_wide, mask_token[None, :], line.wait(decoded_dp)],
            "spread_decoded",
            us=3.5,
            scalars=2,
        )
        line.mark(out[0])
        return out

    def go_home(crossing):
        parts = crossing.parts
        tiles = place_out(codes, [parts[0], line.wait(parts[1]), parts[2]], visible)
        line.mark(tiles)
        return exchange(tiles)

    out = call(
        functools.partial(hidden_kernel, model_size),
        [((2 * (hid_part + part_width), full_width), BF16)] * 2 + [wide_rows, ((8, full_width), F32)],
        [middle, vecs, final_grad, attended] + pre_grads + second_w.blocks,
        "hidden_back",
        us=13.0,
    )
    hid_kept, hid_sent, middle_grad, hid_sums = out
    line.mark(middle_grad)
    red_b = Reduction(
        hid_kept, hid_sent, ["x", 0, 1, 2], data_index, line, (True, False), [w_hidden.shape, w_attn_out.shape], "hidden"
    )
    decoded_mp.relay(line)
    red_a.step()
    start_grad, dq, dk, dv, attn_sums = call(
        functools.partial(attn_back_kernel, (model_size, part_width, sample_rows, pixel_cols)),
        [square] * 4 + [((8, full_width), F32)],
        [line.wait(middle_grad), start, queries, key_rows, value_rows]
        + [probs, chosen, vecs]
        + first_w.blocks,
        "attend_back",
        [weight_scratch, pltpu.VMEM((rows, full_width), BF16)],
        us=18.0,
    )
    line.mark(start_grad)
    decoded_dp = go_home(decoded_mp)
    out = call(
        functools.partial(pixel_grad_kernel, model_size),
        [((rows, pixel_cols), BF16)] * 2 + [((2 * rows, pixel_cols), BF16), ((8, 128), F32)],
        [line.wait(start_grad), cols] + pix.parts + first_w.blocks,
        "pixel_grad",
        us=6.7,
    )
    normed_grad, bands = out[:3], out[3]
    line.mark(bands)
    grad_mp = Crossing(*normed_grad)
    [sums] = call(
        functools.partial(pack_kernel, (model_size, part_width)),
        [((32, full_width), F32)],
        [model_index.astype(jnp.int32)[None], mlp_sums, hid_sums, attn_sums, line.wait(bands)]
        + [mask_rows],
        "pack_sums",
        us=1.5,
        scalars=1,
    )
    line.mark(sums)
    sums = Sums(sums, line)
    sums.step()
    red_b.hold = True
    red_b.step()
    red_a.step()
    spread = decoded_step(decoded_dp)
    first_kept, first_sent = call(
        functools.partial(weight_kernel, (model_size, part_width)),
        [((2 * (base - part_width), full_width), BF16)] * 2,
        [line.wait(start_grad), start, dq, dk, dv, cols, vecs] + pix.parts,
        "weight_grad",
        us=10.0,
    )
    line.mark(first_kept)
    grad_mp.relay(line)
    sums.step()
    red_b.launch(sums.values)
    red_c = Reduction(
        first_kept,
        line.wait(first_sent),
        ["x", 0, 1, 2],
        data_index,
        line,
        (False,) * 4,
        [w_embed.shape] + [w_attn_out.shape] * 3,
        "first",
    )

    def patch_step(grad_dp):
        bands_all = sums.values[5 * model_size + 7 : 5 * model_size + 9, :BANDS]
        grad_all, cross_all = bands_all[0], bands_all[1]
        grad_var = -0.5 * cross_all * band_rstd * band_rstd * band_rstd
        grad_mean = -band_rstd * grad_all - 2.0 * band_mean * grad_var
        terms = jnp.stack([grad_mean / per_band, 2.0 * grad_var / per_band, band_rstd])
        terms = jnp.pad(jnp.tile(terms, (1, pixel_cols // BANDS)), ((0, 5), (0, 0)))
        out = call(
            functools.partial(patch_kernel, tile_tokens),
            [((grid_count, pixel_cols), F32)],
            [order, vis_count, pos_wide, terms, patches, line.wait(grad_dp)],
            "spread_patch_grad",
            us=8.0,
            scalars=2,
        )
        line.mark(out[0])
        return out

    def steps(*chains):
        for chain in chains:
            chain.step()

    kept = {}

    def go(name):
        if name in chains:
            chains[name].step()
        elif name == "H":
            kept["grad"] = go_home(grad_mp)
        elif name == "P":
            while sums.left:
                sums.step()
            kept["patch"] = patch_step(kept["grad"])
    chains = {"a": red_a, "b": red_b, "c": red_c, "s": sums}
    for name in "HcasbasbascaPbacbbccabcbcc":
        go(name)
    while sums.left:
        sums.step()
    while not all(hasattr(chain, "result") for chain in (red_a, red_b, red_c)):
        for chain in (red_a, red_b, red_c):
            if not hasattr(chain, "result"):
                chain.step()
    [patch_grad], [decoded] = kept["patch"], spread

    n = model_size
    sums = sums.values
    own_rows = [
        lax.dynamic_slice_in_dim(sums, model_index + k * n, 1, 0)[0] for k in range(5)
    ]
    sum_hidden = own_rows[0]
    sum_query, sum_value = own_rows[1][:part_width], own_rows[2][:part_width]
    sum_dec, grad_mask_token = own_rows[3][:dec_part], own_rows[4][:dec_part]
    gain_one, bias_one, embed_sum, attn_out_sum, gain_two, bias_two, mlp_out_sum = (
        sums[5 * n + k] for k in range(7)
    )

    def mine_of(vector):
        part = vector.shape[0] // model_size
        return lax.dynamic_slice_in_dim(vector, model_index * part, part, 0)

    (g_out, g_dec), (g_hid, g_attn) = red_a.result, red_b.result
    g_embed, g_query, g_key, g_value = red_c.result

    return (
        decoded,
        patch_grad,
        g_embed,
        mine_of(embed_sum),
        gain_one,
        bias_one,
        g_query.T,
        sum_query,
        g_key.T,
        g_value.T,
        sum_value,
        g_attn,
        mine_of(attn_out_sum),
        gain_two,
        bias_two,
        g_hid,
        sum_hidden,
        g_out,
        mine_of(mlp_out_sum),
        g_dec,
        sum_dec,
        grad_mask_token,
    )


def solution(mesh):
    in_specs = (
        P("dp", "mp"),
        P("dp"),
        P("dp", None),
        P("dp"),
        P("dp"),
        P("mp", None),
        P("mp"),
        P(),
        P(),
        P(None, "mp"),
        P("mp"),
        P(None, "mp"),
        P(None, "mp"),
        P("mp"),
        P("mp", None),
        P("mp"),
        P(),
        P(),
        P(None, "mp"),
        P("mp"),
        P("mp", None),
        P("mp"),
        P(None, "mp"),
        P("mp"),
        P("mp"),
        P("dp", "mp"),
    )
    out_specs = (
        P("dp", "mp"),
        P("dp", "mp"),
        P("mp", None),
        P("mp"),
        P(),
        P(),
        P(None, "mp"),
        P("mp"),
        P(None, "mp"),
        P(None, "mp"),
        P("mp"),
        P("mp", None),
        P("mp"),
        P(),
        P(),
        P(None, "mp"),
        P("mp"),
        P("mp", None),
        P("mp"),
        P(None, "mp"),
        P("mp"),
        P("mp"),
    )
    return jax.shard_map(shards, mesh=mesh, in_specs=in_specs, out_specs=out_specs, check_vma=False)
```

```python
import functools

import jax
import jax.numpy as jnp
import numpy as np
from jax import lax
from jax.experimental import pallas as pl
from jax.experimental.pallas import tpu as pltpu
from jax.sharding import PartitionSpec as P

HEAD_DIM = 64
BANDS = 6
SIDE = 7
SAMP_OWN = 8
WINDOW = 176
VMEM_BYTES = 56 * 1024 * 1024

norm_eps = 1e-06
band_eps = 1e-06
big_negative = -1000000000.0
F32 = jnp.float32
BF16 = jnp.bfloat16


def params():
    return pltpu.CompilerParams(vmem_limit_bytes=VMEM_BYTES)


VM = pl.BlockSpec(memory_space=pltpu.VMEM)
SM = pl.BlockSpec(memory_space=pltpu.SMEM)


def swap(values, axis, bit):
    size = lax.axis_size(axis)
    return lax.ppermute(values, axis, [(i, i ^ bit) for i in range(size)])


def bits_of(axis):
    size = lax.axis_size(axis)
    return [1 << k for k in range(size.bit_length() - 1)]


def after(value, *before):
    return lax.optimization_barrier((value,) + before)[0]


def dot(left, right):
    return jnp.dot(left, right, preferred_element_type=F32)


def dot_t(left, right):
    return lax.dot_general(left, right, (((1,), (1,)), ((), ())), preferred_element_type=F32)


def dot_tl(left, right):
    return lax.dot_general(left, right, (((0,), (0,)), ((), ())), preferred_element_type=F32)


def window_of(tile, tile_tokens, total):
    base = tile * tile_tokens
    start = jnp.minimum((base // 16) * 16, total - WINDOW)
    return pl.multiple_of(start, 16), base - start


def hot_rows(pos_ref, count, tile, rem):
    lane = lax.broadcasted_iota(jnp.int32, (1, 128), 1)
    target = jnp.where(lane < count, pos_ref[pl.ds(tile, 1), :] + rem, -1)
    row = lax.broadcasted_iota(jnp.int32, (WINDOW, 128), 0)
    return row == target


def stats_kernel(patches, stats):
    def sum_step(i, carry):
        first, second = carry
        at = pl.multiple_of(i * 336, 16)
        x = patches[pl.ds(at, 336), :].astype(F32).reshape(42, 8, patches.shape[1])
        return first + jnp.sum(x, axis=0), second + jnp.sum(x * x, axis=0)

    blank = jnp.zeros((8, patches.shape[1]), F32)
    first, second = lax.fori_loop(0, patches.shape[0] // 336, sum_step, (blank, blank))
    stats[...] = band_sums(
        jnp.sum(first, axis=0, keepdims=True), jnp.sum(second, axis=0, keepdims=True)
    )


def pick_kernel(tile_tokens, order, count, pos, patches, cot, picked, cot_picked, mask_sum):
    total = patches.shape[0]
    slots = order.shape[0]
    visible = picked.shape[0] // slots
    mask_total = jnp.zeros((8, cot.shape[1]), F32)
    row = lax.broadcasted_iota(jnp.int32, (WINDOW, 128), 0)
    lane = lax.broadcasted_iota(jnp.int32, (WINDOW, 128), 1)
    for slot in range(slots):
        tile = order[slot]
        start, rem = window_of(tile, tile_tokens, total)
        hot = hot_rows(pos, count[tile], tile, rem).astype(F32)
        shown = jnp.sum(hot, axis=1, keepdims=True)
        inside = jnp.logical_and(row >= rem, row < rem + tile_tokens)
        hidden = jnp.where(inside, 1.0 - shown, 0.0)
        chooser = jnp.where(lane == visible, hidden, hot).astype(BF16)
        got = dot_tl(chooser, patches[pl.ds(start, WINDOW), :])
        got_cot = dot_tl(chooser, cot[pl.ds(start, WINDOW), :])
        here = slice(slot * visible, (slot + 1) * visible)
        picked[here, :] = got[:visible].astype(BF16)
        cot_picked[here, :] = got_cot[:visible].astype(BF16)
        mask_total = mask_total + got_cot[visible : visible + 8]
    mask_sum[...] = mask_total


def place_in(codes, tiles, visible, blocks):
    rows, cols = tiles.shape
    each = rows // blocks

    def kernel(code_ref, tile_ref, *refs):
        outs, held = refs[:-1], refs[-1]
        for k in range(rows // visible):
            at = pl.multiple_of(code_ref[k] * visible, 16)
            held[pl.ds(at, visible), :] = tile_ref[k * visible : (k + 1) * visible, :]
        at = 0
        for out in outs:
            out[...] = held[at : at + out.shape[0], :]
            at += out.shape[0]

    return call(
        kernel,
        [((each, cols), tiles.dtype)] * 2 + [((2 * each, cols), tiles.dtype)],
        [codes, tiles],
        "place_tiles",
        [pltpu.VMEM((rows, cols), tiles.dtype)],
        scalars=1,
    )


def place_out(codes, parts, visible):
    rows, cols = parts[0].shape
    total = 4 * rows

    def kernel(code_ref, own, near, far, out, held):
        for b, ref in enumerate(blocks_of((own, near, far))):
            held[b * rows : (b + 1) * rows, :] = ref[...]
        for k in range(total // visible):
            at = pl.multiple_of(code_ref[k] * visible, 16)
            out[k * visible : (k + 1) * visible, :] = held[pl.ds(at, visible), :]

    return call(
        kernel,
        [((total, cols), parts[0].dtype)],
        [codes] + parts,
        "return_tiles",
        [pltpu.VMEM((total, cols), parts[0].dtype)],
        scalars=1,
    )[0]


def blocks_of(crossed):
    own, near, far = crossed
    rows = own.shape[0]
    return [own, near.at[:rows], far.at[:rows], near.at[rows:]]


class Crossing:
    def __init__(self, own, near, far):
        self.own, self.near = own, near
        self.far = swap(far, "mp", 2)

    def relay(self, line):
        rows = self.own.shape[0]
        both = jnp.concatenate([self.near, line.wait(self.far)[rows:]], axis=0)
        line.mark(both)
        self.parts = [self.own, swap(both, "mp", 1), self.far]


def spread_kernel(tile_tokens, order, count, pos, mask_token, given, out):
    total = out.shape[0]
    slots = order.shape[0]
    visible = given.shape[0] // slots
    out[...] = jnp.broadcast_to(mask_token[...], out.shape)
    for slot in range(slots):
        tile = order[slot]
        start, rem = window_of(tile, tile_tokens, total)
        hot = hot_rows(pos, count[tile], tile, rem).astype(F32)
        shown = jnp.sum(hot, axis=1, keepdims=True) > 0.5
        rows = given[slot * visible : (slot + 1) * visible, :]
        new = dot(hot[:, :visible].astype(BF16), rows).astype(BF16)
        here = pl.ds(start, WINDOW)
        out[here, :] = jnp.where(shown, new, out[here, :])


def patch_kernel(tile_tokens, order, count, pos, cols, patches, given, out):
    total = out.shape[0]
    slots = order.shape[0]
    visible = given.shape[0] // slots

    def base_step(i, carry):
        at = pl.multiple_of(i * 336, 16)
        here = pl.ds(at, 336)
        out[here, :] = cols[0:1, :] + patches[here, :].astype(F32) * cols[1:2, :]
        return carry

    lax.fori_loop(0, total // 336, base_step, 0)
    for slot in range(slots):
        tile = order[slot]
        start, rem = window_of(tile, tile_tokens, total)
        hot = hot_rows(pos, count[tile], tile, rem).astype(F32)
        rows = given[slot * visible : (slot + 1) * visible, :]
        new = dot(hot[:, :visible].astype(BF16), rows)
        here = pl.ds(start, WINDOW)
        out[here, :] = out[here, :] + new * cols[2:3, :]


def sincos_table(limit, full_width):
    half_width = full_width // 2
    frequency = 1.0 / 10000.0 ** (np.arange(half_width, dtype=np.float32) / half_width)
    angles = np.arange(limit, dtype=np.float32)[:, None] * frequency.astype(np.float32)
    return np.concatenate([np.sin(angles), np.cos(angles)], axis=-1).astype(np.float32)


def place_table(full_width, frames):
    part = full_width // 16 * 6
    lines = 2 * SIDE
    table = np.zeros((2 * lines + frames, full_width), np.float32)
    table[:lines, :part] = sincos_table(lines, part)
    table[lines : 2 * lines, part : 2 * part] = sincos_table(lines, part)
    table[2 * lines :, 2 * part :] = sincos_table(frames, full_width - 2 * part)
    return table


def norm_forward(full_rows, gain_vec, bias_vec):
    values = full_rows.astype(F32)
    centred = values - jnp.mean(values, axis=-1, keepdims=True)
    inverse_std = lax.rsqrt(jnp.mean(centred * centred, axis=-1, keepdims=True) + norm_eps)
    unit_rows = centred * inverse_std
    normed_low = (unit_rows * gain_vec + bias_vec).astype(BF16)
    return (unit_rows, inverse_std, normed_low)


def row_sum(values):
    return jnp.sum(values.astype(F32), axis=0, keepdims=True)


def norm_backward(out_grad, unit_rows, inverse_std, gain_vec):
    scaled = out_grad * gain_vec
    first_mean = jnp.mean(scaled, axis=-1, keepdims=True)
    cross_mean = jnp.mean(scaled * unit_rows, axis=-1, keepdims=True)
    input_grad = inverse_std * (scaled - first_mean - unit_rows * cross_mean)
    return (input_grad, row_sum(out_grad * unit_rows), row_sum(out_grad))


def prep_kernel(odd, q, k, v, attn, hid, out, dec, embed, *refs):
    biases, (first, second, first_cut, second_cut) = refs[:-4], refs[-4:]
    e, w, h = embed.shape[0], q.shape[0], hid.shape[1]
    first[:e, :] = embed[...]
    for i, ref in enumerate((q, k, v)):
        first[e + i * w : e + (i + 1) * w, :] = ref[...]
    first[e + 3 * w : e + 4 * w, :] = attn[...]
    base = e + 4 * w
    first[base:, :] = jnp.zeros((first.shape[0] - base, first.shape[1]), BF16)
    for i, ref in enumerate(biases):
        first[base + i : base + i + 1, : ref.shape[1]] = ref[...]
    second[:h, :] = hid[...].T
    second[h : 2 * h, :] = out[...]
    second[2 * h :, :] = dec[...].T
    for whole, part in ((first, first_cut), (second, second_cut)):
        half = part.shape[0]
        part[...] = whole[pl.ds(pl.multiple_of(odd[0] * half, 16), half), :]


def copy_rows(target, refs, start, count):
    for e, ref in enumerate(refs):
        target[e * count : (e + 1) * count, :] = ref[start : start + count, :]


def normed_pixels(pix, cols):
    centred = pix[...].astype(F32) - cols[0:1, :]
    return centred, (centred * cols[1:2, :]).astype(BF16)


def embed_kernel(sizes, chosen, table, cols, vecs, mask, *refs):
    n, part, rows_s = sizes
    pix, weights = blocks_of(refs[:3]), refs[3 : 3 + n]
    start_ref, q_ref, k_ref, v_ref, probs, att_ref, middle, full = refs[3 + n :]
    e_rows = pix[0].shape[1]
    rows, width = start_ref.shape
    total = dot(chosen[...], table[...]) + vecs[0:1, :]
    for e in range(n):
        total = total + dot(normed_pixels(pix[e], cols)[1], weights[e][:e_rows, :])
    live = chosen[:, 127:128].astype(F32) > 0.5
    start = jnp.where(live, total, 0.0).astype(BF16)
    start_ref[...] = start
    normed = norm_forward(start, vecs[1:2, :], vecs[2:3, :])[2]
    copy_rows(full, weights, e_rows, part)
    q_ref[...] = (dot_t(normed, full[...]) + vecs[3:4, :]).astype(BF16)
    copy_rows(full, weights, e_rows + part, part)
    k_ref[...] = dot_t(normed, full[...]).astype(BF16)
    copy_rows(full, weights, e_rows + 2 * part, part)
    v_ref[...] = (dot_t(normed, full[...]) + vecs[4:5, :]).astype(BF16)
    scale = HEAD_DIM ** (-0.5)
    low = lax.broadcasted_iota(jnp.int32, (rows_s, 128), 1) < HEAD_DIM
    zero = jnp.zeros((rows_s, 128), BF16)

    def pair_step(i, carry):
        s, p = i // (width // 128), i % (width // 128)
        here = pl.ds(pl.multiple_of(s * rows_s, 16), rows_s)
        lanes = pl.ds(pl.multiple_of(p * 128, 128), 128)
        q2, k2, v2 = q_ref[here, lanes], k_ref[here, lanes], v_ref[here, lanes]
        extra = mask[pl.ds(s, 1), :]
        got = jnp.zeros((rows_s, 128), F32)
        for h in range(2):
            keep = low if h == 0 else jnp.logical_not(low)
            scores = dot_t(q2, jnp.where(keep, k2, zero)) * scale
            scores = jnp.where(extra > 0.5, scores, big_negative)
            shifted = jnp.exp(scores - jnp.max(scores, axis=-1, keepdims=True))
            share = (shifted / jnp.sum(shifted, axis=-1, keepdims=True)).astype(BF16)
            probs[i * 2 + h] = share
            got = got + dot(share, jnp.where(keep, v2, zero))
        att_ref[here, lanes] = got.astype(BF16)
        return carry

    lax.fori_loop(0, (rows // rows_s) * (width // 128), pair_step, 0)
    copy_rows(full, weights, e_rows + 3 * part, part)
    middle[...] = start_ref[...].astype(F32) + dot(att_ref[...], full[...]) + vecs[5:6, :]


def gelu_pair(x):
    cdf = 0.5 * (1.0 + lax.erf(x * (2.0**-0.5)))
    pdf = jnp.exp(-0.5 * x * x) * float(1.0 / np.sqrt(2.0 * np.pi))
    return x * cdf, cdf + x * pdf


def split_blocks(kept, sent, n):
    count = 2 * kept.shape[0] // n
    return [
        (kept if e % 2 == 0 else sent).at[e // 2 * count : (e // 2 + 1) * count] for e in range(n)
    ]


def mlp_kernel(n, middle, vecs, bias_hid, bias_dec, *refs):
    cot, weights, refs = blocks_of(refs[:3]), refs[3 : 3 + n], refs[3 + n :]
    rows = middle.shape[0]
    decoded = [refs[0], refs[1], refs[2].at[:rows], refs[2].at[rows:]]
    pre_refs = refs[3 : 3 + n]
    kept, sent, final_grad, sums, hidden, slope = refs[3 + n :]
    grads = split_blocks(kept, sent, n)
    h = pre_refs[0].shape[1]
    dec = decoded[0].shape[1]
    normed = norm_forward(middle[...].astype(BF16), vecs[6:7, :], vecs[7:8, :])[2]
    total = middle[...] + vecs[8:9, :]
    for e in range(n):
        pre = dot_t(normed, weights[e][:h, :]) + bias_hid[e : e + 1, :]
        value, grad = gelu_pair(pre)
        value = value.astype(BF16)
        hidden[e] = value
        slope[e] = grad.astype(BF16)
        total = total + dot(value, weights[e][h : 2 * h, :])
    final = total.astype(BF16)
    back = jnp.zeros(total.shape, F32)
    sums[...] = jnp.zeros(sums.shape, F32)
    for e in range(n):
        w_dec = weights[e][2 * h :, :]
        decoded[e][...] = (dot_t(final, w_dec) + bias_dec[e : e + 1, :]).astype(BF16)
        back = back + dot(cot[e][...], w_dec)
        grads[e][h:, :] = dot_tl(cot[e][...], final).astype(BF16)
        sums[n + 1 + e : n + 2 + e, :dec] = row_sum(cot[e][...])
    final_grad[...] = back
    low = back.astype(BF16)
    sums[n : n + 1, :] = row_sum(low)
    for e in range(n):
        grads[e][:h, :] = dot_tl(hidden[e], low).astype(BF16)
        pre_grad = (dot_t(low, weights[e][h : 2 * h, :]) * slope[e].astype(F32)).astype(BF16)
        pre_refs[e][...] = pre_grad
        sums[e : e + 1, :] = row_sum(pre_grad)


def hidden_kernel(n, middle, vecs, final_grad, att, *refs):
    pre, weights = refs[:n], refs[n : 2 * n]
    kept, sent, middle_grad, sums = refs[2 * n :]
    grads = split_blocks(kept, sent, n)
    h = pre[0].shape[1]
    unit, rstd, normed = norm_forward(middle[...].astype(BF16), vecs[6:7, :], vecs[7:8, :])
    total = jnp.zeros(unit.shape, F32)
    for e in range(n):
        total = total + dot(pre[e][...], weights[e][:h, :])
        grads[e][:h, :] = dot_tl(pre[e][...], normed).astype(BF16)
    term, gain, bias = norm_backward(total, unit, rstd, vecs[6:7, :])
    middle_grad[...] = final_grad[...] + term
    part = kept.shape[0] // 2 - h
    low_grad = middle_grad[...].astype(BF16)
    weight_grads(n, part, h, ((att, low_grad),), kept, sent)
    sums[0:1, :] = gain
    sums[1:2, :] = bias
    sums[2:8, :] = jnp.zeros((6, sums.shape[1]), F32)


def attn_back_kernel(sizes, middle_grad, start, q, k, v, probs, chosen, vecs, *refs):
    n, part, rows_s, e_rows = sizes
    weights = refs[:n]
    start_grad, dq, dk, dv, sums, full, ag = refs[n:]
    rows, width = start.shape
    copy_rows(full, weights, e_rows + 3 * part, part)
    low_grad = middle_grad[...].astype(BF16)
    ag[...] = dot_t(low_grad, full[...]).astype(BF16)
    scale = HEAD_DIM ** (-0.5)
    low = lax.broadcasted_iota(jnp.int32, (rows_s, 128), 1) < HEAD_DIM
    zero = jnp.zeros((rows_s, 128), BF16)

    def pair_step(i, carry):
        s, p = i // (width // 128), i % (width // 128)
        here = pl.ds(pl.multiple_of(s * rows_s, 16), rows_s)
        lanes = pl.ds(pl.multiple_of(p * 128, 128), 128)
        q2, k2, v2, g2 = q[here, lanes], k[here, lanes], v[here, lanes], ag[here, lanes]
        tq = jnp.zeros((rows_s, 128), F32)
        tk = jnp.zeros((rows_s, 128), F32)
        tv = jnp.zeros((rows_s, 128), F32)
        for h in range(2):
            keep = low if h == 0 else jnp.logical_not(low)
            share = probs[i * 2 + h]
            wide = share.astype(F32)
            prob_grad = dot_t(g2, jnp.where(keep, v2, zero))
            delta = jnp.sum(wide * prob_grad, axis=-1, keepdims=True)
            score_grad = (wide * (prob_grad - delta)).astype(BF16)
            tv = tv + dot_tl(share, jnp.where(keep, g2, zero))
            tq = tq + dot(score_grad, jnp.where(keep, k2, zero))
            tk = tk + dot_tl(score_grad, jnp.where(keep, q2, zero))
        dq[here, lanes] = (tq * scale).astype(BF16)
        dk[here, lanes] = (tk * scale).astype(BF16)
        dv[here, lanes] = tv.astype(BF16)
        return carry

    lax.fori_loop(0, (rows // rows_s) * (width // 128), pair_step, 0)
    copy_rows(full, weights, e_rows, part)
    total = dot(dq[...], full[...])
    copy_rows(full, weights, e_rows + part, part)
    total = total + dot(dk[...], full[...])
    copy_rows(full, weights, e_rows + 2 * part, part)
    total = total + dot(dv[...], full[...])
    unit, rstd, _ = norm_forward(start[...], vecs[1:2, :], vecs[2:3, :])
    term, gain, bias = norm_backward(total, unit, rstd, vecs[1:2, :])
    live = chosen[:, 127:128].astype(F32) > 0.5
    grad = jnp.where(live, middle_grad[...] + term, 0.0).astype(BF16)
    start_grad[...] = grad
    sums[0:1, :] = gain
    sums[1:2, :] = bias
    sums[2:3, :] = row_sum(grad)
    sums[3:4, :] = row_sum(low_grad)
    sums[4:5, :] = row_sum(dq[...])
    sums[5:6, :] = row_sum(dv[...])
    sums[6:8, :] = jnp.zeros((2, width), F32)


def pixel_grad_kernel(n, start_grad, cols, *refs):
    pix, weights, refs = blocks_of(refs[:3]), refs[3 : 3 + n], refs[3 + n :]
    rows = start_grad.shape[0]
    grads, bands = [refs[0], refs[1], refs[2].at[:rows], refs[2].at[rows:]], refs[3]
    e_rows = pix[0].shape[1]
    first = jnp.zeros((1, e_rows), F32)
    second = jnp.zeros((1, e_rows), F32)
    for e in range(n):
        got = dot_t(start_grad[...], weights[e][:e_rows, :])
        grads[e][...] = got.astype(BF16)
        first = first + row_sum(got)
        second = second + row_sum(got * (pix[e][...].astype(F32) - cols[0:1, :]))
    bands[...] = band_sums(first, second)


def weight_grads(n, part, base, pairs, kept, sent):
    grads = split_blocks(kept, sent, n)
    for i, (left, right) in enumerate(pairs):
        whole = dot_tl(left[...], right).astype(BF16)
        for e in range(n):
            at = base + i * part
            grads[e][at : at + part, :] = whole[e * part : (e + 1) * part, :]


def weight_kernel(sizes, start_grad, start, dq, dk, dv, cols, vecs, *refs):
    n, part = sizes
    pix, (kept, sent) = blocks_of(refs[:3]), refs[3:]
    e_rows = pix[0].shape[1]
    normed = norm_forward(start[...], vecs[1:2, :], vecs[2:3, :])[2]
    pairs = ((dq, normed), (dk, normed), (dv, normed))
    weight_grads(n, part, e_rows, pairs, kept, sent)
    grads = split_blocks(kept, sent, n)
    for e in range(n):
        got = dot_tl(normed_pixels(pix[e], cols)[1], start_grad[...])
        grads[e][:e_rows, :] = got.astype(BF16)


def join_kernel(half, flag, direct, handed, out):
    at = pl.multiple_of(flag[0] * half, 16)
    out[pl.ds(at, half), :] = direct[...]
    at = pl.multiple_of((1 - flag[0]) * half, 16)
    out[pl.ds(at, half), :] = handed[...]


def pack_kernel(sizes, place, mlp_sums, hid_sums, attn_sums, bands, mask_rows, out):
    n, part = sizes
    me = place[0]
    dec, width = mask_rows.shape[1], out.shape[1]
    base = 5 * n
    row = lax.broadcasted_iota(jnp.int32, (base, width), 0)
    total = jnp.zeros((base, width), F32)

    def widened(values):
        return jnp.concatenate([values, jnp.zeros((1, width - values.shape[1]), F32)], axis=1)

    for e in range(n):
        at = e ^ me
        lanes = slice(e * part, (e + 1) * part)
        total = jnp.where(row == at, mlp_sums[e : e + 1, :], total)
        total = jnp.where(row == n + at, widened(attn_sums[4:5, lanes]), total)
        total = jnp.where(row == 2 * n + at, widened(attn_sums[5:6, lanes]), total)
        total = jnp.where(row == 3 * n + at, mlp_sums[n + 1 + e : n + 2 + e, :], total)
    total = jnp.where(row == 4 * n + me, widened(mask_rows[0:1, :]), total)
    out[:base, :] = total
    out[base : base + 4, :] = attn_sums[:4, :]
    out[base + 4 : base + 6, :] = hid_sums[:2, :]
    out[base + 6 : base + 7, :] = mlp_sums[n : n + 1, :]
    out[base + 7 :, :] = jnp.zeros((out.shape[0] - base - 7, width), F32)
    out[base + 7 : base + 9, :128] = bands[:2, :]


def write_out(plan, values, outs):
    at = 0
    for out, turned in zip(outs, plan):
        if turned:
            count = out.shape[1]
            out[...] = values[at : at + count, :].T.astype(F32)
        else:
            count = out.shape[0]
            out[...] = values[at : at + count, :].astype(F32)
        at += count


def finish_kernel(half, plan, flag, own, came, *refs):
    outs, held = refs[:-1], refs[-1]
    first = flag[0] == 0

    @pl.when(first)
    def _():
        held[:half, :] = own[...]
        held[half:, :] = came[...]

    @pl.when(jnp.logical_not(first))
    def _():
        held[:half, :] = came[...]
        held[half:, :] = own[...]

    write_out(plan, held, outs)


def band_sums(first, second):
    columns = first.shape[1]
    band = lax.broadcasted_iota(jnp.int32, (columns, 128), 0) % BANDS
    pick_band = (band == lax.broadcasted_iota(jnp.int32, band.shape, 1)).astype(F32)
    rows = jnp.concatenate([first, second, jnp.zeros((6, columns), F32)], axis=0)
    return jnp.dot(rows, pick_band, precision=lax.Precision.HIGHEST, preferred_element_type=F32)


def call(kernel, outs, args, name, scratch=(), us=2.0, scalars=0):
    run = pl.pallas_call(
        kernel,
        out_shape=[jax.ShapeDtypeStruct(shape, kind) for shape, kind in outs],
        in_specs=[SM] * scalars + [VM] * (len(args) - scalars),
        out_specs=[VM] * len(outs),
        scratch_shapes=list(scratch),
        compiler_params=params(),
        cost_estimate=pl.CostEstimate(
            flops=0, bytes_accessed=int(us * 3.3e6), transcendentals=0
        ),
        name=name,
    )
    return list(run(*args))


class Weights:
    def __init__(self, own, part, data_index):
        self.own, self.half = own, part.shape[0]
        self.flag = (data_index & 1).astype(jnp.int32)[None]
        self.direct = swap(part, "mp", 2)
        self.near = swap(own, "mp", 1)

    def hand_on(self):
        self.handed = swap(self.direct, "dp", 1)

    def join(self, line):
        rows, width = self.own.shape
        [far] = call(
            functools.partial(join_kernel, self.half),
            [((rows, width), BF16)],
            [self.flag, self.direct, line.wait(self.handed)],
            "join_weights",
            us=2.0,
            scalars=1,
        )
        line.mark(far)
        self.blocks = [self.own, self.near, far, swap(far, "mp", 1)]


def to_absolute(blocks, model_index):
    size = blocks.shape[0]
    for bit in bits_of("mp"):
        turned = jnp.stack([blocks[i ^ bit] for i in range(size)])
        blocks = jnp.where((model_index & bit) != 0, turned, blocks)
    return blocks


class Line:
    def __init__(self):
        self.last = None

    def wait(self, value):
        return value if self.last is None else after(value, self.last)

    def mark(self, value):
        self.last = value


class Reduction:
    def __init__(self, kept, sent, order, data_index, line, plan, shapes, name):
        self.kept, self.came = kept, swap(sent, "mp", 1)
        self.quarters, self.line, self.name = 2, line, name
        self.plan, self.shapes = plan, shapes
        self.flags = [((data_index >> k) & 1).astype(jnp.int32)[None] for k in range(len(bits_of("dp")))]
        self.order = list(order) + [k for k in range(len(self.flags)) if k not in order]
        self.done, self.own, self.hold = [], None, False

    def step(self):
        if self.order or self.own is None:
            self.scatter()
        elif len(self.done) > 1:
            self.gather()
        else:
            self.finish()

    def scatter(self):
        came = self.line.wait(self.came)
        axis = self.order.pop(0) if self.order else None
        rows = self.kept.shape[0] // self.quarters
        if axis is None:
            [self.own] = self.stage(came, None, 0)
            self.line.mark(self.own)
            self.came = swap(self.own, "dp", 1 << self.done[-1][0])
        elif axis == "x":
            self.kept, sent = self.stage(came, None, rows)
            self.line.mark(self.kept)
            self.quarters = 1
            self.sent = sent
            if not self.hold:
                self.launch()
        else:
            self.kept, sent = self.stage(came, self.flags[axis], rows // 2)
            self.line.mark(self.kept)
            self.done.append((axis, int(self.kept.shape[1] < came.shape[1])))
            self.came = swap(sent, "dp", 1 << axis)

    def launch(self, *before):
        self.came = swap(after(self.sent, *before) if before else self.sent, "mp", 2)

    def stage(self, came, flag, half):
        total, width = self.kept.shape
        quarters, rows = self.quarters, total // self.quarters
        if flag is not None and half % 16 and width % 256 == 0:
            part = width // 2

            def kernel(mine, a, b, own, other):
                for out, which in ((own, mine[0]), (other, 1 - mine[0])):
                    here = pl.ds(pl.multiple_of(which * part, 128), part)
                    out[...] = (a[:, here].astype(F32) + b[:, here].astype(F32)).astype(BF16)

            return call(
                kernel,
                [((total, part), BF16)] * 2,
                [flag, self.kept, came],
                "reduce_" + self.name,
                scalars=1,
            )
        if flag is not None and half % 16:
            summed = (self.kept.astype(F32) + came.astype(F32)).astype(BF16)
            summed = summed.reshape(quarters, rows, width)
            own = lax.dynamic_slice_in_dim(summed, flag[0] * half, half, 1)
            other = lax.dynamic_slice_in_dim(summed, (1 - flag[0]) * half, half, 1)
            return own.reshape(-1, width), other.reshape(-1, width)

        def total_of(a, b, at, count):
            here = pl.ds(at, count)
            return (a[here, :].astype(F32) + b[here, :].astype(F32)).astype(BF16)

        if flag is None:

            def kernel(a, b, *outs):
                for k, out in enumerate(outs):
                    out[...] = total_of(a, b, k * out.shape[0], out.shape[0])

            count = 1 if half == 0 else 2
            return call(
                kernel, [((total // count, width), BF16)] * count, [self.kept, came], "reduce_" + self.name
            )

        def kernel(mine, a, b, own, other):
            for q in range(quarters):
                here = slice(q * half, (q + 1) * half)
                at = pl.multiple_of(q * rows + mine[0] * half, 16)
                own[here, :] = total_of(a, b, at, half)
                at = pl.multiple_of(q * rows + (1 - mine[0]) * half, 16)
                other[here, :] = total_of(a, b, at, half)

        return call(
            kernel,
            [((total // 2, width), BF16)] * 2,
            [flag, self.kept, came],
            "reduce_" + self.name,
            scalars=1,
        )

    def gather(self):
        axis, dim = self.done.pop()
        came = self.line.wait(self.came)
        self.own = jnp.where(
            self.flags[axis][0] == 0,
            jnp.concatenate([self.own, came], axis=dim),
            jnp.concatenate([came, self.own], axis=dim),
        )
        self.line.mark(self.own)
        self.came = swap(self.own, "dp", 1 << self.done[-1][0])

    def finish(self):
        half, width = self.own.shape
        self.result = call(
            functools.partial(finish_kernel, half, self.plan),
            [(shape, F32) for shape in self.shapes],
            [self.flags[self.done[0][0]], self.own, self.line.wait(self.came)],
            "finish_" + self.name,
            [pltpu.VMEM((2 * half, width), BF16)],
            us=3.0,
            scalars=1,
        )
        self.line.mark(self.result[0])


class Sums:
    def __init__(self, values, line):
        self.values, self.line = values, line
        self.left = [(axis, bit) for axis in ("mp", "dp") for bit in bits_of(axis)]
        self.came = swap(values, *self.left[0])

    def step(self):
        self.values = self.values + self.line.wait(self.came)
        self.line.mark(self.values)
        self.left.pop(0)
        if self.left:
            self.came = swap(self.values, *self.left[0])


def exchange(tiles):
    size = lax.axis_size("dp")
    blocks = tiles.reshape(size, tiles.shape[0] // size, tiles.shape[1])
    return lax.all_to_all(blocks, "dp", split_axis=0, concat_axis=0, tiled=True).reshape(tiles.shape)


def shards(
    patches,
    vis_count,
    vis_pos,
    tile_sample,
    tile_quad,
    w_embed,
    b_embed,
    norm1_gain,
    norm1_bias,
    w_query,
    b_query,
    w_key,
    w_value,
    b_value,
    w_attn_out,
    b_attn_out,
    norm2_gain,
    norm2_bias,
    w_hidden,
    b_hidden,
    w_mlp_out,
    b_mlp_out,
    w_decoder,
    b_decoder,
    mask_token,
    cotangent,
):
    data_size = lax.axis_size("dp")
    model_size = lax.axis_size("mp")
    data_index = lax.axis_index("dp")
    model_index = lax.axis_index("mp")
    tile_count = vis_count.shape[0]
    visible = vis_pos.shape[1]
    grid_count, pixel_cols = patches.shape
    tile_tokens = grid_count // tile_count
    full_width = w_embed.shape[1]
    part_width = b_embed.shape[0]
    dec_part = b_decoder.shape[0]
    hid_part = b_hidden.shape[0]
    pair_tiles = tile_count // data_size
    own_samples = SAMP_OWN // model_size
    sample_rows = 4 * visible
    rows = own_samples * sample_rows
    my_tiles = own_samples * 4
    score_scale = HEAD_DIM ** (-0.5)

    tile_ids = jnp.arange(tile_count, dtype=jnp.int32)
    owners = tile_sample // SAMP_OWN
    earlier = (owners[:, None] == owners[None, :]) & (tile_ids[None, :] < tile_ids[:, None])
    tile_ranks = jnp.sum(earlier.astype(jnp.int32), axis=1)
    slot_of = owners * pair_tiles + tile_ranks
    at_slot = slot_of[None, :] == tile_ids[:, None]
    order = jnp.sum(jnp.where(at_slot, tile_ids[None, :], 0), axis=1)
    tile_code = (tile_sample % SAMP_OWN) * 4 + tile_quad
    pos_wide = jnp.pad(vis_pos, ((0, 0), (0, 128 - visible)), constant_values=-1000)

    line = Line()
    [stats] = call(stats_kernel, [((8, 128), F32)], [patches], "band_sums", us=4.0)
    stats = stats + swap(stats, "mp", 1)
    stats = stats + swap(stats, "mp", 2)

    small = [b_embed, b_query, b_value, b_attn_out, b_mlp_out, b_decoder, b_hidden]
    base = pixel_cols + 4 * part_width
    own_first, own_second, cut_first, cut_second = call(
        prep_kernel,
        [((base + 32, full_width), BF16), ((2 * hid_part + dec_part, full_width), BF16)]
        + [(((base + 32) // 2, full_width), BF16), (((2 * hid_part + dec_part) // 2, full_width), BF16)],
        [(data_index & 1).astype(jnp.int32)[None]]
        + [w_query.T, w_key.T, w_value.T, w_attn_out, w_hidden, w_mlp_out, w_decoder]
        + [after(w_embed, stats)]
        + [v[None, :] for v in small],
        "prep_weights",
        us=5.0,
        scalars=1,
    )
    line.mark(own_first)
    first_w = Weights(own_first, cut_first, data_index)
    by_slot = jnp.where(at_slot, 1.0, 0.0)
    codes_slot = jnp.sum(by_slot * tile_code.astype(F32)[None, :], axis=1)
    counts_slot = jnp.sum(by_slot * vis_count.astype(F32)[None, :], axis=1)
    pos_slot = jnp.sum(by_slot[:, :, None] * vis_pos.astype(F32)[None, :, :], axis=1)
    info = jnp.concatenate([codes_slot[None], counts_slot[None]], axis=0)
    info = jnp.pad(info, ((0, 6), (0, 128 - tile_count)))
    packet = jnp.concatenate([stats, info, pos_slot.reshape(-1, 128)], axis=0)[None]
    for k, bit in enumerate(bits_of("dp")):
        came = swap(packet, "dp", bit)
        if k == 0:
            picked, cot_picked, mask_rows = call(
                functools.partial(pick_kernel, tile_tokens),
                [
                    ((tile_count * visible, pixel_cols), BF16),
                    ((tile_count * visible, dec_part), BF16),
                    ((8, dec_part), F32),
                ],
                [line.wait(order), vis_count, pos_wide, patches, cotangent],
                "pick_rows",
                us=7.5,
                scalars=2,
            )
            came = after(came, picked)
        packet = jnp.where(
            (data_index >> k) & 1 == 0,
            jnp.concatenate([packet, came], axis=0),
            jnp.concatenate([came, packet], axis=0),
        )

    arrived = exchange(after(picked, packet, first_w.direct))

    second_w = Weights(own_second, after(cut_second, first_w.direct), data_index)
    first_w.hand_on()
    second_w.hand_on()

    own_info = lax.dynamic_slice_in_dim(packet[:, 8:10], data_index * pair_tiles, pair_tiles, 2)
    own_info = own_info.transpose(1, 0, 2).reshape(2, tile_count).astype(jnp.int32)
    my_tiles_bit = model_index * my_tiles
    codes = own_info[0] ^ my_tiles_bit
    total = jnp.sum(packet[:, :2, :BANDS], axis=0)
    per_band = float(grid_count * data_size * (pixel_cols // BANDS) * model_size)
    band_mean = total[0] / per_band
    band_var = total[1] / per_band - band_mean * band_mean
    band_rstd = lax.rsqrt(band_var + band_eps)
    mean_cols = jnp.tile(band_mean, pixel_cols // BANDS)
    rstd_cols = jnp.tile(band_rstd, pixel_cols // BANDS)

    own_pos = packet[:, 16:].reshape(data_size, tile_count, visible)
    own_pos = lax.dynamic_slice_in_dim(own_pos, data_index * pair_tiles, pair_tiles, 1)
    own_pos = own_pos.reshape(tile_count, visible)
    mine = (codes[None, :] == jnp.arange(my_tiles)[:, None]).astype(F32)
    my_counts = jnp.sum(mine * own_info[1].astype(F32)[None, :], axis=1)
    my_pos = jnp.sum(mine[:, :, None] * own_pos[None], axis=1)
    my_pos = my_pos.astype(jnp.int32)
    live = jnp.arange(visible)[None, :] < my_counts.astype(jnp.int32)[:, None]
    live_col = live.reshape(rows, 1)
    usable = live.reshape(own_samples, sample_rows)
    quadrant = (jnp.arange(my_tiles) % 4)[:, None]
    inner = my_pos % (SIDE * SIDE)
    frames = tile_tokens // (SIDE * SIDE)
    col_at = quadrant % 2 * SIDE + inner % SIDE
    row_at = quadrant // 2 * SIDE + inner // SIDE + 2 * SIDE
    frame_at = my_pos // (SIDE * SIDE) + 4 * SIDE
    table = place_table(full_width, frames)
    high = table.astype(jnp.bfloat16)
    low = (table - high.astype(np.float32)).astype(jnp.bfloat16)
    wide = np.zeros((128, full_width), jnp.bfloat16)
    wide[: table.shape[0]], wide[64 : 64 + table.shape[0]] = high, low
    lane = jnp.arange(128)[None, :]
    spots = jnp.where(lane < 127, lane % 64, -1)
    chosen = (
        (col_at.reshape(rows, 1) == spots)
        | (row_at.reshape(rows, 1) == spots)
        | (frame_at.reshape(rows, 1) == spots)
        | ((lane == 127) & live_col)
    ).astype(BF16)
    key_mask = jnp.pad(usable.astype(F32), ((0, 8 - own_samples), (0, 0)))
    cols = jnp.pad(jnp.stack([mean_cols, rstd_cols]), ((0, 6), (0, 0)))

    line = Line()
    held = after(arrived, second_w.direct, chosen, key_mask, cols)
    own, near, far = place_in(codes, held, visible, model_size)
    line.mark(far)
    pix = Crossing(own, near, far)
    arrived_cot = exchange(after(cot_picked, far))
    first_w.join(line)
    pix.relay(line)
    line.mark(pix.parts[1])
    own, near, far = place_in(codes, line.wait(arrived_cot), visible, model_size)
    line.mark(far)
    cot = Crossing(own, near, far)
    bias_rel = [first_w.blocks[e][base : base + 16] for e in range(4)]
    bias_rel = jnp.stack(bias_rel).astype(F32)
    bias_abs = to_absolute(bias_rel, model_index)

    def rel_vec(k):
        return bias_rel[:, k, : small[k].shape[0]].reshape(1, -1)

    def abs_vec(k):
        return bias_abs[:, k, : small[k].shape[0]].reshape(1, -1)

    gains = [norm1_gain, norm1_bias, norm2_gain, norm2_bias]
    gains = [v[None].astype(F32) for v in gains]
    vecs = jnp.concatenate(
        [abs_vec(0), gains[0], gains[1], rel_vec(1), rel_vec(2), abs_vec(3)]
        + [gains[2], gains[3], abs_vec(4), jnp.zeros((7, full_width), F32)]
    )
    bias_hid, bias_dec = bias_rel[:, 6, :hid_part], bias_rel[:, 5, :dec_part]

    square = ((rows, full_width), BF16)
    wide_rows = ((rows, full_width), F32)
    heads = own_samples * full_width // HEAD_DIM
    weight_scratch = pltpu.VMEM((full_width, full_width), BF16)
    start, queries, key_rows, value_rows, probs, attended, middle = call(
        functools.partial(embed_kernel, (model_size, part_width, sample_rows)),
        [square] * 4 + [((heads, sample_rows, sample_rows), BF16), square, wide_rows],
        [chosen, jnp.asarray(wide), cols, vecs, line.wait(key_mask)] + pix.parts + first_w.blocks,
        "embed_attend",
        [weight_scratch],
        us=19.0,
    )
    line.mark(middle)
    cot.relay(line)
    second_w.join(line)
    decoded_shape = ((rows, dec_part), BF16)
    hidden_shape = ((rows, hid_part), BF16)
    out = call(
        functools.partial(mlp_kernel, model_size),
        [decoded_shape] * 2
        + [((2 * rows, dec_part), BF16)]
        + [hidden_shape] * model_size
        + [((2 * (hid_part + dec_part), full_width), BF16)] * 2
        + [wide_rows, ((16, full_width), F32)],
        [middle, vecs, bias_hid, bias_dec] + cot.parts + second_w.blocks,
        "mlp_decode",
        [pltpu.VMEM((model_size, rows, hid_part), BF16)] * 2,
        us=20.0,
    )
    decoded_rows, pre_grads = out[:3], out[3 : 3 + model_size]
    out_kept, out_sent, final_grad, mlp_sums = out[3 + model_size :]
    decoded_mp = Crossing(*decoded_rows)
    red_a = Reduction(
        out_kept,
        out_sent,
        ["x", 0, 1, 2],
        data_index,
        line,
        (False, True),
        [w_mlp_out.shape, w_decoder.shape],
        "out",
    )
    def decoded_step(decoded_dp):
        out = call(
            functools.partial(spread_kernel, tile_tokens),
            [((grid_count, dec_part), BF16)],
            [order, vis_count, pos_wide, mask_token[None, :], line.wait(decoded_dp)],
            "spread_decoded",
            us=3.5,
            scalars=2,
        )
        line.mark(out[0])
        return out

    def go_home(crossing):
        parts = crossing.parts
        tiles = place_out(codes, [parts[0], line.wait(parts[1]), parts[2]], visible)
        line.mark(tiles)
        return exchange(tiles)

    out = call(
        functools.partial(hidden_kernel, model_size),
        [((2 * (hid_part + part_width), full_width), BF16)] * 2 + [wide_rows, ((8, full_width), F32)],
        [middle, vecs, final_grad, attended] + pre_grads + second_w.blocks,
        "hidden_back",
        us=13.0,
    )
    hid_kept, hid_sent, middle_grad, hid_sums = out
    line.mark(middle_grad)
    decoded_mp.relay(line)
    red_a.step()
    red_b = Reduction(
        hid_kept, line.wait(hid_sent), ["x", 0, 1, 2], data_index, line, (True, False), [w_hidden.shape, w_attn_out.shape], "hidden"
    )
    start_grad, dq, dk, dv, attn_sums = call(
        functools.partial(attn_back_kernel, (model_size, part_width, sample_rows, pixel_cols)),
        [square] * 4 + [((8, full_width), F32)],
        [line.wait(middle_grad), start, queries, key_rows, value_rows]
        + [probs, chosen, vecs]
        + first_w.blocks,
        "attend_back",
        [weight_scratch, pltpu.VMEM((rows, full_width), BF16)],
        us=18.0,
    )
    line.mark(start_grad)
    decoded_dp = go_home(decoded_mp)
    out = call(
        functools.partial(pixel_grad_kernel, model_size),
        [((rows, pixel_cols), BF16)] * 2 + [((2 * rows, pixel_cols), BF16), ((8, 128), F32)],
        [line.wait(start_grad), cols] + pix.parts + first_w.blocks,
        "pixel_grad",
        us=6.7,
    )
    normed_grad, bands = out[:3], out[3]
    line.mark(bands)
    grad_mp = Crossing(*normed_grad)
    [sums] = call(
        functools.partial(pack_kernel, (model_size, part_width)),
        [((32, full_width), F32)],
        [model_index.astype(jnp.int32)[None], mlp_sums, hid_sums, attn_sums, line.wait(bands)]
        + [mask_rows],
        "pack_sums",
        us=1.5,
        scalars=1,
    )
    line.mark(sums)
    sums = Sums(sums, line)
    sums.step()
    red_b.hold = True
    red_b.step()
    red_a.step()
    spread = decoded_step(decoded_dp)
    first_kept, first_sent = call(
        functools.partial(weight_kernel, (model_size, part_width)),
        [((2 * (base - part_width), full_width), BF16)] * 2,
        [line.wait(start_grad), start, dq, dk, dv, cols, vecs] + pix.parts,
        "weight_grad",
        us=10.0,
    )
    line.mark(first_kept)
    red_a.step()
    grad_mp.relay(line)
    sums.step()
    red_b.launch(sums.values)
    red_c = Reduction(
        first_kept,
        line.wait(first_sent),
        ["x", 0, 1, 2],
        data_index,
        line,
        (False,) * 4,
        [w_embed.shape] + [w_attn_out.shape] * 3,
        "first",
    )

    def patch_step(grad_dp):
        bands_all = sums.values[5 * model_size + 7 : 5 * model_size + 9, :BANDS]
        grad_all, cross_all = bands_all[0], bands_all[1]
        grad_var = -0.5 * cross_all * band_rstd * band_rstd * band_rstd
        grad_mean = -band_rstd * grad_all - 2.0 * band_mean * grad_var
        terms = jnp.stack([grad_mean / per_band, 2.0 * grad_var / per_band, band_rstd])
        terms = jnp.pad(jnp.tile(terms, (1, pixel_cols // BANDS)), ((0, 5), (0, 0)))
        out = call(
            functools.partial(patch_kernel, tile_tokens),
            [((grid_count, pixel_cols), F32)],
            [order, vis_count, pos_wide, terms, patches, line.wait(grad_dp)],
            "spread_patch_grad",
            us=8.0,
            scalars=2,
        )
        line.mark(out[0])
        return out

    def steps(*chains):
        for chain in chains:
            chain.step()

    kept = {}

    def go(name):
        if name in chains:
            chains[name].step()
        elif name == "H":
            kept["grad"] = go_home(grad_mp)
        elif name == "P":
            while sums.left:
                sums.step()
            kept["patch"] = patch_step(kept["grad"])
    chains = {"a": red_a, "b": red_b, "c": red_c, "s": sums}
    for name in "cssHasbabacPbacbbcbaccbcc":
        go(name)
    while sums.left:
        sums.step()
    while not all(hasattr(chain, "result") for chain in (red_a, red_b, red_c)):
        for chain in (red_a, red_b, red_c):
            if not hasattr(chain, "result"):
                chain.step()
    [patch_grad], [decoded] = kept["patch"], spread

    n = model_size
    sums = sums.values
    own_rows = [
        lax.dynamic_slice_in_dim(sums, model_index + k * n, 1, 0)[0] for k in range(5)
    ]
    sum_hidden = own_rows[0]
    sum_query, sum_value = own_rows[1][:part_width], own_rows[2][:part_width]
    sum_dec, grad_mask_token = own_rows[3][:dec_part], own_rows[4][:dec_part]
    gain_one, bias_one, embed_sum, attn_out_sum, gain_two, bias_two, mlp_out_sum = (
        sums[5 * n + k] for k in range(7)
    )

    def mine_of(vector):
        part = vector.shape[0] // model_size
        return lax.dynamic_slice_in_dim(vector, model_index * part, part, 0)

    (g_out, g_dec), (g_hid, g_attn) = red_a.result, red_b.result
    g_embed, g_query, g_key, g_value = red_c.result

    return (
        decoded,
        patch_grad,
        g_embed,
        mine_of(embed_sum),
        gain_one,
        bias_one,
        g_query.T,
        sum_query,
        g_key.T,
        g_value.T,
        sum_value,
        g_attn,
        mine_of(attn_out_sum),
        gain_two,
        bias_two,
        g_hid,
        sum_hidden,
        g_out,
        mine_of(mlp_out_sum),
        g_dec,
        sum_dec,
        grad_mask_token,
    )


def solution(mesh):
    in_specs = (
        P("dp", "mp"),
        P("dp"),
        P("dp", None),
        P("dp"),
        P("dp"),
        P("mp", None),
        P("mp"),
        P(),
        P(),
        P(None, "mp"),
        P("mp"),
        P(None, "mp"),
        P(None, "mp"),
        P("mp"),
        P("mp", None),
        P("mp"),
        P(),
        P(),
        P(None, "mp"),
        P("mp"),
        P("mp", None),
        P("mp"),
        P(None, "mp"),
        P("mp"),
        P("mp"),
        P("dp", "mp"),
    )
    out_specs = (
        P("dp", "mp"),
        P("dp", "mp"),
        P("mp", None),
        P("mp"),
        P(),
        P(),
        P(None, "mp"),
        P("mp"),
        P(None, "mp"),
        P(None, "mp"),
        P("mp"),
        P("mp", None),
        P("mp"),
        P(),
        P(),
        P(None, "mp"),
        P("mp"),
        P("mp", None),
        P("mp"),
        P(None, "mp"),
        P("mp"),
        P("mp"),
    )
    return jax.shard_map(shards, mesh=mesh, in_specs=in_specs, out_specs=out_specs, check_vma=False)
```

```python
import functools

import jax
import jax.numpy as jnp
import numpy as np
from jax import lax
from jax.experimental import pallas as pl
from jax.experimental.pallas import tpu as pltpu
from jax.sharding import PartitionSpec as P

HEAD_DIM = 64
BANDS = 6
SIDE = 7
SAMP_OWN = 8
WINDOW = 176
VMEM_BYTES = 56 * 1024 * 1024

norm_eps = 1e-06
band_eps = 1e-06
big_negative = -1000000000.0
F32 = jnp.float32
BF16 = jnp.bfloat16


def params():
    return pltpu.CompilerParams(vmem_limit_bytes=VMEM_BYTES)


VM = pl.BlockSpec(memory_space=pltpu.VMEM)
SM = pl.BlockSpec(memory_space=pltpu.SMEM)


def swap(values, axis, bit):
    size = lax.axis_size(axis)
    return lax.ppermute(values, axis, [(i, i ^ bit) for i in range(size)])


def bits_of(axis):
    size = lax.axis_size(axis)
    return [1 << k for k in range(size.bit_length() - 1)]


def after(value, *before):
    return lax.optimization_barrier((value,) + before)[0]


def dot(left, right):
    return jnp.dot(left, right, preferred_element_type=F32)


def dot_t(left, right):
    return lax.dot_general(left, right, (((1,), (1,)), ((), ())), preferred_element_type=F32)


def dot_tl(left, right):
    return lax.dot_general(left, right, (((0,), (0,)), ((), ())), preferred_element_type=F32)


def window_of(tile, tile_tokens, total):
    base = tile * tile_tokens
    start = jnp.minimum((base // 16) * 16, total - WINDOW)
    return pl.multiple_of(start, 16), base - start


def hot_rows(pos_ref, count, tile, rem):
    lane = lax.broadcasted_iota(jnp.int32, (1, 128), 1)
    target = jnp.where(lane < count, pos_ref[pl.ds(tile, 1), :] + rem, -1)
    row = lax.broadcasted_iota(jnp.int32, (WINDOW, 128), 0)
    return row == target


def stats_kernel(patches, stats):
    def sum_step(i, carry):
        first, second = carry
        at = pl.multiple_of(i * 336, 16)
        x = patches[pl.ds(at, 336), :].astype(F32).reshape(42, 8, patches.shape[1])
        return first + jnp.sum(x, axis=0), second + jnp.sum(x * x, axis=0)

    blank = jnp.zeros((8, patches.shape[1]), F32)
    first, second = lax.fori_loop(0, patches.shape[0] // 336, sum_step, (blank, blank))
    stats[...] = band_sums(
        jnp.sum(first, axis=0, keepdims=True), jnp.sum(second, axis=0, keepdims=True)
    )


def pick_kernel(tile_tokens, order, count, pos, patches, cot, picked, cot_picked, mask_sum):
    total = patches.shape[0]
    slots = order.shape[0]
    visible = picked.shape[0] // slots
    mask_total = jnp.zeros((8, cot.shape[1]), F32)
    row = lax.broadcasted_iota(jnp.int32, (WINDOW, 128), 0)
    lane = lax.broadcasted_iota(jnp.int32, (WINDOW, 128), 1)
    for slot in range(slots):
        tile = order[slot]
        start, rem = window_of(tile, tile_tokens, total)
        hot = hot_rows(pos, count[tile], tile, rem).astype(F32)
        shown = jnp.sum(hot, axis=1, keepdims=True)
        inside = jnp.logical_and(row >= rem, row < rem + tile_tokens)
        hidden = jnp.where(inside, 1.0 - shown, 0.0)
        chooser = jnp.where(lane == visible, hidden, hot).astype(BF16)
        got = dot_tl(chooser, patches[pl.ds(start, WINDOW), :])
        got_cot = dot_tl(chooser, cot[pl.ds(start, WINDOW), :])
        here = slice(slot * visible, (slot + 1) * visible)
        picked[here, :] = got[:visible].astype(BF16)
        cot_picked[here, :] = got_cot[:visible].astype(BF16)
        mask_total = mask_total + got_cot[visible : visible + 8]
    mask_sum[...] = mask_total


def place_in(codes, tiles, visible, blocks):
    rows, cols = tiles.shape
    each = rows // blocks

    def kernel(code_ref, tile_ref, *refs):
        outs, held = refs[:-1], refs[-1]
        for k in range(rows // visible):
            at = pl.multiple_of(code_ref[k] * visible, 16)
            held[pl.ds(at, visible), :] = tile_ref[k * visible : (k + 1) * visible, :]
        at = 0
        for out in outs:
            out[...] = held[at : at + out.shape[0], :]
            at += out.shape[0]

    return call(
        kernel,
        [((each, cols), tiles.dtype)] * 2 + [((2 * each, cols), tiles.dtype)],
        [codes, tiles],
        "place_tiles",
        [pltpu.VMEM((rows, cols), tiles.dtype)],
        scalars=1,
    )


def place_out(codes, parts, visible):
    rows, cols = parts[0].shape
    total = 4 * rows

    def kernel(code_ref, own, near, far, out, held):
        for b, ref in enumerate(blocks_of((own, near, far))):
            held[b * rows : (b + 1) * rows, :] = ref[...]
        for k in range(total // visible):
            at = pl.multiple_of(code_ref[k] * visible, 16)
            out[k * visible : (k + 1) * visible, :] = held[pl.ds(at, visible), :]

    return call(
        kernel,
        [((total, cols), parts[0].dtype)],
        [codes] + parts,
        "return_tiles",
        [pltpu.VMEM((total, cols), parts[0].dtype)],
        scalars=1,
    )[0]


def blocks_of(crossed):
    own, near, far = crossed
    rows = own.shape[0]
    return [own, near.at[:rows], far.at[:rows], near.at[rows:]]


class Crossing:
    def __init__(self, own, near, far):
        self.own, self.near = own, near
        self.far = swap(far, "mp", 2)

    def relay(self, line):
        rows = self.own.shape[0]
        both = jnp.concatenate([self.near, line.wait(self.far)[rows:]], axis=0)
        line.mark(both)
        self.parts = [self.own, swap(both, "mp", 1), self.far]


def spread_kernel(tile_tokens, order, count, pos, mask_token, given, out):
    total = out.shape[0]
    slots = order.shape[0]
    visible = given.shape[0] // slots
    out[...] = jnp.broadcast_to(mask_token[...], out.shape)
    for slot in range(slots):
        tile = order[slot]
        start, rem = window_of(tile, tile_tokens, total)
        hot = hot_rows(pos, count[tile], tile, rem).astype(F32)
        shown = jnp.sum(hot, axis=1, keepdims=True) > 0.5
        rows = given[slot * visible : (slot + 1) * visible, :]
        new = dot(hot[:, :visible].astype(BF16), rows).astype(BF16)
        here = pl.ds(start, WINDOW)
        out[here, :] = jnp.where(shown, new, out[here, :])


def patch_kernel(tile_tokens, order, count, pos, cols, patches, given, out):
    total = out.shape[0]
    slots = order.shape[0]
    visible = given.shape[0] // slots

    def base_step(i, carry):
        at = pl.multiple_of(i * 336, 16)
        here = pl.ds(at, 336)
        out[here, :] = cols[0:1, :] + patches[here, :].astype(F32) * cols[1:2, :]
        return carry

    lax.fori_loop(0, total // 336, base_step, 0)
    for slot in range(slots):
        tile = order[slot]
        start, rem = window_of(tile, tile_tokens, total)
        hot = hot_rows(pos, count[tile], tile, rem).astype(F32)
        rows = given[slot * visible : (slot + 1) * visible, :]
        new = dot(hot[:, :visible].astype(BF16), rows)
        here = pl.ds(start, WINDOW)
        out[here, :] = out[here, :] + new * cols[2:3, :]


def sincos_table(limit, full_width):
    half_width = full_width // 2
    frequency = 1.0 / 10000.0 ** (np.arange(half_width, dtype=np.float32) / half_width)
    angles = np.arange(limit, dtype=np.float32)[:, None] * frequency.astype(np.float32)
    return np.concatenate([np.sin(angles), np.cos(angles)], axis=-1).astype(np.float32)


def place_table(full_width, frames):
    part = full_width // 16 * 6
    lines = 2 * SIDE
    table = np.zeros((2 * lines + frames, full_width), np.float32)
    table[:lines, :part] = sincos_table(lines, part)
    table[lines : 2 * lines, part : 2 * part] = sincos_table(lines, part)
    table[2 * lines :, 2 * part :] = sincos_table(frames, full_width - 2 * part)
    return table


def norm_forward(full_rows, gain_vec, bias_vec):
    values = full_rows.astype(F32)
    centred = values - jnp.mean(values, axis=-1, keepdims=True)
    inverse_std = lax.rsqrt(jnp.mean(centred * centred, axis=-1, keepdims=True) + norm_eps)
    unit_rows = centred * inverse_std
    normed_low = (unit_rows * gain_vec + bias_vec).astype(BF16)
    return (unit_rows, inverse_std, normed_low)


def row_sum(values):
    return jnp.sum(values.astype(F32), axis=0, keepdims=True)


def norm_backward(out_grad, unit_rows, inverse_std, gain_vec):
    scaled = out_grad * gain_vec
    first_mean = jnp.mean(scaled, axis=-1, keepdims=True)
    cross_mean = jnp.mean(scaled * unit_rows, axis=-1, keepdims=True)
    input_grad = inverse_std * (scaled - first_mean - unit_rows * cross_mean)
    return (input_grad, row_sum(out_grad * unit_rows), row_sum(out_grad))


def prep_kernel(odd, q, k, v, attn, hid, out, dec, embed, *refs):
    biases, (first, second, first_cut, second_cut) = refs[:-4], refs[-4:]
    e, w, h = embed.shape[0], q.shape[0], hid.shape[1]
    first[:e, :] = embed[...]
    for i, ref in enumerate((q, k, v)):
        first[e + i * w : e + (i + 1) * w, :] = ref[...]
    first[e + 3 * w : e + 4 * w, :] = attn[...]
    base = e + 4 * w
    first[base:, :] = jnp.zeros((first.shape[0] - base, first.shape[1]), BF16)
    for i, ref in enumerate(biases):
        first[base + i : base + i + 1, : ref.shape[1]] = ref[...]
    second[:h, :] = hid[...].T
    second[h : 2 * h, :] = out[...]
    second[2 * h :, :] = dec[...].T
    for whole, part in ((first, first_cut), (second, second_cut)):
        half = part.shape[0]
        part[...] = whole[pl.ds(pl.multiple_of(odd[0] * half, 16), half), :]


def copy_rows(target, refs, start, count):
    for e, ref in enumerate(refs):
        target[e * count : (e + 1) * count, :] = ref[start : start + count, :]


def normed_pixels(pix, cols):
    centred = pix[...].astype(F32) - cols[0:1, :]
    return centred, (centred * cols[1:2, :]).astype(BF16)


def embed_kernel(sizes, chosen, table, cols, vecs, mask, *refs):
    n, part, rows_s = sizes
    pix, weights = blocks_of(refs[:3]), refs[3 : 3 + n]
    start_ref, q_ref, k_ref, v_ref, probs, att_ref, middle, full = refs[3 + n :]
    e_rows = pix[0].shape[1]
    rows, width = start_ref.shape
    total = dot(chosen[...], table[...]) + vecs[0:1, :]
    for e in range(n):
        total = total + dot(normed_pixels(pix[e], cols)[1], weights[e][:e_rows, :])
    live = chosen[:, 127:128].astype(F32) > 0.5
    start = jnp.where(live, total, 0.0).astype(BF16)
    start_ref[...] = start
    normed = norm_forward(start, vecs[1:2, :], vecs[2:3, :])[2]
    copy_rows(full, weights, e_rows, part)
    q_ref[...] = (dot_t(normed, full[...]) + vecs[3:4, :]).astype(BF16)
    copy_rows(full, weights, e_rows + part, part)
    k_ref[...] = dot_t(normed, full[...]).astype(BF16)
    copy_rows(full, weights, e_rows + 2 * part, part)
    v_ref[...] = (dot_t(normed, full[...]) + vecs[4:5, :]).astype(BF16)
    scale = HEAD_DIM ** (-0.5)
    low = lax.broadcasted_iota(jnp.int32, (rows_s, 128), 1) < HEAD_DIM
    zero = jnp.zeros((rows_s, 128), BF16)

    def pair_step(i, carry):
        s, p = i // (width // 128), i % (width // 128)
        here = pl.ds(pl.multiple_of(s * rows_s, 16), rows_s)
        lanes = pl.ds(pl.multiple_of(p * 128, 128), 128)
        q2, k2, v2 = q_ref[here, lanes], k_ref[here, lanes], v_ref[here, lanes]
        extra = mask[pl.ds(s, 1), :]
        got = jnp.zeros((rows_s, 128), F32)
        for h in range(2):
            keep = low if h == 0 else jnp.logical_not(low)
            scores = dot_t(q2, jnp.where(keep, k2, zero)) * scale
            scores = jnp.where(extra > 0.5, scores, big_negative)
            shifted = jnp.exp(scores - jnp.max(scores, axis=-1, keepdims=True))
            share = (shifted / jnp.sum(shifted, axis=-1, keepdims=True)).astype(BF16)
            probs[i * 2 + h] = share
            got = got + dot(share, jnp.where(keep, v2, zero))
        att_ref[here, lanes] = got.astype(BF16)
        return carry

    lax.fori_loop(0, (rows // rows_s) * (width // 128), pair_step, 0)
    copy_rows(full, weights, e_rows + 3 * part, part)
    middle[...] = start_ref[...].astype(F32) + dot(att_ref[...], full[...]) + vecs[5:6, :]


def gelu_pair(x):
    cdf = 0.5 * (1.0 + lax.erf(x * (2.0**-0.5)))
    pdf = jnp.exp(-0.5 * x * x) * float(1.0 / np.sqrt(2.0 * np.pi))
    return x * cdf, cdf + x * pdf


def split_blocks(kept, sent, n):
    count = 2 * kept.shape[0] // n
    return [
        (kept if e % 2 == 0 else sent).at[e // 2 * count : (e // 2 + 1) * count] for e in range(n)
    ]


def mlp_kernel(n, middle, vecs, bias_hid, bias_dec, *refs):
    cot, weights, refs = blocks_of(refs[:3]), refs[3 : 3 + n], refs[3 + n :]
    rows = middle.shape[0]
    decoded = [refs[0], refs[1], refs[2].at[:rows], refs[2].at[rows:]]
    pre_refs = refs[3 : 3 + n]
    kept, sent, final_grad, sums, hidden, slope = refs[3 + n :]
    grads = split_blocks(kept, sent, n)
    h = pre_refs[0].shape[1]
    dec = decoded[0].shape[1]
    normed = norm_forward(middle[...].astype(BF16), vecs[6:7, :], vecs[7:8, :])[2]
    total = middle[...] + vecs[8:9, :]
    for e in range(n):
        pre = dot_t(normed, weights[e][:h, :]) + bias_hid[e : e + 1, :]
        value, grad = gelu_pair(pre)
        value = value.astype(BF16)
        hidden[e] = value
        slope[e] = grad.astype(BF16)
        total = total + dot(value, weights[e][h : 2 * h, :])
    final = total.astype(BF16)
    back = jnp.zeros(total.shape, F32)
    sums[...] = jnp.zeros(sums.shape, F32)
    for e in range(n):
        w_dec = weights[e][2 * h :, :]
        decoded[e][...] = (dot_t(final, w_dec) + bias_dec[e : e + 1, :]).astype(BF16)
        back = back + dot(cot[e][...], w_dec)
        grads[e][h:, :] = dot_tl(cot[e][...], final).astype(BF16)
        sums[n + 1 + e : n + 2 + e, :dec] = row_sum(cot[e][...])
    final_grad[...] = back
    low = back.astype(BF16)
    sums[n : n + 1, :] = row_sum(low)
    for e in range(n):
        grads[e][:h, :] = dot_tl(hidden[e], low).astype(BF16)
        pre_grad = (dot_t(low, weights[e][h : 2 * h, :]) * slope[e].astype(F32)).astype(BF16)
        pre_refs[e][...] = pre_grad
        sums[e : e + 1, :] = row_sum(pre_grad)


def hidden_kernel(n, middle, vecs, final_grad, att, *refs):
    pre, weights = refs[:n], refs[n : 2 * n]
    kept, sent, middle_grad, sums = refs[2 * n :]
    grads = split_blocks(kept, sent, n)
    h = pre[0].shape[1]
    unit, rstd, normed = norm_forward(middle[...].astype(BF16), vecs[6:7, :], vecs[7:8, :])
    total = jnp.zeros(unit.shape, F32)
    for e in range(n):
        total = total + dot(pre[e][...], weights[e][:h, :])
        grads[e][:h, :] = dot_tl(pre[e][...], normed).astype(BF16)
    term, gain, bias = norm_backward(total, unit, rstd, vecs[6:7, :])
    middle_grad[...] = final_grad[...] + term
    part = kept.shape[0] // 2 - h
    low_grad = middle_grad[...].astype(BF16)
    weight_grads(n, part, h, ((att, low_grad),), kept, sent)
    sums[0:1, :] = gain
    sums[1:2, :] = bias
    sums[2:8, :] = jnp.zeros((6, sums.shape[1]), F32)


def attn_back_kernel(sizes, middle_grad, start, q, k, v, probs, chosen, vecs, *refs):
    n, part, rows_s, e_rows = sizes
    weights = refs[:n]
    start_grad, dq, dk, dv, sums, full, ag = refs[n:]
    rows, width = start.shape
    copy_rows(full, weights, e_rows + 3 * part, part)
    low_grad = middle_grad[...].astype(BF16)
    ag[...] = dot_t(low_grad, full[...]).astype(BF16)
    scale = HEAD_DIM ** (-0.5)
    low = lax.broadcasted_iota(jnp.int32, (rows_s, 128), 1) < HEAD_DIM
    zero = jnp.zeros((rows_s, 128), BF16)

    def pair_step(i, carry):
        s, p = i // (width // 128), i % (width // 128)
        here = pl.ds(pl.multiple_of(s * rows_s, 16), rows_s)
        lanes = pl.ds(pl.multiple_of(p * 128, 128), 128)
        q2, k2, v2, g2 = q[here, lanes], k[here, lanes], v[here, lanes], ag[here, lanes]
        tq = jnp.zeros((rows_s, 128), F32)
        tk = jnp.zeros((rows_s, 128), F32)
        tv = jnp.zeros((rows_s, 128), F32)
        for h in range(2):
            keep = low if h == 0 else jnp.logical_not(low)
            share = probs[i * 2 + h]
            wide = share.astype(F32)
            prob_grad = dot_t(g2, jnp.where(keep, v2, zero))
            delta = jnp.sum(wide * prob_grad, axis=-1, keepdims=True)
            score_grad = (wide * (prob_grad - delta)).astype(BF16)
            tv = tv + dot_tl(share, jnp.where(keep, g2, zero))
            tq = tq + dot(score_grad, jnp.where(keep, k2, zero))
            tk = tk + dot_tl(score_grad, jnp.where(keep, q2, zero))
        dq[here, lanes] = (tq * scale).astype(BF16)
        dk[here, lanes] = (tk * scale).astype(BF16)
        dv[here, lanes] = tv.astype(BF16)
        return carry

    lax.fori_loop(0, (rows // rows_s) * (width // 128), pair_step, 0)
    copy_rows(full, weights, e_rows, part)
    total = dot(dq[...], full[...])
    copy_rows(full, weights, e_rows + part, part)
    total = total + dot(dk[...], full[...])
    copy_rows(full, weights, e_rows + 2 * part, part)
    total = total + dot(dv[...], full[...])
    unit, rstd, _ = norm_forward(start[...], vecs[1:2, :], vecs[2:3, :])
    term, gain, bias = norm_backward(total, unit, rstd, vecs[1:2, :])
    live = chosen[:, 127:128].astype(F32) > 0.5
    grad = jnp.where(live, middle_grad[...] + term, 0.0).astype(BF16)
    start_grad[...] = grad
    sums[0:1, :] = gain
    sums[1:2, :] = bias
    sums[2:3, :] = row_sum(grad)
    sums[3:4, :] = row_sum(low_grad)
    sums[4:5, :] = row_sum(dq[...])
    sums[5:6, :] = row_sum(dv[...])
    sums[6:8, :] = jnp.zeros((2, width), F32)


def pixel_grad_kernel(n, start_grad, cols, *refs):
    pix, weights, refs = blocks_of(refs[:3]), refs[3 : 3 + n], refs[3 + n :]
    rows = start_grad.shape[0]
    grads, bands = [refs[0], refs[1], refs[2].at[:rows], refs[2].at[rows:]], refs[3]
    e_rows = pix[0].shape[1]
    first = jnp.zeros((1, e_rows), F32)
    second = jnp.zeros((1, e_rows), F32)
    for e in range(n):
        got = dot_t(start_grad[...], weights[e][:e_rows, :])
        grads[e][...] = got.astype(BF16)
        first = first + row_sum(got)
        second = second + row_sum(got * (pix[e][...].astype(F32) - cols[0:1, :]))
    bands[...] = band_sums(first, second)


def weight_grads(n, part, base, pairs, kept, sent):
    grads = split_blocks(kept, sent, n)
    for i, (left, right) in enumerate(pairs):
        whole = dot_tl(left[...], right).astype(BF16)
        for e in range(n):
            at = base + i * part
            grads[e][at : at + part, :] = whole[e * part : (e + 1) * part, :]


def weight_kernel(sizes, start_grad, start, dq, dk, dv, cols, vecs, *refs):
    n, part = sizes
    pix, (kept, sent) = blocks_of(refs[:3]), refs[3:]
    e_rows = pix[0].shape[1]
    normed = norm_forward(start[...], vecs[1:2, :], vecs[2:3, :])[2]
    pairs = ((dq, normed), (dk, normed), (dv, normed))
    weight_grads(n, part, e_rows, pairs, kept, sent)
    grads = split_blocks(kept, sent, n)
    for e in range(n):
        got = dot_tl(normed_pixels(pix[e], cols)[1], start_grad[...])
        grads[e][:e_rows, :] = got.astype(BF16)


def join_kernel(half, flag, direct, handed, out):
    at = pl.multiple_of(flag[0] * half, 16)
    out[pl.ds(at, half), :] = direct[...]
    at = pl.multiple_of((1 - flag[0]) * half, 16)
    out[pl.ds(at, half), :] = handed[...]


def pack_kernel(sizes, place, mlp_sums, hid_sums, attn_sums, bands, mask_rows, out):
    n, part = sizes
    me = place[0]
    dec, width = mask_rows.shape[1], out.shape[1]
    base = 5 * n
    row = lax.broadcasted_iota(jnp.int32, (base, width), 0)
    total = jnp.zeros((base, width), F32)

    def widened(values):
        return jnp.concatenate([values, jnp.zeros((1, width - values.shape[1]), F32)], axis=1)

    for e in range(n):
        at = e ^ me
        lanes = slice(e * part, (e + 1) * part)
        total = jnp.where(row == at, mlp_sums[e : e + 1, :], total)
        total = jnp.where(row == n + at, widened(attn_sums[4:5, lanes]), total)
        total = jnp.where(row == 2 * n + at, widened(attn_sums[5:6, lanes]), total)
        total = jnp.where(row == 3 * n + at, mlp_sums[n + 1 + e : n + 2 + e, :], total)
    total = jnp.where(row == 4 * n + me, widened(mask_rows[0:1, :]), total)
    out[:base, :] = total
    out[base : base + 4, :] = attn_sums[:4, :]
    out[base + 4 : base + 6, :] = hid_sums[:2, :]
    out[base + 6 : base + 7, :] = mlp_sums[n : n + 1, :]
    out[base + 7 :, :] = jnp.zeros((out.shape[0] - base - 7, width), F32)
    out[base + 7 : base + 9, :128] = bands[:2, :]


def write_out(plan, values, outs):
    at = 0
    for out, turned in zip(outs, plan):
        if turned:
            count = out.shape[1]
            out[...] = values[at : at + count, :].T.astype(F32)
        else:
            count = out.shape[0]
            out[...] = values[at : at + count, :].astype(F32)
        at += count


def finish_kernel(half, plan, flag, own, came, *refs):
    outs, held = refs[:-1], refs[-1]
    first = flag[0] == 0

    @pl.when(first)
    def _():
        held[:half, :] = own[...]
        held[half:, :] = came[...]

    @pl.when(jnp.logical_not(first))
    def _():
        held[:half, :] = came[...]
        held[half:, :] = own[...]

    write_out(plan, held, outs)


def band_sums(first, second):
    columns = first.shape[1]
    band = lax.broadcasted_iota(jnp.int32, (columns, 128), 0) % BANDS
    pick_band = (band == lax.broadcasted_iota(jnp.int32, band.shape, 1)).astype(F32)
    rows = jnp.concatenate([first, second, jnp.zeros((6, columns), F32)], axis=0)
    return jnp.dot(rows, pick_band, precision=lax.Precision.HIGHEST, preferred_element_type=F32)


def call(kernel, outs, args, name, scratch=(), us=2.0, scalars=0):
    run = pl.pallas_call(
        kernel,
        out_shape=[jax.ShapeDtypeStruct(shape, kind) for shape, kind in outs],
        in_specs=[SM] * scalars + [VM] * (len(args) - scalars),
        out_specs=[VM] * len(outs),
        scratch_shapes=list(scratch),
        compiler_params=params(),
        cost_estimate=pl.CostEstimate(
            flops=0, bytes_accessed=int(us * 3.3e6), transcendentals=0
        ),
        name=name,
    )
    return list(run(*args))


class Weights:
    def __init__(self, own, part, data_index):
        self.own, self.half = own, part.shape[0]
        self.flag = (data_index & 1).astype(jnp.int32)[None]
        self.direct = swap(part, "mp", 2)
        self.near = swap(own, "mp", 1)

    def hand_on(self):
        self.handed = swap(self.direct, "dp", 1)

    def join(self, line):
        rows, width = self.own.shape
        [far] = call(
            functools.partial(join_kernel, self.half),
            [((rows, width), BF16)],
            [self.flag, self.direct, line.wait(self.handed)],
            "join_weights",
            us=2.0,
            scalars=1,
        )
        line.mark(far)
        self.blocks = [self.own, self.near, far, swap(far, "mp", 1)]


def to_absolute(blocks, model_index):
    size = blocks.shape[0]
    for bit in bits_of("mp"):
        turned = jnp.stack([blocks[i ^ bit] for i in range(size)])
        blocks = jnp.where((model_index & bit) != 0, turned, blocks)
    return blocks


class Line:
    def __init__(self):
        self.last = None

    def wait(self, value):
        return value if self.last is None else after(value, self.last)

    def mark(self, value):
        self.last = value


class Reduction:
    def __init__(self, kept, sent, order, data_index, line, plan, shapes, name):
        self.kept, self.came = kept, swap(sent, "mp", 1)
        self.quarters, self.line, self.name = 2, line, name
        self.plan, self.shapes = plan, shapes
        self.flags = [((data_index >> k) & 1).astype(jnp.int32)[None] for k in range(len(bits_of("dp")))]
        self.order = list(order) + [k for k in range(len(self.flags)) if k not in order]
        self.done, self.own, self.hold = [], None, False

    def step(self):
        if self.order or self.own is None:
            self.scatter()
        elif len(self.done) > 1:
            self.gather()
        else:
            self.finish()

    def scatter(self):
        came = self.line.wait(self.came)
        axis = self.order.pop(0) if self.order else None
        rows = self.kept.shape[0] // self.quarters
        if axis is None:
            [self.own] = self.stage(came, None, 0)
            self.line.mark(self.own)
            self.came = swap(self.own, "dp", 1 << self.done[-1][0])
        elif axis == "x":
            self.kept, sent = self.stage(came, None, rows)
            self.line.mark(self.kept)
            self.quarters = 1
            self.sent = sent
            if not self.hold:
                self.launch()
        else:
            self.kept, sent = self.stage(came, self.flags[axis], rows // 2)
            self.line.mark(self.kept)
            self.done.append((axis, int(self.kept.shape[1] < came.shape[1])))
            self.came = swap(sent, "dp", 1 << axis)

    def launch(self, *before):
        self.came = swap(after(self.sent, *before) if before else self.sent, "mp", 2)

    def stage(self, came, flag, half):
        total, width = self.kept.shape
        quarters, rows = self.quarters, total // self.quarters
        if flag is not None and half % 16 and width % 256 == 0:
            part = width // 2

            def kernel(mine, a, b, own, other):
                for out, which in ((own, mine[0]), (other, 1 - mine[0])):
                    here = pl.ds(pl.multiple_of(which * part, 128), part)
                    out[...] = (a[:, here].astype(F32) + b[:, here].astype(F32)).astype(BF16)

            return call(
                kernel,
                [((total, part), BF16)] * 2,
                [flag, self.kept, came],
                "reduce_" + self.name,
                scalars=1,
            )
        if flag is not None and half % 16:
            summed = (self.kept.astype(F32) + came.astype(F32)).astype(BF16)
            summed = summed.reshape(quarters, rows, width)
            own = lax.dynamic_slice_in_dim(summed, flag[0] * half, half, 1)
            other = lax.dynamic_slice_in_dim(summed, (1 - flag[0]) * half, half, 1)
            return own.reshape(-1, width), other.reshape(-1, width)

        def total_of(a, b, at, count):
            here = pl.ds(at, count)
            return (a[here, :].astype(F32) + b[here, :].astype(F32)).astype(BF16)

        if flag is None:

            def kernel(a, b, *outs):
                for k, out in enumerate(outs):
                    out[...] = total_of(a, b, k * out.shape[0], out.shape[0])

            count = 1 if half == 0 else 2
            return call(
                kernel, [((total // count, width), BF16)] * count, [self.kept, came], "reduce_" + self.name
            )

        def kernel(mine, a, b, own, other):
            for q in range(quarters):
                here = slice(q * half, (q + 1) * half)
                at = pl.multiple_of(q * rows + mine[0] * half, 16)
                own[here, :] = total_of(a, b, at, half)
                at = pl.multiple_of(q * rows + (1 - mine[0]) * half, 16)
                other[here, :] = total_of(a, b, at, half)

        return call(
            kernel,
            [((total // 2, width), BF16)] * 2,
            [flag, self.kept, came],
            "reduce_" + self.name,
            scalars=1,
        )

    def gather(self):
        axis, dim = self.done.pop()
        came = self.line.wait(self.came)
        self.own = jnp.where(
            self.flags[axis][0] == 0,
            jnp.concatenate([self.own, came], axis=dim),
            jnp.concatenate([came, self.own], axis=dim),
        )
        self.line.mark(self.own)
        self.came = swap(self.own, "dp", 1 << self.done[-1][0])

    def finish(self):
        half, width = self.own.shape
        self.result = call(
            functools.partial(finish_kernel, half, self.plan),
            [(shape, F32) for shape in self.shapes],
            [self.flags[self.done[0][0]], self.own, self.line.wait(self.came)],
            "finish_" + self.name,
            [pltpu.VMEM((2 * half, width), BF16)],
            us=3.0,
            scalars=1,
        )
        self.line.mark(self.result[0])


class Sums:
    def __init__(self, values, line):
        self.values, self.line = values, line
        self.left = [(axis, bit) for axis in ("mp", "dp") for bit in bits_of(axis)]
        self.came = swap(values, *self.left[0])

    def step(self):
        self.values = self.values + self.line.wait(self.came)
        self.line.mark(self.values)
        self.left.pop(0)
        if self.left:
            self.came = swap(self.values, *self.left[0])


def exchange(tiles):
    size = lax.axis_size("dp")
    blocks = tiles.reshape(size, tiles.shape[0] // size, tiles.shape[1])
    return lax.all_to_all(blocks, "dp", split_axis=0, concat_axis=0, tiled=True).reshape(tiles.shape)


def shards(
    patches,
    vis_count,
    vis_pos,
    tile_sample,
    tile_quad,
    w_embed,
    b_embed,
    norm1_gain,
    norm1_bias,
    w_query,
    b_query,
    w_key,
    w_value,
    b_value,
    w_attn_out,
    b_attn_out,
    norm2_gain,
    norm2_bias,
    w_hidden,
    b_hidden,
    w_mlp_out,
    b_mlp_out,
    w_decoder,
    b_decoder,
    mask_token,
    cotangent,
):
    data_size = lax.axis_size("dp")
    model_size = lax.axis_size("mp")
    data_index = lax.axis_index("dp")
    model_index = lax.axis_index("mp")
    tile_count = vis_count.shape[0]
    visible = vis_pos.shape[1]
    grid_count, pixel_cols = patches.shape
    tile_tokens = grid_count // tile_count
    full_width = w_embed.shape[1]
    part_width = b_embed.shape[0]
    dec_part = b_decoder.shape[0]
    hid_part = b_hidden.shape[0]
    pair_tiles = tile_count // data_size
    own_samples = SAMP_OWN // model_size
    sample_rows = 4 * visible
    rows = own_samples * sample_rows
    my_tiles = own_samples * 4
    score_scale = HEAD_DIM ** (-0.5)

    tile_ids = jnp.arange(tile_count, dtype=jnp.int32)
    owners = tile_sample // SAMP_OWN
    earlier = (owners[:, None] == owners[None, :]) & (tile_ids[None, :] < tile_ids[:, None])
    tile_ranks = jnp.sum(earlier.astype(jnp.int32), axis=1)
    slot_of = owners * pair_tiles + tile_ranks
    at_slot = slot_of[None, :] == tile_ids[:, None]
    order = jnp.sum(jnp.where(at_slot, tile_ids[None, :], 0), axis=1)
    tile_code = (tile_sample % SAMP_OWN) * 4 + tile_quad
    pos_wide = jnp.pad(vis_pos, ((0, 0), (0, 128 - visible)), constant_values=-1000)

    line = Line()
    [stats] = call(stats_kernel, [((8, 128), F32)], [patches], "band_sums", us=4.0)
    stats = stats + swap(stats, "mp", 1)
    stats = stats + swap(stats, "mp", 2)

    small = [b_embed, b_query, b_value, b_attn_out, b_mlp_out, b_decoder, b_hidden]
    base = pixel_cols + 4 * part_width
    own_first, own_second, cut_first, cut_second = call(
        prep_kernel,
        [((base + 32, full_width), BF16), ((2 * hid_part + dec_part, full_width), BF16)]
        + [(((base + 32) // 2, full_width), BF16), (((2 * hid_part + dec_part) // 2, full_width), BF16)],
        [(data_index & 1).astype(jnp.int32)[None]]
        + [w_query.T, w_key.T, w_value.T, w_attn_out, w_hidden, w_mlp_out, w_decoder]
        + [after(w_embed, stats)]
        + [v[None, :] for v in small],
        "prep_weights",
        us=5.0,
        scalars=1,
    )
    line.mark(own_first)
    first_w = Weights(own_first, cut_first, data_index)
    by_slot = jnp.where(at_slot, 1.0, 0.0)
    codes_slot = jnp.sum(by_slot * tile_code.astype(F32)[None, :], axis=1)
    counts_slot = jnp.sum(by_slot * vis_count.astype(F32)[None, :], axis=1)
    pos_slot = jnp.sum(by_slot[:, :, None] * vis_pos.astype(F32)[None, :, :], axis=1)
    info = jnp.concatenate([codes_slot[None], counts_slot[None]], axis=0)
    info = jnp.pad(info, ((0, 6), (0, 128 - tile_count)))
    packet = jnp.concatenate([stats, info, pos_slot.reshape(-1, 128)], axis=0)[None]
    for k, bit in enumerate(bits_of("dp")):
        came = swap(packet, "dp", bit)
        if k == 0:
            picked, cot_picked, mask_rows = call(
                functools.partial(pick_kernel, tile_tokens),
                [
                    ((tile_count * visible, pixel_cols), BF16),
                    ((tile_count * visible, dec_part), BF16),
                    ((8, dec_part), F32),
                ],
                [line.wait(order), vis_count, pos_wide, patches, cotangent],
                "pick_rows",
                us=7.5,
                scalars=2,
            )
            came = after(came, picked)
        packet = jnp.where(
            (data_index >> k) & 1 == 0,
            jnp.concatenate([packet, came], axis=0),
            jnp.concatenate([came, packet], axis=0),
        )

    arrived = exchange(after(picked, packet, first_w.direct))

    second_w = Weights(own_second, after(cut_second, first_w.direct), data_index)
    first_w.hand_on()
    second_w.hand_on()

    own_info = lax.dynamic_slice_in_dim(packet[:, 8:10], data_index * pair_tiles, pair_tiles, 2)
    own_info = own_info.transpose(1, 0, 2).reshape(2, tile_count).astype(jnp.int32)
    my_tiles_bit = model_index * my_tiles
    codes = own_info[0] ^ my_tiles_bit
    total = jnp.sum(packet[:, :2, :BANDS], axis=0)
    per_band = float(grid_count * data_size * (pixel_cols // BANDS) * model_size)
    band_mean = total[0] / per_band
    band_var = total[1] / per_band - band_mean * band_mean
    band_rstd = lax.rsqrt(band_var + band_eps)
    mean_cols = jnp.tile(band_mean, pixel_cols // BANDS)
    rstd_cols = jnp.tile(band_rstd, pixel_cols // BANDS)

    own_pos = packet[:, 16:].reshape(data_size, tile_count, visible)
    own_pos = lax.dynamic_slice_in_dim(own_pos, data_index * pair_tiles, pair_tiles, 1)
    own_pos = own_pos.reshape(tile_count, visible)
    mine = (codes[None, :] == jnp.arange(my_tiles)[:, None]).astype(F32)
    my_counts = jnp.sum(mine * own_info[1].astype(F32)[None, :], axis=1)
    my_pos = jnp.sum(mine[:, :, None] * own_pos[None], axis=1)
    my_pos = my_pos.astype(jnp.int32)
    live = jnp.arange(visible)[None, :] < my_counts.astype(jnp.int32)[:, None]
    live_col = live.reshape(rows, 1)
    usable = live.reshape(own_samples, sample_rows)
    quadrant = (jnp.arange(my_tiles) % 4)[:, None]
    inner = my_pos % (SIDE * SIDE)
    frames = tile_tokens // (SIDE * SIDE)
    col_at = quadrant % 2 * SIDE + inner % SIDE
    row_at = quadrant // 2 * SIDE + inner // SIDE + 2 * SIDE
    frame_at = my_pos // (SIDE * SIDE) + 4 * SIDE
    table = place_table(full_width, frames)
    high = table.astype(jnp.bfloat16)
    low = (table - high.astype(np.float32)).astype(jnp.bfloat16)
    wide = np.zeros((128, full_width), jnp.bfloat16)
    wide[: table.shape[0]], wide[64 : 64 + table.shape[0]] = high, low
    lane = jnp.arange(128)[None, :]
    spots = jnp.where(lane < 127, lane % 64, -1)
    chosen = (
        (col_at.reshape(rows, 1) == spots)
        | (row_at.reshape(rows, 1) == spots)
        | (frame_at.reshape(rows, 1) == spots)
        | ((lane == 127) & live_col)
    ).astype(BF16)
    key_mask = jnp.pad(usable.astype(F32), ((0, 8 - own_samples), (0, 0)))
    cols = jnp.pad(jnp.stack([mean_cols, rstd_cols]), ((0, 6), (0, 0)))

    line = Line()
    held = after(arrived, second_w.direct, chosen, key_mask, cols)
    own, near, far = place_in(codes, held, visible, model_size)
    line.mark(far)
    pix = Crossing(own, near, far)
    arrived_cot = exchange(after(cot_picked, far))
    first_w.join(line)
    pix.relay(line)
    line.mark(pix.parts[1])
    own, near, far = place_in(codes, line.wait(arrived_cot), visible, model_size)
    line.mark(far)
    cot = Crossing(own, near, far)
    bias_rel = [first_w.blocks[e][base : base + 16] for e in range(4)]
    bias_rel = jnp.stack(bias_rel).astype(F32)
    bias_abs = to_absolute(bias_rel, model_index)

    def rel_vec(k):
        return bias_rel[:, k, : small[k].shape[0]].reshape(1, -1)

    def abs_vec(k):
        return bias_abs[:, k, : small[k].shape[0]].reshape(1, -1)

    gains = [norm1_gain, norm1_bias, norm2_gain, norm2_bias]
    gains = [v[None].astype(F32) for v in gains]
    vecs = jnp.concatenate(
        [abs_vec(0), gains[0], gains[1], rel_vec(1), rel_vec(2), abs_vec(3)]
        + [gains[2], gains[3], abs_vec(4), jnp.zeros((7, full_width), F32)]
    )
    bias_hid, bias_dec = bias_rel[:, 6, :hid_part], bias_rel[:, 5, :dec_part]

    square = ((rows, full_width), BF16)
    wide_rows = ((rows, full_width), F32)
    heads = own_samples * full_width // HEAD_DIM
    weight_scratch = pltpu.VMEM((full_width, full_width), BF16)
    start, queries, key_rows, value_rows, probs, attended, middle = call(
        functools.partial(embed_kernel, (model_size, part_width, sample_rows)),
        [square] * 4 + [((heads, sample_rows, sample_rows), BF16), square, wide_rows],
        [chosen, jnp.asarray(wide), cols, vecs, line.wait(key_mask)] + pix.parts + first_w.blocks,
        "embed_attend",
        [weight_scratch],
        us=19.0,
    )
    line.mark(middle)
    cot.relay(line)
    second_w.join(line)
    decoded_shape = ((rows, dec_part), BF16)
    hidden_shape = ((rows, hid_part), BF16)
    out = call(
        functools.partial(mlp_kernel, model_size),
        [decoded_shape] * 2
        + [((2 * rows, dec_part), BF16)]
        + [hidden_shape] * model_size
        + [((2 * (hid_part + dec_part), full_width), BF16)] * 2
        + [wide_rows, ((16, full_width), F32)],
        [middle, vecs, bias_hid, bias_dec] + cot.parts + second_w.blocks,
        "mlp_decode",
        [pltpu.VMEM((model_size, rows, hid_part), BF16)] * 2,
        us=20.0,
    )
    decoded_rows, pre_grads = out[:3], out[3 : 3 + model_size]
    out_kept, out_sent, final_grad, mlp_sums = out[3 + model_size :]
    decoded_mp = Crossing(*decoded_rows)
    red_a = Reduction(
        out_kept,
        out_sent,
        ["x", 0, 1, 2],
        data_index,
        line,
        (False, True),
        [w_mlp_out.shape, w_decoder.shape],
        "out",
    )
    def decoded_step(decoded_dp):
        out = call(
            functools.partial(spread_kernel, tile_tokens),
            [((grid_count, dec_part), BF16)],
            [order, vis_count, pos_wide, mask_token[None, :], line.wait(decoded_dp)],
            "spread_decoded",
            us=3.5,
            scalars=2,
        )
        line.mark(out[0])
        return out

    def go_home(crossing):
        parts = crossing.parts
        tiles = place_out(codes, [parts[0], line.wait(parts[1]), parts[2]], visible)
        line.mark(tiles)
        return exchange(tiles)

    out = call(
        functools.partial(hidden_kernel, model_size),
        [((2 * (hid_part + part_width), full_width), BF16)] * 2 + [wide_rows, ((8, full_width), F32)],
        [middle, vecs, final_grad, attended] + pre_grads + second_w.blocks,
        "hidden_back",
        us=13.0,
    )
    hid_kept, hid_sent, middle_grad, hid_sums = out
    line.mark(middle_grad)
    decoded_mp.relay(line)
    red_a.step()
    red_b = Reduction(
        hid_kept, line.wait(hid_sent), ["x", 0, 1, 2], data_index, line, (True, False), [w_hidden.shape, w_attn_out.shape], "hidden"
    )
    start_grad, dq, dk, dv, attn_sums = call(
        functools.partial(attn_back_kernel, (model_size, part_width, sample_rows, pixel_cols)),
        [square] * 4 + [((8, full_width), F32)],
        [line.wait(middle_grad), start, queries, key_rows, value_rows]
        + [probs, chosen, vecs]
        + first_w.blocks,
        "attend_back",
        [weight_scratch, pltpu.VMEM((rows, full_width), BF16)],
        us=18.0,
    )
    line.mark(start_grad)
    decoded_dp = go_home(decoded_mp)
    out = call(
        functools.partial(pixel_grad_kernel, model_size),
        [((rows, pixel_cols), BF16)] * 2 + [((2 * rows, pixel_cols), BF16), ((8, 128), F32)],
        [line.wait(start_grad), cols] + pix.parts + first_w.blocks,
        "pixel_grad",
        us=6.7,
    )
    normed_grad, bands = out[:3], out[3]
    line.mark(bands)
    grad_mp = Crossing(*normed_grad)
    [sums] = call(
        functools.partial(pack_kernel, (model_size, part_width)),
        [((32, full_width), F32)],
        [model_index.astype(jnp.int32)[None], mlp_sums, hid_sums, attn_sums, line.wait(bands)]
        + [mask_rows],
        "pack_sums",
        us=1.5,
        scalars=1,
    )
    line.mark(sums)
    sums = Sums(sums, line)
    sums.step()
    red_b.hold = True
    red_b.step()
    red_a.step()
    spread = decoded_step(decoded_dp)
    first_kept, first_sent = call(
        functools.partial(weight_kernel, (model_size, part_width)),
        [((2 * (base - part_width), full_width), BF16)] * 2,
        [line.wait(start_grad), start, dq, dk, dv, cols, vecs] + pix.parts,
        "weight_grad",
        us=10.0,
    )
    line.mark(first_kept)
    red_a.step()
    grad_mp.relay(line)
    sums.step()
    red_b.launch(sums.values)
    red_c = Reduction(
        first_kept,
        line.wait(first_sent),
        ["x", 0, 1, 2],
        data_index,
        line,
        (False,) * 4,
        [w_embed.shape] + [w_attn_out.shape] * 3,
        "first",
    )

    def patch_step(grad_dp):
        bands_all = sums.values[5 * model_size + 7 : 5 * model_size + 9, :BANDS]
        grad_all, cross_all = bands_all[0], bands_all[1]
        grad_var = -0.5 * cross_all * band_rstd * band_rstd * band_rstd
        grad_mean = -band_rstd * grad_all - 2.0 * band_mean * grad_var
        terms = jnp.stack([grad_mean / per_band, 2.0 * grad_var / per_band, band_rstd])
        terms = jnp.pad(jnp.tile(terms, (1, pixel_cols // BANDS)), ((0, 5), (0, 0)))
        out = call(
            functools.partial(patch_kernel, tile_tokens),
            [((grid_count, pixel_cols), F32)],
            [order, vis_count, pos_wide, terms, patches, line.wait(grad_dp)],
            "spread_patch_grad",
            us=8.0,
            scalars=2,
        )
        line.mark(out[0])
        return out

    def steps(*chains):
        for chain in chains:
            chain.step()

    kept = {}

    def go(name):
        if name in chains:
            chains[name].step()
        elif name == "H":
            kept["grad"] = go_home(grad_mp)
        elif name == "P":
            while sums.left:
                sums.step()
            kept["patch"] = patch_step(kept["grad"])
    chains = {"a": red_a, "b": red_b, "c": red_c, "s": sums}
    for name in "cassasabHabcabcbPcbcbcbcc":
        go(name)
    while sums.left:
        sums.step()
    while not all(hasattr(chain, "result") for chain in (red_a, red_b, red_c)):
        for chain in (red_a, red_b, red_c):
            if not hasattr(chain, "result"):
                chain.step()
    [patch_grad], [decoded] = kept["patch"], spread

    n = model_size
    sums = sums.values
    own_rows = [
        lax.dynamic_slice_in_dim(sums, model_index + k * n, 1, 0)[0] for k in range(5)
    ]
    sum_hidden = own_rows[0]
    sum_query, sum_value = own_rows[1][:part_width], own_rows[2][:part_width]
    sum_dec, grad_mask_token = own_rows[3][:dec_part], own_rows[4][:dec_part]
    gain_one, bias_one, embed_sum, attn_out_sum, gain_two, bias_two, mlp_out_sum = (
        sums[5 * n + k] for k in range(7)
    )

    def mine_of(vector):
        part = vector.shape[0] // model_size
        return lax.dynamic_slice_in_dim(vector, model_index * part, part, 0)

    (g_out, g_dec), (g_hid, g_attn) = red_a.result, red_b.result
    g_embed, g_query, g_key, g_value = red_c.result

    return (
        decoded,
        patch_grad,
        g_embed,
        mine_of(embed_sum),
        gain_one,
        bias_one,
        g_query.T,
        sum_query,
        g_key.T,
        g_value.T,
        sum_value,
        g_attn,
        mine_of(attn_out_sum),
        gain_two,
        bias_two,
        g_hid,
        sum_hidden,
        g_out,
        mine_of(mlp_out_sum),
        g_dec,
        sum_dec,
        grad_mask_token,
    )


def solution(mesh):
    in_specs = (
        P("dp", "mp"),
        P("dp"),
        P("dp", None),
        P("dp"),
        P("dp"),
        P("mp", None),
        P("mp"),
        P(),
        P(),
        P(None, "mp"),
        P("mp"),
        P(None, "mp"),
        P(None, "mp"),
        P("mp"),
        P("mp", None),
        P("mp"),
        P(),
        P(),
        P(None, "mp"),
        P("mp"),
        P("mp", None),
        P("mp"),
        P(None, "mp"),
        P("mp"),
        P("mp"),
        P("dp", "mp"),
    )
    out_specs = (
        P("dp", "mp"),
        P("dp", "mp"),
        P("mp", None),
        P("mp"),
        P(),
        P(),
        P(None, "mp"),
        P("mp"),
        P(None, "mp"),
        P(None, "mp"),
        P("mp"),
        P("mp", None),
        P("mp"),
        P(),
        P(),
        P(None, "mp"),
        P("mp"),
        P("mp", None),
        P("mp"),
        P(None, "mp"),
        P("mp"),
        P("mp"),
    )
    return jax.shard_map(shards, mesh=mesh, in_specs=in_specs, out_specs=out_specs, check_vma=False)
```

```python
import functools

import jax
import jax.numpy as jnp
import numpy as np
from jax import lax
from jax.experimental import pallas as pl
from jax.experimental.pallas import tpu as pltpu
from jax.sharding import PartitionSpec as P

HEAD_DIM = 64
BANDS = 6
SIDE = 7
SAMP_OWN = 8
WINDOW = 176
VMEM_BYTES = 56 * 1024 * 1024

norm_eps = 1e-06
band_eps = 1e-06
big_negative = -1000000000.0
F32 = jnp.float32
BF16 = jnp.bfloat16


def params():
    return pltpu.CompilerParams(vmem_limit_bytes=VMEM_BYTES)


VM = pl.BlockSpec(memory_space=pltpu.VMEM)
SM = pl.BlockSpec(memory_space=pltpu.SMEM)


def swap(values, axis, bit):
    size = lax.axis_size(axis)
    return lax.ppermute(values, axis, [(i, i ^ bit) for i in range(size)])


def bits_of(axis):
    size = lax.axis_size(axis)
    return [1 << k for k in range(size.bit_length() - 1)]


def after(value, *before):
    return lax.optimization_barrier((value,) + before)[0]


def dot(left, right):
    return jnp.dot(left, right, preferred_element_type=F32)


def dot_t(left, right):
    return lax.dot_general(left, right, (((1,), (1,)), ((), ())), preferred_element_type=F32)


def dot_tl(left, right):
    return lax.dot_general(left, right, (((0,), (0,)), ((), ())), preferred_element_type=F32)


def window_of(tile, tile_tokens, total):
    base = tile * tile_tokens
    start = jnp.minimum((base // 16) * 16, total - WINDOW)
    return pl.multiple_of(start, 16), base - start


def hot_rows(pos_ref, count, tile, rem):
    lane = lax.broadcasted_iota(jnp.int32, (1, 128), 1)
    target = jnp.where(lane < count, pos_ref[pl.ds(tile, 1), :] + rem, -1)
    row = lax.broadcasted_iota(jnp.int32, (WINDOW, 128), 0)
    return row == target


def stats_kernel(patches, stats):
    def sum_step(i, carry):
        first, second = carry
        at = pl.multiple_of(i * 336, 16)
        x = patches[pl.ds(at, 336), :].astype(F32).reshape(42, 8, patches.shape[1])
        return first + jnp.sum(x, axis=0), second + jnp.sum(x * x, axis=0)

    blank = jnp.zeros((8, patches.shape[1]), F32)
    first, second = lax.fori_loop(0, patches.shape[0] // 336, sum_step, (blank, blank))
    stats[...] = band_sums(
        jnp.sum(first, axis=0, keepdims=True), jnp.sum(second, axis=0, keepdims=True)
    )


def pick_kernel(tile_tokens, order, count, pos, patches, cot, picked, cot_picked, mask_sum):
    total = patches.shape[0]
    slots = order.shape[0]
    visible = picked.shape[0] // slots
    mask_total = jnp.zeros((8, cot.shape[1]), F32)
    row = lax.broadcasted_iota(jnp.int32, (WINDOW, 128), 0)
    lane = lax.broadcasted_iota(jnp.int32, (WINDOW, 128), 1)
    for slot in range(slots):
        tile = order[slot]
        start, rem = window_of(tile, tile_tokens, total)
        hot = hot_rows(pos, count[tile], tile, rem).astype(F32)
        shown = jnp.sum(hot, axis=1, keepdims=True)
        inside = jnp.logical_and(row >= rem, row < rem + tile_tokens)
        hidden = jnp.where(inside, 1.0 - shown, 0.0)
        chooser = jnp.where(lane == visible, hidden, hot).astype(BF16)
        got = dot_tl(chooser, patches[pl.ds(start, WINDOW), :])
        got_cot = dot_tl(chooser, cot[pl.ds(start, WINDOW), :])
        here = slice(slot * visible, (slot + 1) * visible)
        picked[here, :] = got[:visible].astype(BF16)
        cot_picked[here, :] = got_cot[:visible].astype(BF16)
        mask_total = mask_total + got_cot[visible : visible + 8]
    mask_sum[...] = mask_total


def place_in(codes, tiles, visible, blocks):
    rows, cols = tiles.shape
    each = rows // blocks

    def kernel(code_ref, tile_ref, *refs):
        outs, held = refs[:-1], refs[-1]
        for k in range(rows // visible):
            at = pl.multiple_of(code_ref[k] * visible, 16)
            held[pl.ds(at, visible), :] = tile_ref[k * visible : (k + 1) * visible, :]
        at = 0
        for out in outs:
            out[...] = held[at : at + out.shape[0], :]
            at += out.shape[0]

    return call(
        kernel,
        [((each, cols), tiles.dtype)] * 2 + [((2 * each, cols), tiles.dtype)],
        [codes, tiles],
        "place_tiles",
        [pltpu.VMEM((rows, cols), tiles.dtype)],
        scalars=1,
    )


def place_out(codes, parts, visible):
    rows, cols = parts[0].shape
    total = 4 * rows

    def kernel(code_ref, own, near, far, out, held):
        for b, ref in enumerate(blocks_of((own, near, far))):
            held[b * rows : (b + 1) * rows, :] = ref[...]
        for k in range(total // visible):
            at = pl.multiple_of(code_ref[k] * visible, 16)
            out[k * visible : (k + 1) * visible, :] = held[pl.ds(at, visible), :]

    return call(
        kernel,
        [((total, cols), parts[0].dtype)],
        [codes] + parts,
        "return_tiles",
        [pltpu.VMEM((total, cols), parts[0].dtype)],
        scalars=1,
    )[0]


def blocks_of(crossed):
    own, near, far = crossed
    rows = own.shape[0]
    return [own, near.at[:rows], far.at[:rows], near.at[rows:]]


class Crossing:
    def __init__(self, own, near, far):
        self.own, self.near = own, near
        self.far = swap(far, "mp", 2)

    def relay(self, line):
        rows = self.own.shape[0]
        both = jnp.concatenate([self.near, line.wait(self.far)[rows:]], axis=0)
        line.mark(both)
        self.parts = [self.own, swap(both, "mp", 1), self.far]


def spread_kernel(tile_tokens, order, count, pos, mask_token, given, out):
    total = out.shape[0]
    slots = order.shape[0]
    visible = given.shape[0] // slots
    out[...] = jnp.broadcast_to(mask_token[...], out.shape)
    for slot in range(slots):
        tile = order[slot]
        start, rem = window_of(tile, tile_tokens, total)
        hot = hot_rows(pos, count[tile], tile, rem).astype(F32)
        shown = jnp.sum(hot, axis=1, keepdims=True) > 0.5
        rows = given[slot * visible : (slot + 1) * visible, :]
        new = dot(hot[:, :visible].astype(BF16), rows).astype(BF16)
        here = pl.ds(start, WINDOW)
        out[here, :] = jnp.where(shown, new, out[here, :])


def patch_kernel(tile_tokens, order, count, pos, cols, patches, given, out):
    total = out.shape[0]
    slots = order.shape[0]
    visible = given.shape[0] // slots

    def base_step(i, carry):
        at = pl.multiple_of(i * 336, 16)
        here = pl.ds(at, 336)
        out[here, :] = cols[0:1, :] + patches[here, :].astype(F32) * cols[1:2, :]
        return carry

    lax.fori_loop(0, total // 336, base_step, 0)
    for slot in range(slots):
        tile = order[slot]
        start, rem = window_of(tile, tile_tokens, total)
        hot = hot_rows(pos, count[tile], tile, rem).astype(F32)
        rows = given[slot * visible : (slot + 1) * visible, :]
        new = dot(hot[:, :visible].astype(BF16), rows)
        here = pl.ds(start, WINDOW)
        out[here, :] = out[here, :] + new * cols[2:3, :]


def sincos_table(limit, full_width):
    half_width = full_width // 2
    frequency = 1.0 / 10000.0 ** (np.arange(half_width, dtype=np.float32) / half_width)
    angles = np.arange(limit, dtype=np.float32)[:, None] * frequency.astype(np.float32)
    return np.concatenate([np.sin(angles), np.cos(angles)], axis=-1).astype(np.float32)


def place_table(full_width, frames):
    part = full_width // 16 * 6
    lines = 2 * SIDE
    table = np.zeros((2 * lines + frames, full_width), np.float32)
    table[:lines, :part] = sincos_table(lines, part)
    table[lines : 2 * lines, part : 2 * part] = sincos_table(lines, part)
    table[2 * lines :, 2 * part :] = sincos_table(frames, full_width - 2 * part)
    return table


def norm_forward(full_rows, gain_vec, bias_vec):
    values = full_rows.astype(F32)
    centred = values - jnp.mean(values, axis=-1, keepdims=True)
    inverse_std = lax.rsqrt(jnp.mean(centred * centred, axis=-1, keepdims=True) + norm_eps)
    unit_rows = centred * inverse_std
    normed_low = (unit_rows * gain_vec + bias_vec).astype(BF16)
    return (unit_rows, inverse_std, normed_low)


def row_sum(values):
    return jnp.sum(values.astype(F32), axis=0, keepdims=True)


def norm_backward(out_grad, unit_rows, inverse_std, gain_vec):
    scaled = out_grad * gain_vec
    first_mean = jnp.mean(scaled, axis=-1, keepdims=True)
    cross_mean = jnp.mean(scaled * unit_rows, axis=-1, keepdims=True)
    input_grad = inverse_std * (scaled - first_mean - unit_rows * cross_mean)
    return (input_grad, row_sum(out_grad * unit_rows), row_sum(out_grad))


def prep_kernel(odd, q, k, v, attn, hid, out, dec, embed, *refs):
    biases, (first, second, first_cut, second_cut) = refs[:-4], refs[-4:]
    e, w, h = embed.shape[0], q.shape[0], hid.shape[1]
    first[:e, :] = embed[...]
    for i, ref in enumerate((q, k, v)):
        first[e + i * w : e + (i + 1) * w, :] = ref[...]
    first[e + 3 * w : e + 4 * w, :] = attn[...]
    base = e + 4 * w
    first[base:, :] = jnp.zeros((first.shape[0] - base, first.shape[1]), BF16)
    for i, ref in enumerate(biases):
        first[base + i : base + i + 1, : ref.shape[1]] = ref[...]
    second[:h, :] = hid[...].T
    second[h : 2 * h, :] = out[...]
    second[2 * h :, :] = dec[...].T
    for whole, part in ((first, first_cut), (second, second_cut)):
        half = part.shape[0]
        part[...] = whole[pl.ds(pl.multiple_of(odd[0] * half, 16), half), :]


def copy_rows(target, refs, start, count):
    for e, ref in enumerate(refs):
        target[e * count : (e + 1) * count, :] = ref[start : start + count, :]


def normed_pixels(pix, cols):
    centred = pix[...].astype(F32) - cols[0:1, :]
    return centred, (centred * cols[1:2, :]).astype(BF16)


def embed_kernel(sizes, chosen, table, cols, vecs, mask, *refs):
    n, part, rows_s = sizes
    pix, weights = blocks_of(refs[:3]), refs[3 : 3 + n]
    start_ref, q_ref, k_ref, v_ref, probs, att_ref, middle, full = refs[3 + n :]
    e_rows = pix[0].shape[1]
    rows, width = start_ref.shape
    total = dot(chosen[...], table[...]) + vecs[0:1, :]
    for e in range(n):
        total = total + dot(normed_pixels(pix[e], cols)[1], weights[e][:e_rows, :])
    live = chosen[:, 127:128].astype(F32) > 0.5
    start = jnp.where(live, total, 0.0).astype(BF16)
    start_ref[...] = start
    normed = norm_forward(start, vecs[1:2, :], vecs[2:3, :])[2]
    copy_rows(full, weights, e_rows, part)
    q_ref[...] = (dot_t(normed, full[...]) + vecs[3:4, :]).astype(BF16)
    copy_rows(full, weights, e_rows + part, part)
    k_ref[...] = dot_t(normed, full[...]).astype(BF16)
    copy_rows(full, weights, e_rows + 2 * part, part)
    v_ref[...] = (dot_t(normed, full[...]) + vecs[4:5, :]).astype(BF16)
    scale = HEAD_DIM ** (-0.5)
    low = lax.broadcasted_iota(jnp.int32, (rows_s, 128), 1) < HEAD_DIM
    zero = jnp.zeros((rows_s, 128), BF16)

    def pair_step(i, carry):
        s, p = i // (width // 128), i % (width // 128)
        here = pl.ds(pl.multiple_of(s * rows_s, 16), rows_s)
        lanes = pl.ds(pl.multiple_of(p * 128, 128), 128)
        q2, k2, v2 = q_ref[here, lanes], k_ref[here, lanes], v_ref[here, lanes]
        extra = mask[pl.ds(s, 1), :]
        got = jnp.zeros((rows_s, 128), F32)
        for h in range(2):
            keep = low if h == 0 else jnp.logical_not(low)
            scores = dot_t(q2, jnp.where(keep, k2, zero)) * scale
            scores = jnp.where(extra > 0.5, scores, big_negative)
            shifted = jnp.exp(scores - jnp.max(scores, axis=-1, keepdims=True))
            share = (shifted / jnp.sum(shifted, axis=-1, keepdims=True)).astype(BF16)
            probs[i * 2 + h] = share
            got = got + dot(share, jnp.where(keep, v2, zero))
        att_ref[here, lanes] = got.astype(BF16)
        return carry

    lax.fori_loop(0, (rows // rows_s) * (width // 128), pair_step, 0)
    copy_rows(full, weights, e_rows + 3 * part, part)
    middle[...] = start_ref[...].astype(F32) + dot(att_ref[...], full[...]) + vecs[5:6, :]


def gelu_pair(x):
    cdf = 0.5 * (1.0 + lax.erf(x * (2.0**-0.5)))
    pdf = jnp.exp(-0.5 * x * x) * float(1.0 / np.sqrt(2.0 * np.pi))
    return x * cdf, cdf + x * pdf


def split_blocks(kept, sent, n):
    count = 2 * kept.shape[0] // n
    return [
        (kept if e % 2 == 0 else sent).at[e // 2 * count : (e // 2 + 1) * count] for e in range(n)
    ]


def mlp_kernel(n, middle, vecs, bias_hid, bias_dec, *refs):
    cot, weights, refs = blocks_of(refs[:3]), refs[3 : 3 + n], refs[3 + n :]
    rows = middle.shape[0]
    decoded = [refs[0], refs[1], refs[2].at[:rows], refs[2].at[rows:]]
    pre_refs = refs[3 : 3 + n]
    kept, sent, final_grad, sums, hidden, slope = refs[3 + n :]
    grads = split_blocks(kept, sent, n)
    h = pre_refs[0].shape[1]
    dec = decoded[0].shape[1]
    normed = norm_forward(middle[...].astype(BF16), vecs[6:7, :], vecs[7:8, :])[2]
    total = middle[...] + vecs[8:9, :]
    for e in range(n):
        pre = dot_t(normed, weights[e][:h, :]) + bias_hid[e : e + 1, :]
        value, grad = gelu_pair(pre)
        value = value.astype(BF16)
        hidden[e] = value
        slope[e] = grad.astype(BF16)
        total = total + dot(value, weights[e][h : 2 * h, :])
    final = total.astype(BF16)
    back = jnp.zeros(total.shape, F32)
    sums[...] = jnp.zeros(sums.shape, F32)
    for e in range(n):
        w_dec = weights[e][2 * h :, :]
        decoded[e][...] = (dot_t(final, w_dec) + bias_dec[e : e + 1, :]).astype(BF16)
        back = back + dot(cot[e][...], w_dec)
        grads[e][h:, :] = dot_tl(cot[e][...], final).astype(BF16)
        sums[n + 1 + e : n + 2 + e, :dec] = row_sum(cot[e][...])
    final_grad[...] = back
    low = back.astype(BF16)
    sums[n : n + 1, :] = row_sum(low)
    for e in range(n):
        grads[e][:h, :] = dot_tl(hidden[e], low).astype(BF16)
        pre_grad = (dot_t(low, weights[e][h : 2 * h, :]) * slope[e].astype(F32)).astype(BF16)
        pre_refs[e][...] = pre_grad
        sums[e : e + 1, :] = row_sum(pre_grad)


def hidden_kernel(n, middle, vecs, final_grad, att, *refs):
    pre, weights = refs[:n], refs[n : 2 * n]
    kept, sent, middle_grad, sums = refs[2 * n :]
    grads = split_blocks(kept, sent, n)
    h = pre[0].shape[1]
    unit, rstd, normed = norm_forward(middle[...].astype(BF16), vecs[6:7, :], vecs[7:8, :])
    total = jnp.zeros(unit.shape, F32)
    for e in range(n):
        total = total + dot(pre[e][...], weights[e][:h, :])
        grads[e][:h, :] = dot_tl(pre[e][...], normed).astype(BF16)
    term, gain, bias = norm_backward(total, unit, rstd, vecs[6:7, :])
    middle_grad[...] = final_grad[...] + term
    part = kept.shape[0] // 2 - h
    low_grad = middle_grad[...].astype(BF16)
    weight_grads(n, part, h, ((att, low_grad),), kept, sent)
    sums[0:1, :] = gain
    sums[1:2, :] = bias
    sums[2:8, :] = jnp.zeros((6, sums.shape[1]), F32)


def attn_back_kernel(sizes, middle_grad, start, q, k, v, probs, chosen, vecs, *refs):
    n, part, rows_s, e_rows = sizes
    weights = refs[:n]
    start_grad, dq, dk, dv, sums, full, ag = refs[n:]
    rows, width = start.shape
    copy_rows(full, weights, e_rows + 3 * part, part)
    low_grad = middle_grad[...].astype(BF16)
    ag[...] = dot_t(low_grad, full[...]).astype(BF16)
    scale = HEAD_DIM ** (-0.5)
    low = lax.broadcasted_iota(jnp.int32, (rows_s, 128), 1) < HEAD_DIM
    zero = jnp.zeros((rows_s, 128), BF16)

    def pair_step(i, carry):
        s, p = i // (width // 128), i % (width // 128)
        here = pl.ds(pl.multiple_of(s * rows_s, 16), rows_s)
        lanes = pl.ds(pl.multiple_of(p * 128, 128), 128)
        q2, k2, v2, g2 = q[here, lanes], k[here, lanes], v[here, lanes], ag[here, lanes]
        tq = jnp.zeros((rows_s, 128), F32)
        tk = jnp.zeros((rows_s, 128), F32)
        tv = jnp.zeros((rows_s, 128), F32)
        for h in range(2):
            keep = low if h == 0 else jnp.logical_not(low)
            share = probs[i * 2 + h]
            wide = share.astype(F32)
            prob_grad = dot_t(g2, jnp.where(keep, v2, zero))
            delta = jnp.sum(wide * prob_grad, axis=-1, keepdims=True)
            score_grad = (wide * (prob_grad - delta)).astype(BF16)
            tv = tv + dot_tl(share, jnp.where(keep, g2, zero))
            tq = tq + dot(score_grad, jnp.where(keep, k2, zero))
            tk = tk + dot_tl(score_grad, jnp.where(keep, q2, zero))
        dq[here, lanes] = (tq * scale).astype(BF16)
        dk[here, lanes] = (tk * scale).astype(BF16)
        dv[here, lanes] = tv.astype(BF16)
        return carry

    lax.fori_loop(0, (rows // rows_s) * (width // 128), pair_step, 0)
    copy_rows(full, weights, e_rows, part)
    total = dot(dq[...], full[...])
    copy_rows(full, weights, e_rows + part, part)
    total = total + dot(dk[...], full[...])
    copy_rows(full, weights, e_rows + 2 * part, part)
    total = total + dot(dv[...], full[...])
    unit, rstd, _ = norm_forward(start[...], vecs[1:2, :], vecs[2:3, :])
    term, gain, bias = norm_backward(total, unit, rstd, vecs[1:2, :])
    live = chosen[:, 127:128].astype(F32) > 0.5
    grad = jnp.where(live, middle_grad[...] + term, 0.0).astype(BF16)
    start_grad[...] = grad
    sums[0:1, :] = gain
    sums[1:2, :] = bias
    sums[2:3, :] = row_sum(grad)
    sums[3:4, :] = row_sum(low_grad)
    sums[4:5, :] = row_sum(dq[...])
    sums[5:6, :] = row_sum(dv[...])
    sums[6:8, :] = jnp.zeros((2, width), F32)


def pixel_grad_kernel(n, start_grad, cols, *refs):
    pix, weights, refs = blocks_of(refs[:3]), refs[3 : 3 + n], refs[3 + n :]
    rows = start_grad.shape[0]
    grads, bands = [refs[0], refs[1], refs[2].at[:rows], refs[2].at[rows:]], refs[3]
    e_rows = pix[0].shape[1]
    first = jnp.zeros((1, e_rows), F32)
    second = jnp.zeros((1, e_rows), F32)
    for e in range(n):
        got = dot_t(start_grad[...], weights[e][:e_rows, :])
        grads[e][...] = got.astype(BF16)
        first = first + row_sum(got)
        second = second + row_sum(got * (pix[e][...].astype(F32) - cols[0:1, :]))
    bands[...] = band_sums(first, second)


def weight_grads(n, part, base, pairs, kept, sent):
    grads = split_blocks(kept, sent, n)
    for i, (left, right) in enumerate(pairs):
        whole = dot_tl(left[...], right).astype(BF16)
        for e in range(n):
            at = base + i * part
            grads[e][at : at + part, :] = whole[e * part : (e + 1) * part, :]


def weight_kernel(sizes, start_grad, start, dq, dk, dv, cols, vecs, *refs):
    n, part = sizes
    pix, (kept, sent) = blocks_of(refs[:3]), refs[3:]
    e_rows = pix[0].shape[1]
    normed = norm_forward(start[...], vecs[1:2, :], vecs[2:3, :])[2]
    pairs = ((dq, normed), (dk, normed), (dv, normed))
    weight_grads(n, part, e_rows, pairs, kept, sent)
    grads = split_blocks(kept, sent, n)
    for e in range(n):
        got = dot_tl(normed_pixels(pix[e], cols)[1], start_grad[...])
        grads[e][:e_rows, :] = got.astype(BF16)


def join_kernel(half, flag, direct, handed, out):
    at = pl.multiple_of(flag[0] * half, 16)
    out[pl.ds(at, half), :] = direct[...]
    at = pl.multiple_of((1 - flag[0]) * half, 16)
    out[pl.ds(at, half), :] = handed[...]


def pack_kernel(sizes, place, mlp_sums, hid_sums, attn_sums, bands, mask_rows, out):
    n, part = sizes
    me = place[0]
    dec, width = mask_rows.shape[1], out.shape[1]
    base = 5 * n
    row = lax.broadcasted_iota(jnp.int32, (base, width), 0)
    total = jnp.zeros((base, width), F32)

    def widened(values):
        return jnp.concatenate([values, jnp.zeros((1, width - values.shape[1]), F32)], axis=1)

    for e in range(n):
        at = e ^ me
        lanes = slice(e * part, (e + 1) * part)
        total = jnp.where(row == at, mlp_sums[e : e + 1, :], total)
        total = jnp.where(row == n + at, widened(attn_sums[4:5, lanes]), total)
        total = jnp.where(row == 2 * n + at, widened(attn_sums[5:6, lanes]), total)
        total = jnp.where(row == 3 * n + at, mlp_sums[n + 1 + e : n + 2 + e, :], total)
    total = jnp.where(row == 4 * n + me, widened(mask_rows[0:1, :]), total)
    out[:base, :] = total
    out[base : base + 4, :] = attn_sums[:4, :]
    out[base + 4 : base + 6, :] = hid_sums[:2, :]
    out[base + 6 : base + 7, :] = mlp_sums[n : n + 1, :]
    out[base + 7 :, :] = jnp.zeros((out.shape[0] - base - 7, width), F32)
    out[base + 7 : base + 9, :128] = bands[:2, :]


def write_out(plan, values, outs):
    at = 0
    for out, turned in zip(outs, plan):
        if turned:
            count = out.shape[1]
            out[...] = values[at : at + count, :].T.astype(F32)
        else:
            count = out.shape[0]
            out[...] = values[at : at + count, :].astype(F32)
        at += count


def finish_kernel(half, plan, flag, own, came, *refs):
    outs, held = refs[:-1], refs[-1]
    first = flag[0] == 0

    @pl.when(first)
    def _():
        held[:half, :] = own[...]
        held[half:, :] = came[...]

    @pl.when(jnp.logical_not(first))
    def _():
        held[:half, :] = came[...]
        held[half:, :] = own[...]

    write_out(plan, held, outs)


def band_sums(first, second):
    columns = first.shape[1]
    band = lax.broadcasted_iota(jnp.int32, (columns, 128), 0) % BANDS
    pick_band = (band == lax.broadcasted_iota(jnp.int32, band.shape, 1)).astype(F32)
    rows = jnp.concatenate([first, second, jnp.zeros((6, columns), F32)], axis=0)
    return jnp.dot(rows, pick_band, precision=lax.Precision.HIGHEST, preferred_element_type=F32)


def call(kernel, outs, args, name, scratch=(), us=2.0, scalars=0):
    run = pl.pallas_call(
        kernel,
        out_shape=[jax.ShapeDtypeStruct(shape, kind) for shape, kind in outs],
        in_specs=[SM] * scalars + [VM] * (len(args) - scalars),
        out_specs=[VM] * len(outs),
        scratch_shapes=list(scratch),
        compiler_params=params(),
        cost_estimate=pl.CostEstimate(
            flops=0, bytes_accessed=int(us * 3.3e6), transcendentals=0
        ),
        name=name,
    )
    return list(run(*args))


class Weights:
    def __init__(self, own, part, data_index):
        self.own, self.half = own, part.shape[0]
        self.flag = (data_index & 1).astype(jnp.int32)[None]
        self.direct = swap(part, "mp", 2)
        self.near = swap(own, "mp", 1)

    def hand_on(self):
        self.handed = swap(self.direct, "dp", 1)

    def join(self, line):
        rows, width = self.own.shape
        [far] = call(
            functools.partial(join_kernel, self.half),
            [((rows, width), BF16)],
            [self.flag, self.direct, line.wait(self.handed)],
            "join_weights",
            us=2.0,
            scalars=1,
        )
        line.mark(far)
        self.blocks = [self.own, self.near, far, swap(far, "mp", 1)]


def to_absolute(blocks, model_index):
    size = blocks.shape[0]
    for bit in bits_of("mp"):
        turned = jnp.stack([blocks[i ^ bit] for i in range(size)])
        blocks = jnp.where((model_index & bit) != 0, turned, blocks)
    return blocks


class Line:
    def __init__(self):
        self.last = None

    def wait(self, value):
        return value if self.last is None else after(value, self.last)

    def mark(self, value):
        self.last = value


class Reduction:
    def __init__(self, kept, sent, order, data_index, line, plan, shapes, name):
        self.kept, self.came = kept, swap(sent, "mp", 1)
        self.quarters, self.line, self.name = 2, line, name
        self.plan, self.shapes = plan, shapes
        self.flags = [((data_index >> k) & 1).astype(jnp.int32)[None] for k in range(len(bits_of("dp")))]
        self.order = list(order) + [k for k in range(len(self.flags)) if k not in order]
        self.done, self.own, self.hold = [], None, False

    def step(self):
        if self.order or self.own is None:
            self.scatter()
        elif len(self.done) > 1:
            self.gather()
        else:
            self.finish()

    def scatter(self):
        came = self.line.wait(self.came)
        axis = self.order.pop(0) if self.order else None
        rows = self.kept.shape[0] // self.quarters
        if axis is None:
            [self.own] = self.stage(came, None, 0)
            self.line.mark(self.own)
            self.came = swap(self.own, "dp", 1 << self.done[-1][0])
        elif axis == "x":
            self.kept, sent = self.stage(came, None, rows)
            self.line.mark(self.kept)
            self.quarters = 1
            self.sent = sent
            if not self.hold:
                self.launch()
        else:
            self.kept, sent = self.stage(came, self.flags[axis], rows // 2)
            self.line.mark(self.kept)
            self.done.append((axis, int(self.kept.shape[1] < came.shape[1])))
            self.came = swap(sent, "dp", 1 << axis)

    def launch(self, *before):
        self.came = swap(after(self.sent, *before) if before else self.sent, "mp", 2)

    def stage(self, came, flag, half):
        total, width = self.kept.shape
        quarters, rows = self.quarters, total // self.quarters
        if flag is not None and half % 16 and width % 256 == 0:
            part = width // 2

            def kernel(mine, a, b, own, other):
                for out, which in ((own, mine[0]), (other, 1 - mine[0])):
                    here = pl.ds(pl.multiple_of(which * part, 128), part)
                    out[...] = (a[:, here].astype(F32) + b[:, here].astype(F32)).astype(BF16)

            return call(
                kernel,
                [((total, part), BF16)] * 2,
                [flag, self.kept, came],
                "reduce_" + self.name,
                scalars=1,
            )
        if flag is not None and half % 16:
            summed = (self.kept.astype(F32) + came.astype(F32)).astype(BF16)
            summed = summed.reshape(quarters, rows, width)
            own = lax.dynamic_slice_in_dim(summed, flag[0] * half, half, 1)
            other = lax.dynamic_slice_in_dim(summed, (1 - flag[0]) * half, half, 1)
            return own.reshape(-1, width), other.reshape(-1, width)

        def total_of(a, b, at, count):
            here = pl.ds(at, count)
            return (a[here, :].astype(F32) + b[here, :].astype(F32)).astype(BF16)

        if flag is None:

            def kernel(a, b, *outs):
                for k, out in enumerate(outs):
                    out[...] = total_of(a, b, k * out.shape[0], out.shape[0])

            count = 1 if half == 0 else 2
            return call(
                kernel, [((total // count, width), BF16)] * count, [self.kept, came], "reduce_" + self.name
            )

        def kernel(mine, a, b, own, other):
            for q in range(quarters):
                here = slice(q * half, (q + 1) * half)
                at = pl.multiple_of(q * rows + mine[0] * half, 16)
                own[here, :] = total_of(a, b, at, half)
                at = pl.multiple_of(q * rows + (1 - mine[0]) * half, 16)
                other[here, :] = total_of(a, b, at, half)

        return call(
            kernel,
            [((total // 2, width), BF16)] * 2,
            [flag, self.kept, came],
            "reduce_" + self.name,
            scalars=1,
        )

    def gather(self):
        axis, dim = self.done.pop()
        came = self.line.wait(self.came)
        self.own = jnp.where(
            self.flags[axis][0] == 0,
            jnp.concatenate([self.own, came], axis=dim),
            jnp.concatenate([came, self.own], axis=dim),
        )
        self.line.mark(self.own)
        self.came = swap(self.own, "dp", 1 << self.done[-1][0])

    def finish(self):
        half, width = self.own.shape
        self.result = call(
            functools.partial(finish_kernel, half, self.plan),
            [(shape, F32) for shape in self.shapes],
            [self.flags[self.done[0][0]], self.own, self.line.wait(self.came)],
            "finish_" + self.name,
            [pltpu.VMEM((2 * half, width), BF16)],
            us=3.0,
            scalars=1,
        )
        self.line.mark(self.result[0])


class Sums:
    def __init__(self, values, line):
        self.values, self.line = values, line
        self.left = [(axis, bit) for axis in ("mp", "dp") for bit in bits_of(axis)]
        self.came = swap(values, *self.left[0])

    def step(self):
        self.values = self.values + self.line.wait(self.came)
        self.line.mark(self.values)
        self.left.pop(0)
        if self.left:
            self.came = swap(self.values, *self.left[0])


def exchange(tiles):
    size = lax.axis_size("dp")
    blocks = tiles.reshape(size, tiles.shape[0] // size, tiles.shape[1])
    return lax.all_to_all(blocks, "dp", split_axis=0, concat_axis=0, tiled=True).reshape(tiles.shape)


def shards(
    patches,
    vis_count,
    vis_pos,
    tile_sample,
    tile_quad,
    w_embed,
    b_embed,
    norm1_gain,
    norm1_bias,
    w_query,
    b_query,
    w_key,
    w_value,
    b_value,
    w_attn_out,
    b_attn_out,
    norm2_gain,
    norm2_bias,
    w_hidden,
    b_hidden,
    w_mlp_out,
    b_mlp_out,
    w_decoder,
    b_decoder,
    mask_token,
    cotangent,
):
    data_size = lax.axis_size("dp")
    model_size = lax.axis_size("mp")
    data_index = lax.axis_index("dp")
    model_index = lax.axis_index("mp")
    tile_count = vis_count.shape[0]
    visible = vis_pos.shape[1]
    grid_count, pixel_cols = patches.shape
    tile_tokens = grid_count // tile_count
    full_width = w_embed.shape[1]
    part_width = b_embed.shape[0]
    dec_part = b_decoder.shape[0]
    hid_part = b_hidden.shape[0]
    pair_tiles = tile_count // data_size
    own_samples = SAMP_OWN // model_size
    sample_rows = 4 * visible
    rows = own_samples * sample_rows
    my_tiles = own_samples * 4
    score_scale = HEAD_DIM ** (-0.5)

    tile_ids = jnp.arange(tile_count, dtype=jnp.int32)
    owners = tile_sample // SAMP_OWN
    earlier = (owners[:, None] == owners[None, :]) & (tile_ids[None, :] < tile_ids[:, None])
    tile_ranks = jnp.sum(earlier.astype(jnp.int32), axis=1)
    slot_of = owners * pair_tiles + tile_ranks
    at_slot = slot_of[None, :] == tile_ids[:, None]
    order = jnp.sum(jnp.where(at_slot, tile_ids[None, :], 0), axis=1)
    tile_code = (tile_sample % SAMP_OWN) * 4 + tile_quad
    pos_wide = jnp.pad(vis_pos, ((0, 0), (0, 128 - visible)), constant_values=-1000)

    line = Line()
    [stats] = call(stats_kernel, [((8, 128), F32)], [patches], "band_sums", us=4.0)
    stats = stats + swap(stats, "mp", 1)
    stats = stats + swap(stats, "mp", 2)

    small = [b_embed, b_query, b_value, b_attn_out, b_mlp_out, b_decoder, b_hidden]
    base = pixel_cols + 4 * part_width
    own_first, own_second, cut_first, cut_second = call(
        prep_kernel,
        [((base + 32, full_width), BF16), ((2 * hid_part + dec_part, full_width), BF16)]
        + [(((base + 32) // 2, full_width), BF16), (((2 * hid_part + dec_part) // 2, full_width), BF16)],
        [(data_index & 1).astype(jnp.int32)[None]]
        + [w_query.T, w_key.T, w_value.T, w_attn_out, w_hidden, w_mlp_out, w_decoder]
        + [after(w_embed, stats)]
        + [v[None, :] for v in small],
        "prep_weights",
        us=5.0,
        scalars=1,
    )
    line.mark(own_first)
    first_w = Weights(own_first, cut_first, data_index)
    by_slot = jnp.where(at_slot, 1.0, 0.0)
    codes_slot = jnp.sum(by_slot * tile_code.astype(F32)[None, :], axis=1)
    counts_slot = jnp.sum(by_slot * vis_count.astype(F32)[None, :], axis=1)
    pos_slot = jnp.sum(by_slot[:, :, None] * vis_pos.astype(F32)[None, :, :], axis=1)
    info = jnp.concatenate([codes_slot[None], counts_slot[None]], axis=0)
    info = jnp.pad(info, ((0, 6), (0, 128 - tile_count)))
    packet = jnp.concatenate([stats, info, pos_slot.reshape(-1, 128)], axis=0)[None]
    for k, bit in enumerate(bits_of("dp")):
        came = swap(packet, "dp", bit)
        if k == 0:
            picked, cot_picked, mask_rows = call(
                functools.partial(pick_kernel, tile_tokens),
                [
                    ((tile_count * visible, pixel_cols), BF16),
                    ((tile_count * visible, dec_part), BF16),
                    ((8, dec_part), F32),
                ],
                [line.wait(order), vis_count, pos_wide, patches, cotangent],
                "pick_rows",
                us=7.5,
                scalars=2,
            )
            came = after(came, picked)
        packet = jnp.where(
            (data_index >> k) & 1 == 0,
            jnp.concatenate([packet, came], axis=0),
            jnp.concatenate([came, packet], axis=0),
        )

    arrived = exchange(after(picked, packet, first_w.direct))

    second_w = Weights(own_second, after(cut_second, first_w.direct), data_index)
    first_w.hand_on()
    second_w.hand_on()

    own_info = lax.dynamic_slice_in_dim(packet[:, 8:10], data_index * pair_tiles, pair_tiles, 2)
    own_info = own_info.transpose(1, 0, 2).reshape(2, tile_count).astype(jnp.int32)
    my_tiles_bit = model_index * my_tiles
    codes = own_info[0] ^ my_tiles_bit
    total = jnp.sum(packet[:, :2, :BANDS], axis=0)
    per_band = float(grid_count * data_size * (pixel_cols // BANDS) * model_size)
    band_mean = total[0] / per_band
    band_var = total[1] / per_band - band_mean * band_mean
    band_rstd = lax.rsqrt(band_var + band_eps)
    mean_cols = jnp.tile(band_mean, pixel_cols // BANDS)
    rstd_cols = jnp.tile(band_rstd, pixel_cols // BANDS)

    own_pos = packet[:, 16:].reshape(data_size, tile_count, visible)
    own_pos = lax.dynamic_slice_in_dim(own_pos, data_index * pair_tiles, pair_tiles, 1)
    own_pos = own_pos.reshape(tile_count, visible)
    mine = (codes[None, :] == jnp.arange(my_tiles)[:, None]).astype(F32)
    my_counts = jnp.sum(mine * own_info[1].astype(F32)[None, :], axis=1)
    my_pos = jnp.sum(mine[:, :, None] * own_pos[None], axis=1)
    my_pos = my_pos.astype(jnp.int32)
    live = jnp.arange(visible)[None, :] < my_counts.astype(jnp.int32)[:, None]
    live_col = live.reshape(rows, 1)
    usable = live.reshape(own_samples, sample_rows)
    quadrant = (jnp.arange(my_tiles) % 4)[:, None]
    inner = my_pos % (SIDE * SIDE)
    frames = tile_tokens // (SIDE * SIDE)
    col_at = quadrant % 2 * SIDE + inner % SIDE
    row_at = quadrant // 2 * SIDE + inner // SIDE + 2 * SIDE
    frame_at = my_pos // (SIDE * SIDE) + 4 * SIDE
    table = place_table(full_width, frames)
    high = table.astype(jnp.bfloat16)
    low = (table - high.astype(np.float32)).astype(jnp.bfloat16)
    wide = np.zeros((128, full_width), jnp.bfloat16)
    wide[: table.shape[0]], wide[64 : 64 + table.shape[0]] = high, low
    lane = jnp.arange(128)[None, :]
    spots = jnp.where(lane < 127, lane % 64, -1)
    chosen = (
        (col_at.reshape(rows, 1) == spots)
        | (row_at.reshape(rows, 1) == spots)
        | (frame_at.reshape(rows, 1) == spots)
        | ((lane == 127) & live_col)
    ).astype(BF16)
    key_mask = jnp.pad(usable.astype(F32), ((0, 8 - own_samples), (0, 0)))
    cols = jnp.pad(jnp.stack([mean_cols, rstd_cols]), ((0, 6), (0, 0)))

    line = Line()
    held = after(arrived, second_w.direct, chosen, key_mask, cols)
    own, near, far = place_in(codes, held, visible, model_size)
    line.mark(far)
    pix = Crossing(own, near, far)
    arrived_cot = exchange(after(cot_picked, far))
    first_w.join(line)
    pix.relay(line)
    line.mark(pix.parts[1])
    own, near, far = place_in(codes, line.wait(arrived_cot), visible, model_size)
    line.mark(far)
    cot = Crossing(own, near, far)
    bias_rel = [first_w.blocks[e][base : base + 16] for e in range(4)]
    bias_rel = jnp.stack(bias_rel).astype(F32)
    bias_abs = to_absolute(bias_rel, model_index)

    def rel_vec(k):
        return bias_rel[:, k, : small[k].shape[0]].reshape(1, -1)

    def abs_vec(k):
        return bias_abs[:, k, : small[k].shape[0]].reshape(1, -1)

    gains = [norm1_gain, norm1_bias, norm2_gain, norm2_bias]
    gains = [v[None].astype(F32) for v in gains]
    vecs = jnp.concatenate(
        [abs_vec(0), gains[0], gains[1], rel_vec(1), rel_vec(2), abs_vec(3)]
        + [gains[2], gains[3], abs_vec(4), jnp.zeros((7, full_width), F32)]
    )
    bias_hid, bias_dec = bias_rel[:, 6, :hid_part], bias_rel[:, 5, :dec_part]

    square = ((rows, full_width), BF16)
    wide_rows = ((rows, full_width), F32)
    heads = own_samples * full_width // HEAD_DIM
    weight_scratch = pltpu.VMEM((full_width, full_width), BF16)
    start, queries, key_rows, value_rows, probs, attended, middle = call(
        functools.partial(embed_kernel, (model_size, part_width, sample_rows)),
        [square] * 4 + [((heads, sample_rows, sample_rows), BF16), square, wide_rows],
        [chosen, jnp.asarray(wide), cols, vecs, line.wait(key_mask)] + pix.parts + first_w.blocks,
        "embed_attend",
        [weight_scratch],
        us=19.0,
    )
    line.mark(middle)
    cot.relay(line)
    second_w.join(line)
    decoded_shape = ((rows, dec_part), BF16)
    hidden_shape = ((rows, hid_part), BF16)
    out = call(
        functools.partial(mlp_kernel, model_size),
        [decoded_shape] * 2
        + [((2 * rows, dec_part), BF16)]
        + [hidden_shape] * model_size
        + [((2 * (hid_part + dec_part), full_width), BF16)] * 2
        + [wide_rows, ((16, full_width), F32)],
        [middle, vecs, bias_hid, bias_dec] + cot.parts + second_w.blocks,
        "mlp_decode",
        [pltpu.VMEM((model_size, rows, hid_part), BF16)] * 2,
        us=20.0,
    )
    decoded_rows, pre_grads = out[:3], out[3 : 3 + model_size]
    out_kept, out_sent, final_grad, mlp_sums = out[3 + model_size :]
    decoded_mp = Crossing(*decoded_rows)
    red_a = Reduction(
        out_kept,
        out_sent,
        ["x", 0, 1, 2],
        data_index,
        line,
        (False, True),
        [w_mlp_out.shape, w_decoder.shape],
        "out",
    )
    def decoded_step(decoded_dp):
        out = call(
            functools.partial(spread_kernel, tile_tokens),
            [((grid_count, dec_part), BF16)],
            [order, vis_count, pos_wide, mask_token[None, :], line.wait(decoded_dp)],
            "spread_decoded",
            us=3.5,
            scalars=2,
        )
        line.mark(out[0])
        return out

    def go_home(crossing):
        parts = crossing.parts
        tiles = place_out(codes, [parts[0], line.wait(parts[1]), parts[2]], visible)
        line.mark(tiles)
        return exchange(tiles)

    out = call(
        functools.partial(hidden_kernel, model_size),
        [((2 * (hid_part + part_width), full_width), BF16)] * 2 + [wide_rows, ((8, full_width), F32)],
        [middle, vecs, final_grad, attended] + pre_grads + second_w.blocks,
        "hidden_back",
        us=13.0,
    )
    hid_kept, hid_sent, middle_grad, hid_sums = out
    line.mark(middle_grad)
    decoded_mp.relay(line)
    red_a.step()
    red_b = Reduction(
        hid_kept, line.wait(hid_sent), ["x", 0, 1, 2], data_index, line, (True, False), [w_hidden.shape, w_attn_out.shape], "hidden"
    )
    start_grad, dq, dk, dv, attn_sums = call(
        functools.partial(attn_back_kernel, (model_size, part_width, sample_rows, pixel_cols)),
        [square] * 4 + [((8, full_width), F32)],
        [line.wait(middle_grad), start, queries, key_rows, value_rows]
        + [probs, chosen, vecs]
        + first_w.blocks,
        "attend_back",
        [weight_scratch, pltpu.VMEM((rows, full_width), BF16)],
        us=18.0,
    )
    line.mark(start_grad)
    decoded_dp = go_home(decoded_mp)
    out = call(
        functools.partial(pixel_grad_kernel, model_size),
        [((rows, pixel_cols), BF16)] * 2 + [((2 * rows, pixel_cols), BF16), ((8, 128), F32)],
        [line.wait(start_grad), cols] + pix.parts + first_w.blocks,
        "pixel_grad",
        us=6.7,
    )
    normed_grad, bands = out[:3], out[3]
    line.mark(bands)
    grad_mp = Crossing(*normed_grad)
    [sums] = call(
        functools.partial(pack_kernel, (model_size, part_width)),
        [((32, full_width), F32)],
        [model_index.astype(jnp.int32)[None], mlp_sums, hid_sums, attn_sums, line.wait(bands)]
        + [mask_rows],
        "pack_sums",
        us=1.5,
        scalars=1,
    )
    line.mark(sums)
    sums = Sums(sums, line)
    sums.step()
    red_b.hold = True
    red_b.step()
    red_a.step()
    spread = decoded_step(decoded_dp)
    first_kept, first_sent = call(
        functools.partial(weight_kernel, (model_size, part_width)),
        [((2 * (base - part_width), full_width), BF16)] * 2,
        [line.wait(start_grad), start, dq, dk, dv, cols, vecs] + pix.parts,
        "weight_grad",
        us=10.0,
    )
    line.mark(first_kept)
    red_a.step()
    grad_mp.relay(line)
    sums.step()
    red_b.launch(sums.values)
    red_c = Reduction(
        first_kept,
        line.wait(first_sent),
        ["x", 0, 1, 2],
        data_index,
        line,
        (False,) * 4,
        [w_embed.shape] + [w_attn_out.shape] * 3,
        "first",
    )

    def patch_step(grad_dp):
        bands_all = sums.values[5 * model_size + 7 : 5 * model_size + 9, :BANDS]
        grad_all, cross_all = bands_all[0], bands_all[1]
        grad_var = -0.5 * cross_all * band_rstd * band_rstd * band_rstd
        grad_mean = -band_rstd * grad_all - 2.0 * band_mean * grad_var
        terms = jnp.stack([grad_mean / per_band, 2.0 * grad_var / per_band, band_rstd])
        terms = jnp.pad(jnp.tile(terms, (1, pixel_cols // BANDS)), ((0, 5), (0, 0)))
        out = call(
            functools.partial(patch_kernel, tile_tokens),
            [((grid_count, pixel_cols), F32)],
            [order, vis_count, pos_wide, terms, patches, line.wait(grad_dp)],
            "spread_patch_grad",
            us=8.0,
            scalars=2,
        )
        line.mark(out[0])
        return out

    def steps(*chains):
        for chain in chains:
            chain.step()

    kept = {}

    def go(name):
        if name in chains:
            chains[name].step()
        elif name == "H":
            kept["grad"] = go_home(grad_mp)
        elif name == "P":
            while sums.left:
                sums.step()
            kept["patch"] = patch_step(kept["grad"])
    chains = {"a": red_a, "b": red_b, "c": red_c, "s": sums}
    for name in "cassabsabacbHabcbcPbccbcc":
        go(name)
    while sums.left:
        sums.step()
    while not all(hasattr(chain, "result") for chain in (red_a, red_b, red_c)):
        for chain in (red_a, red_b, red_c):
            if not hasattr(chain, "result"):
                chain.step()
    [patch_grad], [decoded] = kept["patch"], spread

    n = model_size
    sums = sums.values
    own_rows = [
        lax.dynamic_slice_in_dim(sums, model_index + k * n, 1, 0)[0] for k in range(5)
    ]
    sum_hidden = own_rows[0]
    sum_query, sum_value = own_rows[1][:part_width], own_rows[2][:part_width]
    sum_dec, grad_mask_token = own_rows[3][:dec_part], own_rows[4][:dec_part]
    gain_one, bias_one, embed_sum, attn_out_sum, gain_two, bias_two, mlp_out_sum = (
        sums[5 * n + k] for k in range(7)
    )

    def mine_of(vector):
        part = vector.shape[0] // model_size
        return lax.dynamic_slice_in_dim(vector, model_index * part, part, 0)

    (g_out, g_dec), (g_hid, g_attn) = red_a.result, red_b.result
    g_embed, g_query, g_key, g_value = red_c.result

    return (
        decoded,
        patch_grad,
        g_embed,
        mine_of(embed_sum),
        gain_one,
        bias_one,
        g_query.T,
        sum_query,
        g_key.T,
        g_value.T,
        sum_value,
        g_attn,
        mine_of(attn_out_sum),
        gain_two,
        bias_two,
        g_hid,
        sum_hidden,
        g_out,
        mine_of(mlp_out_sum),
        g_dec,
        sum_dec,
        grad_mask_token,
    )


def solution(mesh):
    in_specs = (
        P("dp", "mp"),
        P("dp"),
        P("dp", None),
        P("dp"),
        P("dp"),
        P("mp", None),
        P("mp"),
        P(),
        P(),
        P(None, "mp"),
        P("mp"),
        P(None, "mp"),
        P(None, "mp"),
        P("mp"),
        P("mp", None),
        P("mp"),
        P(),
        P(),
        P(None, "mp"),
        P("mp"),
        P("mp", None),
        P("mp"),
        P(None, "mp"),
        P("mp"),
        P("mp"),
        P("dp", "mp"),
    )
    out_specs = (
        P("dp", "mp"),
        P("dp", "mp"),
        P("mp", None),
        P("mp"),
        P(),
        P(),
        P(None, "mp"),
        P("mp"),
        P(None, "mp"),
        P(None, "mp"),
        P("mp"),
        P("mp", None),
        P("mp"),
        P(),
        P(),
        P(None, "mp"),
        P("mp"),
        P("mp", None),
        P("mp"),
        P(None, "mp"),
        P("mp"),
        P("mp"),
    )
    return jax.shard_map(shards, mesh=mesh, in_specs=in_specs, out_specs=out_specs, check_vma=False)
```
